32 devices in a mesh: batch: 8 (over z, y), tm: 4 (over x, core).
Axes of the slice: x: 2, y: 2, z: 4, core: 2. Of those that a mesh axis runs over, the one named last changes fastest.
Arguments:
- signal: float32 [16, 512, 512], P('batch', None, 'tm'), may hold values from -6 to 6
- quant_cot: float32 [16, 64, 1024], P('batch', 'tm'), may hold values from -6 to 6
- commit_cot: float32 [16, 9, 64], P('batch', None, 'tm'), may hold values from -6 to 6
- lengths: int32 [16], P('batch'), may hold values from 85 to 512, as said below
- codes: int32 [16, 9, 64], P('batch', None, 'tm'), may hold values from 0 to 1023
- wide_weight: bfloat16 [3, 512, 7, 512], replicated, may hold values from -0.09375 to 0.09375
- wide_bias: float32 [3, 512], replicated, may hold values from -1.8 to 1.8
- narrow_weight: bfloat16 [3, 512, 512], replicated, may hold values from -0.25 to 0.25
- narrow_bias: float32 [3, 512], replicated, may hold values from -1.8 to 1.8
- snake_alpha: float32 [7, 512], replicated, may hold values from 0.5 to 1
- down_weight: bfloat16 [1024, 16, 512], replicated, may hold values from -0.0625 to 0.0625
- down_bias: float32 [1024], replicated, may hold values from -1.8 to 1.8
- in_weight: float32 [9, 8, 1024], replicated, may hold values from -0.1875 to 0.1875
- in_bias: float32 [9, 8], replicated, may hold values from -1.8 to 1.8
- codebook: float32 [9, 8, 1024], replicated, may hold values from -6 to 6
- out_weight: float32 [9, 8, 1024], replicated, may hold values from -0.75 to 0.75
- out_bias: float32 [9, 1024], replicated, may hold values from -0.6 to 0.6
Outputs:
- quantized: float32 [16, 64, 1024], P('batch', 'tm')
- commit: float32 [16, 9, 64], P('batch', None, 'tm')
- signal_grad: float32 [16, 512, 512], P('batch', None, 'tm')
- wide_weight_grad: float32 [3, 512, 7, 512], P(None, 'tm')
- wide_bias_grad: float32 [3, 512], P(None, 'tm')
- narrow_weight_grad: float32 [3, 512, 512], P(None, 'tm')
- narrow_bias_grad: float32 [3, 512], P(None, 'tm')
- alpha_grad: float32 [7, 512], P(None, 'tm')
- down_weight_grad: float32 [1024, 16, 512], P('tm')
- down_bias_grad: float32 [1024], P('tm')
- in_weight_grad: float32 [9, 8, 1024], P(None, None, 'tm')
- in_bias_grad: float32 [9, 8], P(None, 'tm')
- codebook_grad: float32 [9, 8, 1024], P(None, None, 'tm')
- out_weight_grad: float32 [9, 8, 1024], P(None, None, 'tm')
- out_bias_grad: float32 [9, 1024], P(None, 'tm')
The draws below stay inside these ranges and needn't reach their ends.
Inputs may be any that keep to these rules, and one draw needn't show every extreme that they name: `lengths`: in each group of 2 crops that one index of batch holds, one crop has the full length 512; the others are drawn evenly.
All inputs are finite; a program needn't handle non-finite values.
Results may differ from the reference program's by a relative error of at most 0.035.
The reference program's roundings to bfloat16 on the way count: a program that leaves them out, or rounds other values in their place, can miss the bound.
Values may be sent and summed in bfloat16 or wider, within the bound.
A program may use at most 320 MiB of HBM per device.

```python
import math
import jax
import jax.numpy as jnp
from jax import lax

CHANNELS = 512
LATENT = 1024
CODES = 1024
CODE_DIM = 8
SECTIONS = 9
STRIDE = 8
KERNEL = 16
CROPS_DEV = 2
SEQ = 512
FRAMES = 64
CROPS = 16


def draw_lengths(key, part):
    key = jax.random.fold_in(key, 11)
    first_key, second_key = jax.random.split(key)
    groups = CROPS // CROPS_DEV
    drawn = jax.random.randint(first_key, (groups, CROPS_DEV), SEQ // 6, SEQ + 1, dtype=jnp.int32)
    chosen = jax.random.randint(second_key, (groups, 1), 0, CROPS_DEV, dtype=jnp.int32)
    slots = jnp.arange(CROPS_DEV, dtype=jnp.int32)[None, :]
    filled = jnp.where(slots == chosen, jnp.int32(SEQ), drawn)
    return filled.reshape(CROPS)


def touch_ends(array, rng, smallest, high):
    index_at = [jax.random.randint(jax.random.fold_in(rng, axis), (), 0, length) for axis, length in enumerate(array.shape)]
    main_axis = array.shape.index(max(array.shape))
    neighbour = index_at[:main_axis] + [(index_at[main_axis] + 1) % array.shape[main_axis]] + index_at[main_axis + 1:]
    return array.at[tuple(index_at)].set(smallest).at[tuple(neighbour)].set(high)


def level_of(key, shape, cuts, smallest, high):
    factor_of, own = 1.0, jax.random.fold_in(key, 6)
    for dim, blocks in cuts:
        heights = jnp.exp(jax.random.uniform(jax.random.fold_in(own, dim), (blocks,), jnp.float32, smallest / len(cuts), high / len(cuts)))
        factor_of = factor_of * jnp.repeat(heights, shape[dim] // blocks).reshape([-1 if axis == dim else 1 for axis in range(len(shape))])
    return factor_of


def scatter_about(key, extent, scale, reach, cuts=(), kind=jnp.bfloat16):
    values = jax.random.normal(key, extent, jnp.float32) * scale
    if len(cuts) > 0:
        values = level_of(key, extent, cuts, -0.22, 0.18) * values
    return jnp.clip(values, min=-reach, max=reach).astype(kind)


def setup_inputs(seed: int = 0) -> dict:
    seeds = jax.random.split(jax.random.key(seed), 18)
    signal = scatter_about(seeds[0], (CROPS, CHANNELS, SEQ), 1.0, 6.0, ((0, 8), (2, 4)), jnp.float32)
    quant_cot = scatter_about(seeds[1], (CROPS, FRAMES, LATENT), 1.0, 6.0, ((0, 8), (1, 4)), jnp.float32)
    commit_cot = scatter_about(seeds[2], (CROPS, SECTIONS, FRAMES), 1.0, 6.0, ((0, 8), (2, 4)), jnp.float32)
    lengths = draw_lengths(jax.random.fold_in(seeds[17], 71), 0)
    codes = touch_ends(jax.random.randint(seeds[4], (CROPS, SECTIONS, FRAMES), 0, CODES), jax.random.fold_in(seeds[4], 1), 0, CODES - 1).astype(jnp.int32)
    wide_weight = scatter_about(seeds[5], (3, CHANNELS, 7, CHANNELS), (7 * CHANNELS) ** -0.5, 0.09375)
    wide_bias = scatter_about(seeds[6], (3, CHANNELS), 0.3, 1.8, (), jnp.float32)
    narrow_weight = scatter_about(seeds[7], (3, CHANNELS, CHANNELS), CHANNELS ** -0.5, 0.25)
    narrow_bias = scatter_about(seeds[8], (3, CHANNELS), 0.3, 1.8, (), jnp.float32)
    snake_alpha = jnp.clip(jnp.exp(jax.random.uniform(seeds[9], (7, CHANNELS), jnp.float32, math.log(0.5), math.log(1.0))), 0.5, 1.0)
    down_weight = scatter_about(seeds[10], (LATENT, KERNEL, CHANNELS), (KERNEL * CHANNELS) ** -0.5, 0.0625)
    down_bias = scatter_about(seeds[11], (LATENT,), 0.3, 1.8, (), jnp.float32)
    in_weight = scatter_about(seeds[12], (SECTIONS, CODE_DIM, LATENT), LATENT ** -0.5, 0.1875, (), jnp.float32)
    in_bias = scatter_about(seeds[13], (SECTIONS, CODE_DIM), 0.3, 1.8, (), jnp.float32)
    codebook = scatter_about(seeds[14], (SECTIONS, CODE_DIM, CODES), 1.0, 6.0, (), jnp.float32)
    out_weight = scatter_about(seeds[15], (SECTIONS, CODE_DIM, LATENT), (CODE_DIM * SECTIONS) ** -0.5, 0.75, (), jnp.float32)
    out_bias = scatter_about(seeds[16], (SECTIONS, LATENT), 0.1, 0.6, (), jnp.float32)
    return dict(signal=signal, quant_cot=quant_cot, commit_cot=commit_cot, lengths=lengths, codes=codes, wide_weight=wide_weight, wide_bias=wide_bias, narrow_weight=narrow_weight, narrow_bias=narrow_bias, snake_alpha=snake_alpha, down_weight=down_weight, down_bias=down_bias, in_weight=in_weight, in_bias=in_bias, codebook=codebook, out_weight=out_weight, out_bias=out_bias)


@jax.custom_vjp
def low(v):
    return lax.optimization_barrier(v.astype(jnp.bfloat16)).astype(jnp.float32)

@jax.custom_vjp
def low_back(v):
    return v

def low_keep(v):
    return (low(v), None)

def low_pass(kept, grad):
    return (grad,)

def back_keep(v):
    return (v, None)

def back_low(kept, grad):
    return (low(grad),)
low.defvjp(low_keep, low_pass)
low_back.defvjp(back_keep, back_low)
DILATIONS = (1, 3, 9)

def snake(values, alphas):
    factor = alphas[None, :, None]
    return values + jnp.square(jnp.sin(factor * values)) / factor

def dilated(snaked, weight, bias, dilation):
    kernel = jnp.transpose(weight, (0, 2, 1))
    result = lax.conv_general_dilated(snaked, kernel, (1,), [(3 * dilation, 3 * dilation)], rhs_dilation=(dilation,), dimension_numbers=('NCH', 'OIH', 'NCH'), precision=lax.Precision.HIGHEST)
    return result + bias[None, :, None]

def forward(signal, valid, frame_valid, onehots, wide_weight, wide_bias, narrow_weight, narrow_bias, snake_alpha, down_weight, down_bias, in_weight, in_bias, codebook, out_weight, out_bias):
    hidden = signal * valid
    for number in range(3):
        snaked = low(snake(hidden, snake_alpha[2 * number]))
        conv_out = low_back(dilated(snaked, wide_weight[number], wide_bias[number], DILATIONS[number]))
        rounded = low(snake(conv_out, snake_alpha[2 * number + 1]))
        branch = jnp.einsum('oi,bit->bot', narrow_weight[number], rounded, precision=lax.Precision.HIGHEST)
        hidden = hidden + low_back(branch + narrow_bias[number][None, :, None])
    mixed = low(snake(hidden, snake_alpha[6]) * valid)
    kernel = jnp.transpose(down_weight, (0, 2, 1))
    strided = lax.conv_general_dilated(mixed, kernel, (STRIDE,), [(STRIDE // 2, STRIDE // 2)], dimension_numbers=('NCH', 'OIH', 'NCH'), precision=lax.Precision.HIGHEST)
    latent = low_back(jnp.transpose(strided, (0, 2, 1)) + down_bias[None, None, :])
    residual = latent
    quantized = jnp.zeros_like(latent)
    commits = []
    for phase_index in range(SECTIONS):
        encoded = jnp.einsum('dc,bfc->bfd', in_weight[phase_index], residual, precision=lax.Precision.HIGHEST) + in_bias[phase_index]
        looked = jnp.einsum('bfn,dn->bfd', onehots[:, phase_index], codebook[phase_index], precision=lax.Precision.HIGHEST)
        added_term = jnp.einsum('dc,bfd->bfc', out_weight[phase_index], looked, precision=lax.Precision.HIGHEST) + out_bias[phase_index]
        commits.append(lax.optimization_barrier(jnp.sum(jnp.square(encoded - looked), axis=2)) * frame_valid)
        residual = residual - added_term
        quantized = quantized + added_term
    return (quantized * frame_valid[:, :, None], jnp.stack(commits, axis=1))

def reference(signal, quant_cot, commit_cot, lengths, codes, wide_weight, wide_bias, narrow_weight, narrow_bias, snake_alpha, down_weight, down_bias, in_weight, in_bias, codebook, out_weight, out_bias):
    weights = tuple((weight.astype(jnp.float32) for weight in (wide_weight, wide_bias, narrow_weight, narrow_bias, snake_alpha, down_weight, down_bias, in_weight, in_bias, codebook, out_weight, out_bias)))
    places = jnp.arange(SEQ, dtype=jnp.int32)
    valid = (places[None, :] < lengths[:, None]).astype(jnp.float32)[:, None, :]
    frame_places = jnp.arange(FRAMES, dtype=jnp.int32)
    frame_valid = (STRIDE * frame_places[None, :] < lengths[:, None]).astype(jnp.float32)
    groups = CROPS // CROPS_DEV
    code_range = jnp.arange(CODES, dtype=jnp.int32)

    def scan_step(totals, batch_item):
        sig_part, quant_part, commit_part, valid_part, frame_part, code_part = batch_item
        onehots = (code_part[..., None] == code_range).astype(jnp.float32)

        def apply_block(inputs, *params):
            return forward(inputs, valid_part, frame_part, onehots, *params)
        result, pullback = jax.vjp(apply_block, sig_part, *weights)
        gradients = pullback((quant_part, commit_part))
        summed = tuple((first + second for first, second in zip(totals, gradients[1:])))
        return (summed, (result[0], result[1], gradients[0]))
    initial = tuple((jnp.zeros_like(weight) for weight in weights))
    stacked = (signal.astype(jnp.float32).reshape(groups, CROPS_DEV, CHANNELS, SEQ), quant_cot.astype(jnp.float32).reshape(groups, CROPS_DEV, FRAMES, LATENT), commit_cot.astype(jnp.float32).reshape(groups, CROPS_DEV, SECTIONS, FRAMES), valid.reshape(groups, CROPS_DEV, 1, SEQ), frame_valid.reshape(groups, CROPS_DEV, FRAMES), codes.reshape(groups, CROPS_DEV, SECTIONS, FRAMES))
    totals, (quant_all, commit_all, signal_grads) = lax.scan(scan_step, initial, stacked)
    quantized = quant_all.reshape(CROPS, FRAMES, LATENT)
    commit = commit_all.reshape(CROPS, SECTIONS, FRAMES)
    signal_grad = signal_grads.reshape(CROPS, CHANNELS, SEQ)
    return (quantized, commit, signal_grad, totals[0], totals[1], totals[2], totals[3], totals[4], totals[5], totals[6], totals[7], totals[8], totals[9], totals[10], totals[11])
```

```python
import functools

import jax
import jax.numpy as jnp
from jax import lax
from jax.experimental import pallas as pl
from jax.experimental.pallas import tpu as pltpu
from jax.sharding import PartitionSpec as P

STRIDE = 8


DILATIONS = (1, 3, 9)
MESH = pl.DeviceIdType.MESH
BLOCK = 64


def with_halo(block, sides, width):
    for axis, dim in sides:
        count = lax.axis_size(axis)
        forward = [(i, i + 1) for i in range(count - 1)]
        backward = [(target, source) for source, target in forward]
        low = lax.ppermute(
            lax.slice_in_dim(block, block.shape[dim] - width, None, axis=dim), axis, forward
        )
        high = lax.ppermute(lax.slice_in_dim(block, 0, width, axis=dim), axis, backward)
        block = jnp.concatenate([low, block, high], axis=dim)
    return block


def snake(values, alphas):
    factor = alphas[None, :, None]
    return values + jnp.square(jnp.sin(factor * values)) / factor


def snake_back(values, alphas, upstream):
    factor = alphas[None, :, None]
    double_sin = jnp.sin(2.0 * factor * values)
    square = jnp.square(jnp.sin(factor * values))
    grad_values = upstream * (1.0 + double_sin)
    grad_alphas = jnp.sum(
        upstream * (values * double_sin / factor - square / jnp.square(factor)), axis=(0, 2)
    )
    return (grad_values, grad_alphas)


def stacked_windows(padded, dilation, extent, backward):
    pieces = []
    for tap_index in range(7):
        offset = (6 - tap_index if backward else tap_index) * dilation
        pieces.append(lax.slice_in_dim(padded, offset, offset + extent, axis=2))
    return jnp.stack(pieces, axis=1)


def wide_conv(padded, weight, bias, dilation, extent):
    windows = stacked_windows(padded, dilation, extent, False)
    return (
        jnp.einsum("oki,bkit->bot", weight, windows, preferred_element_type=jnp.float32)
        + bias[None, :, None]
    )


def narrow_conv(rounded, weight, bias):
    return (
        jnp.einsum("oi,bit->bot", weight, rounded, preferred_element_type=jnp.float32)
        + bias[None, :, None]
    )


def unit_forward(hidden, number, unit_weights):
    wide_weight, wide_bias, narrow_weight, narrow_bias, snake_alpha = unit_weights
    dilation = DILATIONS[number]
    length = hidden.shape[2]
    snaked = snake(hidden, snake_alpha[2 * number]).astype(jnp.bfloat16)
    padded = with_halo(snaked, (("tm", 2),), 3 * dilation)
    conv_out = wide_conv(padded, wide_weight[number], wide_bias[number], dilation, length)
    rounded = snake(conv_out, snake_alpha[2 * number + 1]).astype(jnp.bfloat16)
    return (padded, conv_out, rounded)


def add_rows(rows, sources, target):
    def step(index, carry):
        at = index * BLOCK
        total = None
        for ref, start in sources:
            block = ref[pl.ds(start + at, BLOCK), :].astype(jnp.float32)
            total = block if total is None else total + block
        ref, start = target
        ref[pl.ds(start + at, BLOCK), :] = total.astype(ref.dtype)
        return carry

    lax.fori_loop(0, rows // BLOCK, step, 0)


def reduce_kernel(pieces, batch_size, packed, final, own, from_core, to_x, from_x, to_y, from_y, to_z, from_z, local_sems, send_sems, recv_sems):
    members = batch_size // 2
    batch = lax.axis_index("batch")
    time = lax.axis_index("tm")
    low, high = lax.rem(time, 2), time // 2
    core = 2 * high + 1 - low
    across = 2 * (1 - high) + low
    half = lax.rem(batch, 2)
    place = batch // 2
    pair = 2 * place + 1 - half

    def member(step):
        return 2 * lax.rem(place + step, members) + half

    barrier = pltpu.get_barrier_semaphore()
    peers = [(batch, core), (batch, across), (pair, time)]
    peers += [(member(step), time) for step in range(1, members)]
    for peer in peers:
        pl.semaphore_signal(barrier, inc=1, device_id=peer, device_id_type=MESH)
    pl.semaphore_wait(barrier, len(peers))

    def send(source, target, number, slot, device):
        return pltpu.make_async_remote_copy(
            src_ref=source,
            dst_ref=target,
            send_sem=send_sems.at[number, slot],
            recv_sem=recv_sems.at[number, slot],
            device_id=device,
            device_id_type=MESH,
        )

    spread = members - 1
    slot_y, slot_z, slot_back, slot_last = 3, 4, 4 + spread, 4 + 2 * spread
    copies = {}
    for number, (start, rows) in enumerate(pieces):
        here = pl.ds(start, rows)
        copies[number, 0] = send(
            packed.at[core, here], from_core.at[0, here], number, 0, (batch, core)
        )
        far = 2 * (1 - high) + 1 - low
        copies[number, 1] = send(
            packed.at[far, here], from_core.at[1, here], number, 1, (batch, core)
        )
        copies[number, 1].start()
        copies[number, 0].start()
    locals_ = []
    for number, (start, rows) in enumerate(pieces):
        here = pl.ds(start, rows)
        first = pltpu.make_async_copy(packed.at[across, here], own.at[1, here], local_sems.at[number, 1])
        second = pltpu.make_async_copy(packed.at[time, here], own.at[0, here], local_sems.at[number, 0])
        first.start()
        second.start()
        locals_.append((second, first))

    def stage_core(number):
        start, rows = pieces[number]
        locals_[number][1].wait()
        copies[number, 1].wait_recv()
        add_rows(rows, [(own.at[1], start), (from_core.at[1], start)], (to_x, start))
        here = pl.ds(start, rows)
        copies[number, 2] = send(to_x.at[here], from_x.at[here], number, 2, (batch, across))
        copies[number, 2].start()

    def stage_x(number):
        start, rows = pieces[number]
        locals_[number][0].wait()
        copies[number, 0].wait_recv()
        copies[number, 2].wait_recv()
        add_rows(
            rows, [(own.at[0], start), (from_core.at[0], start), (from_x, start)], (to_y, start)
        )
        other = pl.ds(start + (1 - half) * (rows // 2), rows // 2)
        copies[number, slot_y] = send(
            to_y.at[other], from_y.at[pl.ds(start // 2, rows // 2)], number, slot_y, (pair, time)
        )
        copies[number, slot_y].start()

    def stage_y(number):
        start, rows = pieces[number]
        copies[number, slot_y].wait_recv()
        add_rows(
            rows // 2,
            [(to_y, start + half * (rows // 2)), (from_y, start // 2)],
            (to_z, start // 2),
        )
        chunk = rows // batch_size
        for step in range(1, members):
            target = lax.rem(place + step, members)
            copies[number, slot_z + step - 1] = send(
                to_z.at[pl.ds(start // 2 + target * chunk, chunk)],
                from_z.at[step - 1, pl.ds(start // batch_size, chunk)],
                number,
                slot_z + step - 1,
                (member(step), time),
            )
            copies[number, slot_z + step - 1].start()

    def stage_z(number):
        start, rows = pieces[number]
        chunk = rows // batch_size
        for step in range(1, members):
            copies[number, slot_z + step - 1].wait_recv()
        mine = start + half * (rows // 2) + place * chunk
        sources = [(to_z, start // 2 + place * chunk)]
        sources += [(from_z.at[step], start // batch_size) for step in range(members - 1)]
        total = None
        for ref, at in sources:
            block = ref[pl.ds(at, chunk), :].astype(jnp.float32)
            total = block if total is None else total + block
        final[pl.ds(mine, chunk), :] = total.astype(final.dtype)
        for step in range(1, members):
            copies[number, slot_back + step - 1] = send(
                final.at[pl.ds(mine, chunk)],
                final.at[pl.ds(mine, chunk)],
                number,
                slot_back + step - 1,
                (member(step), time),
            )
            copies[number, slot_back + step - 1].start()

    def stage_back(number):
        start, rows = pieces[number]
        for step in range(1, members):
            copies[number, slot_back + step - 1].wait_recv()
        mine = pl.ds(start + half * (rows // 2), rows // 2)
        copies[number, slot_last] = send(
            final.at[mine], final.at[mine], number, slot_last, (pair, time)
        )
        copies[number, slot_last].start()

    def stage_last(number):
        copies[number, slot_last].wait_recv()

    stages = [stage_core, stage_x, stage_y, stage_z, stage_back, stage_last]
    for wave in range(len(pieces) + len(stages) - 1):
        for depth in range(len(stages)):
            number = wave - depth
            if 0 <= number < len(pieces):
                stages[depth](number)
    for copy in copies.values():
        copy.wait_send()


def reduce_all(packed, pieces, batch_size):
    rows, width = packed.shape[1:]
    members = batch_size // 2
    slots = 5 + 2 * (members - 1)
    kind = packed.dtype
    return pl.pallas_call(
        functools.partial(reduce_kernel, pieces, batch_size),
        out_shape=jax.ShapeDtypeStruct((rows, width), kind),
        in_specs=[pl.BlockSpec(memory_space=pl.ANY)],
        out_specs=pl.BlockSpec(memory_space=pltpu.VMEM),
        scratch_shapes=[
            pltpu.VMEM((2, rows, width), kind),
            pltpu.VMEM((2, rows, width), kind),
            pltpu.VMEM((rows, width), kind),
            pltpu.VMEM((rows, width), kind),
            pltpu.VMEM((rows, width), kind),
            pltpu.VMEM((rows // 2, width), kind),
            pltpu.VMEM((rows // 2, width), kind),
            pltpu.VMEM((members - 1, rows // batch_size, width), kind),
            pltpu.SemaphoreType.DMA((len(pieces), 2)),
            pltpu.SemaphoreType.DMA((len(pieces), slots)),
            pltpu.SemaphoreType.DMA((len(pieces), slots)),
        ],
        compiler_params=pltpu.CompilerParams(
            collective_id=0, has_side_effects=True, vmem_limit_bytes=56 * 2**20
        ),
    )(packed)


def by_share(array, dim, time_count):
    extent = array.shape[-1] // time_count
    flat = array.reshape(-1, time_count, extent)
    return jnp.swapaxes(flat, 0, 1)


def body(
    signal,
    quant_cot,
    commit_cot,
    lengths,
    codes,
    wide_weight,
    wide_bias,
    narrow_weight,
    narrow_bias,
    snake_alpha,
    down_weight,
    down_bias,
    in_weight,
    in_bias,
    codebook,
    out_weight,
    out_bias,
):
    crop_count, channel_count, length = signal.shape
    places = lax.axis_index("tm") * length + jnp.arange(length, dtype=jnp.int32)
    valid = (places[None, :] < lengths[:, None]).astype(jnp.float32)[:, None, :]
    unit_weights = (wide_weight, wide_bias, narrow_weight, narrow_bias, snake_alpha)
    current = signal * valid
    hiddens = [current]
    for number in range(3):
        padded, conv_out, rounded = unit_forward(current, number, unit_weights)
        current = current + narrow_conv(rounded, narrow_weight[number], narrow_bias[number])
        hiddens.append(current)
    mixed = (snake(current, snake_alpha[6]) * valid).astype(jnp.bfloat16)
    mixed_all = lax.all_gather(jnp.swapaxes(mixed, 1, 2), ("batch", "tm"), axis=0, tiled=False)
    edged = with_halo(mixed, (("tm", 2),), STRIDE // 2)
    frame_count = length // STRIDE
    blocks = edged.reshape(crop_count, channel_count, frame_count + 1, STRIDE)
    frame_windows = jnp.concatenate([blocks[:, :, :frame_count], blocks[:, :, 1:]], axis=3)
    latent = (
        jnp.einsum("cki,bifk->bfc", down_weight, frame_windows, preferred_element_type=jnp.float32)
        + down_bias[None, None, :]
    )
    frame_places = lax.axis_index("tm") * frame_count + jnp.arange(frame_count, dtype=jnp.int32)
    frame_valid = (STRIDE * frame_places[None, :] < lengths[:, None]).astype(jnp.float32)
    code_range = jnp.arange(codebook.shape[2], dtype=jnp.int32)
    phase_count = in_weight.shape[0]
    residual = latent
    quantized = jnp.zeros_like(latent)
    commits = []
    phase_saved = []
    for phase_index in range(phase_count):
        onehot = (codes[:, phase_index, :, None] == code_range).astype(jnp.float32)
        encoded = (
            jnp.einsum(
                "dc,bfc->bfd", in_weight[phase_index], residual, precision=lax.Precision.HIGHEST
            )
            + in_bias[phase_index]
        )
        looked = jnp.einsum(
            "bfn,dn->bfd", onehot, codebook[phase_index], precision=lax.Precision.HIGHEST
        )
        added_term = (
            jnp.einsum(
                "dc,bfd->bfc", out_weight[phase_index], looked, precision=lax.Precision.HIGHEST
            )
            + out_bias[phase_index]
        )
        spread_gap = encoded - looked
        commits.append(jnp.sum(jnp.square(spread_gap), axis=2) * frame_valid)
        phase_saved.append((residual, onehot, looked, spread_gap))
        residual = residual - added_term
        quantized = quantized + added_term
    quantized_out = quantized * frame_valid[:, :, None]
    commit_out = jnp.stack(commits, axis=1)
    quant_grad = quant_cot * frame_valid[:, :, None]
    carried = jnp.zeros_like(latent)
    in_weight_grads = [None] * phase_count
    in_bias_grads = [None] * phase_count
    codebook_grads = [None] * phase_count
    out_weight_grads = [None] * phase_count
    out_bias_grads = [None] * phase_count
    for phase_index in reversed(range(phase_count)):
        phase_input, onehot, looked, spread_gap = phase_saved[phase_index]
        gap_grad = 2.0 * (commit_cot[:, phase_index, :] * frame_valid)[:, :, None] * spread_gap
        push_grad = quant_grad - carried
        out_bias_grads[phase_index] = jnp.sum(push_grad, axis=(0, 1))
        out_weight_grads[phase_index] = jnp.einsum(
            "bfd,bfc->dc", looked, push_grad, precision=lax.Precision.HIGHEST
        )
        looked_grad = (
            jnp.einsum(
                "dc,bfc->bfd", out_weight[phase_index], push_grad, precision=lax.Precision.HIGHEST
            )
            - gap_grad
        )
        codebook_grads[phase_index] = jnp.einsum(
            "bfn,bfd->dn", onehot, looked_grad, precision=lax.Precision.HIGHEST
        )
        in_bias_grads[phase_index] = jnp.sum(gap_grad, axis=(0, 1))
        in_weight_grads[phase_index] = jnp.einsum(
            "bfd,bfc->dc", gap_grad, phase_input, precision=lax.Precision.HIGHEST
        )
        carried = carried + jnp.einsum(
            "dc,bfd->bfc", in_weight[phase_index], gap_grad, precision=lax.Precision.HIGHEST
        )
    latent_low = carried.astype(jnp.bfloat16)
    down_bias_grad = jnp.sum(latent_low, axis=(0, 1), dtype=jnp.float32)
    time_count = lax.axis_size("tm")
    batch_count = lax.axis_size("batch")
    crops_all = batch_count * crop_count
    latent_all = lax.all_gather(latent_low, "tm", axis=1, tiled=True)
    latent_all = lax.all_gather(latent_all, "batch", axis=0, tiled=True)
    share = latent_low.shape[2] // time_count
    latent_mine = lax.dynamic_slice_in_dim(latent_all, lax.axis_index("tm") * share, share, axis=2)
    frame_edges = with_halo(latent_low, (("tm", 1),), 1)
    spread_back = jnp.einsum(
        "cki,bfc->bifk", down_weight, frame_edges, preferred_element_type=jnp.float32
    )
    leading = jnp.pad(spread_back[:, :, :, :STRIDE], ((0, 0), (0, 0), (0, 1), (0, 0)))
    trailing = jnp.pad(spread_back[:, :, :, STRIDE:], ((0, 0), (0, 0), (1, 0), (0, 0)))
    joined = (leading + trailing).reshape(crop_count, channel_count, (frame_count + 3) * STRIDE)
    first_place = STRIDE + STRIDE // 2
    mixed_grad = joined[:, :, first_place : first_place + length]
    upstream, alpha_last = snake_back(current, snake_alpha[6], mixed_grad * valid)
    alpha_rows = [None] * 7
    alpha_rows[6] = alpha_last
    wide_grads = [None] * 3
    wide_bias_grads = [None] * 3
    narrow_grads = [None] * 3
    narrow_bias_grads = [None] * 3
    for number in reversed(range(3)):
        dilation = DILATIONS[number]
        rim_width = 3 * dilation
        hidden_in = hiddens[number]
        padded, conv_out, rounded = unit_forward(hidden_in, number, unit_weights)
        grad_branch = upstream.astype(jnp.bfloat16)
        narrow_bias_grads[number] = jnp.sum(grad_branch, axis=(0, 2), dtype=jnp.float32)
        narrow_grads[number] = jnp.einsum(
            "bot,bit->oi", grad_branch, rounded, preferred_element_type=jnp.float32
        )
        grad_rounded = jnp.einsum(
            "oi,bot->bit", narrow_weight[number], grad_branch, preferred_element_type=jnp.float32
        )
        grad_conv, alpha_rows[2 * number + 1] = snake_back(
            conv_out, snake_alpha[2 * number + 1], grad_rounded
        )
        grad_conv = grad_conv.astype(jnp.bfloat16)
        wide_bias_grads[number] = jnp.sum(grad_conv, axis=(0, 2), dtype=jnp.float32)
        windows = stacked_windows(padded, dilation, length, False)
        wide_grads[number] = jnp.einsum(
            "bot,bkit->oki", grad_conv, windows, preferred_element_type=jnp.float32
        )
        grad_padded = with_halo(grad_conv, (("tm", 2),), rim_width)
        grad_windows = stacked_windows(grad_padded, dilation, length, True)
        grad_snaked = jnp.einsum(
            "oki,bkot->bit", wide_weight[number], grad_windows, preferred_element_type=jnp.float32
        )
        grad_hidden, alpha_rows[2 * number] = snake_back(
            hidden_in, snake_alpha[2 * number], grad_snaked
        )
        upstream = upstream + grad_hidden
    signal_grad = upstream * valid

    unit_rows = []
    for number in reversed(range(3)):
        wide = wide_grads[number].reshape(time_count, -1, 7, channel_count)
        wide = jnp.swapaxes(wide, 1, 2).reshape(time_count, -1, channel_count)
        narrow = narrow_grads[number].reshape(time_count, -1, channel_count)
        unit_rows += [wide.astype(jnp.bfloat16), narrow.astype(jnp.bfloat16)]
    by_latent = [
        by_share(jnp.stack(rows), 2, time_count)
        for rows in (in_weight_grads, codebook_grads, out_weight_grads, out_bias_grads)
    ]
    by_latent.append(by_share(down_bias_grad, 0, time_count))
    by_channel = [
        by_share(jnp.stack(rows), 1, time_count)
        for rows in (wide_bias_grads, narrow_bias_grads, alpha_rows)
    ]
    by_channel = jnp.concatenate(by_channel, axis=1)
    in_bias_rows = by_share(jnp.stack(in_bias_grads), 1, time_count).reshape(time_count, 1, -1)
    wide_of = by_latent[0].shape[2]

    def widened(rows):
        return jnp.pad(rows, ((0, 0), (0, 0), (0, wide_of - rows.shape[2])))

    small = jnp.concatenate(by_latent + [widened(by_channel), widened(in_bias_rows)], axis=1)
    fold = channel_count // wide_of
    quantum = max(16 * batch_count, 2 * BLOCK)
    small_rows = -(-small.shape[1] // (fold * quantum)) * quantum
    small = jnp.pad(small, ((0, 0), (0, fold * small_rows - small.shape[1]), (0, 0)))
    small = jnp.concatenate(
        [small[:, part * small_rows : (part + 1) * small_rows] for part in range(fold)], axis=2
    )
    packed = jnp.concatenate([small.astype(jnp.bfloat16)] + unit_rows, axis=1)
    unit_extent = (packed.shape[1] - small_rows) // 3
    piece = max(unit_extent // 2, 16 * batch_count)
    pieces = [(0, small_rows)]
    pieces += [(at, piece) for at in range(small_rows, packed.shape[1], piece)]
    summed = reduce_all(packed, tuple(pieces), batch_count)

    small = summed[:small_rows]
    small = jnp.concatenate(
        [small[:, part * wide_of : (part + 1) * wide_of] for part in range(fold)], axis=0
    ).astype(jnp.float32)
    phases, dims = in_weight.shape[:2]
    count = phases * dims
    offset = 3 * count
    in_weight_out = small[:count].reshape(phases, dims, -1)
    codebook_out = small[count : 2 * count].reshape(phases, dims, -1)
    out_weight_out = small[2 * count : offset].reshape(phases, dims, -1)
    out_bias_out = small[offset : offset + phases]
    down_bias_out = small[offset + phases]
    offset = offset + phases + 1
    narrow_of = channel_count // time_count
    wide_bias_out = small[offset : offset + 3, :narrow_of]
    narrow_bias_out = small[offset + 3 : offset + 6, :narrow_of]
    alpha_out = small[offset + 6 : offset + 13, :narrow_of]
    in_bias_out = small[offset + 13, : count // time_count].reshape(phases, -1)
    units = summed[small_rows:].reshape(3, unit_extent, channel_count)[::-1].astype(jnp.float32)
    wide_out = units[:, : 7 * narrow_of].reshape(3, 7, narrow_of, channel_count)
    wide_out = jnp.swapaxes(wide_out, 1, 2)
    narrow_out = units[:, 7 * narrow_of :]

    mixed_all = mixed_all.reshape(batch_count, time_count, crop_count, length, channel_count)
    mixed_all = jnp.swapaxes(mixed_all, 1, 2).reshape(crops_all, time_count * length, channel_count)
    half = STRIDE // 2
    padded_all = jnp.pad(mixed_all, ((0, 0), (half, half), (0, 0)))
    grouped = padded_all.reshape(crops_all, -1, STRIDE, channel_count)
    early = jnp.einsum(
        "bfc,bfki->cki", latent_mine, grouped[:, :-1], preferred_element_type=jnp.float32
    )
    late = jnp.einsum(
        "bfc,bfki->cki", latent_mine, grouped[:, 1:], preferred_element_type=jnp.float32
    )
    down_weight_out = jnp.concatenate([early, late], axis=1)
    return (
        quantized_out,
        commit_out,
        signal_grad,
        wide_out,
        wide_bias_out,
        narrow_out,
        narrow_bias_out,
        alpha_out,
        down_weight_out,
        down_bias_out,
        in_weight_out,
        in_bias_out,
        codebook_out,
        out_weight_out,
        out_bias_out,
    )


def solution(mesh):
    return jax.shard_map(
        body,
        mesh=mesh,
        in_specs=(
            P("batch", None, "tm"),
            P("batch", "tm", None),
            P("batch", None, "tm"),
            P("batch"),
            P("batch", None, "tm"),
            P(),
            P(),
            P(),
            P(),
            P(),
            P(),
            P(),
            P(),
            P(),
            P(),
            P(),
            P(),
        ),
        out_specs=(
            P("batch", "tm", None),
            P("batch", None, "tm"),
            P("batch", None, "tm"),
            P(None, "tm", None, None),
            P(None, "tm"),
            P(None, "tm", None),
            P(None, "tm"),
            P(None, "tm"),
            P("tm", None, None),
            P("tm"),
            P(None, None, "tm"),
            P(None, "tm"),
            P(None, None, "tm"),
            P(None, None, "tm"),
            P(None, "tm"),
        ),
        check_vma=False,
    )
```

```python
import functools

import jax
import jax.numpy as jnp
from jax import lax
from jax.experimental import pallas as pl
from jax.experimental.pallas import tpu as pltpu
from jax.sharding import PartitionSpec as P

STRIDE = 8


DILATIONS = (1, 3, 9)
MESH = pl.DeviceIdType.MESH
BLOCK = 64


TAPS = 7
RIM = 32
ROWS = 32


def dot(left, right, left_dim, right_dim, precision=None):
    return lax.dot_general(
        left,
        right,
        (((left_dim,), (right_dim,)), ((), ())),
        precision=precision,
        preferred_element_type=jnp.float32,
    )


def exact(left, right, left_dim, right_dim):
    return dot(left, right, left_dim, right_dim, lax.Precision.HIGHEST)


def reduced_angle(angle):
    turns = jnp.floor(angle * 0.3183098861837907 + 0.5)
    rest = angle - turns * 3.140625
    rest = rest - turns * 9.67502593994140625e-4
    return rest - turns * 1.509957990978376432e-7


def sine(rest, square):
    series = -1.0 / 5040.0 + square * (1.0 / 362880.0 - square * (1.0 / 39916800.0))
    return rest + rest * square * (-1.0 / 6.0 + square * (1.0 / 120.0 + square * series))


def cosine(square):
    series = 1.0 / 40320.0 + square * (-1.0 / 3628800.0 + square * (1.0 / 479001600.0))
    return 1.0 + square * (-0.5 + square * (1.0 / 24.0 + square * (-1.0 / 720.0 + square * series)))


def snake_of(values, alpha, inverse):
    rest = reduced_angle(alpha * values)
    wave = sine(rest, rest * rest)
    return values + wave * wave * inverse


def snake_slopes(values, alpha, inverse):
    rest = reduced_angle(alpha * values)
    square = rest * rest
    wave = sine(rest, square)
    double = 2.0 * wave * cosine(square)
    return 1.0 + double, (values * double - wave * wave * inverse) * inverse


def split_three(values):
    first = values.astype(jnp.bfloat16)
    rest = values - first.astype(jnp.float32)
    second = rest.astype(jnp.bfloat16)
    third = (rest - second.astype(jnp.float32)).astype(jnp.bfloat16)
    return first, second, third


def folded(values):
    return jnp.sum(values.reshape(values.shape[0] // 8, 8, values.shape[1]), axis=0)


def block_kernel(
    time_count,
    small_rows,
    lengths,
    signal,
    quant_cot,
    commit_cot,
    codes,
    wide_hbm,
    wide_bias,
    narrow_hbm,
    narrow_bias,
    snake_alpha,
    down_hbm,
    down_bias,
    in_weight,
    in_bias,
    codebook,
    out_weight,
    out_bias,
    quantized,
    commit,
    signal_grad,
    packed,
    phases_out,
    latent_low,
    wide,
    narrow,
    down,
    down_raw,
    hidden,
    conv,
    windows,
    rounded,
    pad,
    grad,
    work,
    branch,
    moved,
    mixed_pad,
    frames,
    latent,
    latent_pad,
    spread,
    looked,
    gap_grad,
    correction,
    units,
    small,
    small_low,
    halo_out,
    halo_in,
    latent_in,
    weight_sems,
    out_sems,
    send_sems,
    recv_sems,
):
    f32, bf16 = jnp.float32, jnp.bfloat16
    batch = lax.axis_index("batch")
    time = lax.axis_index("tm")
    left = lax.rem(time + time_count - 1, time_count)
    right = lax.rem(time + 1, time_count)
    crops, channels, length = signal.shape
    latents = down_bias.shape[1]
    per_crop = length // ROWS
    blocks = crops * per_crop
    frame_count = length // STRIDE
    frames_all = crops * frame_count
    phases = codes.shape[1]
    dims = in_weight.shape[0] // phases
    count = phases * dims
    share = channels // time_count
    wide_of = latents // time_count

    barrier = pltpu.get_barrier_semaphore()
    for peer in (left, right):
        pl.semaphore_signal(barrier, inc=1, device_id=(batch, peer), device_id_type=MESH)

    wide_copies = [
        pltpu.make_async_copy(wide_hbm.at[unit], wide.at[unit], weight_sems.at[unit])
        for unit in range(3)
    ]
    narrow_copy = pltpu.make_async_copy(narrow_hbm, narrow, weight_sems.at[3])
    raw_rows = down_raw.shape[1]
    parts = down_hbm.shape[0] // raw_rows

    def raw_copy(part):
        return pltpu.make_async_copy(
            down_hbm.at[pl.ds(part * raw_rows, raw_rows)],
            down_raw.at[part % 2],
            weight_sems.at[4 + part % 2],
        )

    wide_copies[0].start()
    narrow_copy.start()
    raw_copy(0).start()
    raw_copy(1).start()
    wide_copies[1].start()
    wide_copies[2].start()

    def halo_copies(number, source_rows, target):
        made = []
        for side, peer in ((0, left), (1, right)):
            made.append(
                pltpu.make_async_remote_copy(
                    src_ref=source_rows(side),
                    dst_ref=target(1 - side),
                    send_sem=send_sems.at[number, side],
                    recv_sem=recv_sems.at[number, 1 - side],
                    device_id=(batch, peer),
                    device_id_type=MESH,
                )
            )
        return made

    sent = []

    def start_halo(number, width):
        made = halo_copies(
            number,
            lambda side: halo_out.at[number, side, :, pl.ds(RIM - width if side else 0, width)],
            lambda side: halo_in.at[number, side, :, pl.ds(RIM - width if side == 0 else 0, width)],
        )
        for copy in made:
            copy.start()
        sent.extend(made)
        return made

    def fill_rims(made, number, width):
        made[1].wait_recv()
        made[0].wait_recv()
        low = jnp.where(time > 0, 1.0, 0.0)
        high = jnp.where(time < time_count - 1, 1.0, 0.0)
        for crop in range(crops):
            start = RIM - width
            pad[crop, start:RIM, :] = halo_in[number, 0, crop, start:RIM, :].astype(f32) * low
            pad[crop, RIM + length : RIM + length + width, :] = (
                halo_in[number, 1, crop, 0:width, :].astype(f32) * high
            )

    def each_block(step, carry, edges_then=None):
        def edge(index, carry):
            side = lax.rem(index, 2)
            return step(index // 2, side * (per_crop - 1), carry, side)

        def inside(index, carry):
            return step(index // (per_crop - 2), 1 + lax.rem(index, per_crop - 2), carry, None)

        carry = lax.fori_loop(0, 2 * crops, edge, carry)
        made = edges_then() if edges_then is not None else None
        return lax.fori_loop(0, crops * (per_crop - 2), inside, carry), made

    def keep_edge(number, crop, side, rows):
        if side is not None:
            halo_out[number, side, crop] = rows

    def row_of(ref, row):
        return ref[row : row + 1, :]

    def valid_rows(crop, place):
        places = time * length + place * ROWS + lax.broadcasted_iota(jnp.int32, (ROWS, 1), 0)
        return jnp.where(places < lengths[crop], 1.0, 0.0)

    def reorder(part):
        raw_copy(part).wait()
        taps = down.shape[0]
        size = taps * 16
        rows = lax.broadcasted_iota(jnp.int32, (size, size), 0)
        columns = lax.broadcasted_iota(jnp.int32, (size, size), 1)
        swap = jnp.where(columns == lax.rem(rows, 16) * taps + rows // 16, 1.0, 0.0).astype(bf16)

        def step(index, carry):
            source = down_raw[part % 2, pl.ds(pl.multiple_of(index * size, size), size), :]
            swapped = dot(swap, source, 1, 0).astype(bf16)
            at = pl.multiple_of(part * (raw_rows // taps) + index * 16, 16)
            for tap in range(taps):
                down[tap, pl.ds(at, 16), :] = swapped[tap * 16 : (tap + 1) * 16, :]
            return carry

        lax.fori_loop(0, raw_rows // size, step, 0, unroll=4)
        if part + 2 < parts:
            raw_copy(part + 2).start()

    frame_rows = lax.broadcasted_iota(jnp.int32, (frames_all, 1), 0)
    frame_place = time * frame_count + lax.rem(frame_rows, frame_count)
    frame_length = jnp.where(frame_rows < frame_count, lengths[0], lengths[crops - 1])
    frame_valid = jnp.where(STRIDE * frame_place < frame_length, 1.0, 0.0)
    code_lanes = lax.broadcasted_iota(jnp.int32, (frames_all, codebook.shape[1]), 1)

    def onehot(phase):
        return jnp.where(codes[:, phase : phase + 1] == code_lanes, 1.0, 0.0).astype(bf16)

    for phase in range(phases):
        rows = codebook[phase * dims : (phase + 1) * dims, :]
        three = jnp.concatenate([part.astype(f32) for part in split_three(rows)], axis=0)
        found = dot(three.astype(bf16), onehot(phase), 1, 1)
        looked[phase * dims : (phase + 1) * dims, :] = (
            found[:dims] + found[dims : 2 * dims] + found[2 * dims :]
        )
    looked_rows = looked[...].T
    quantized[...] = (
        (exact(looked_rows, out_weight[...], 1, 0) + jnp.sum(out_bias[...], axis=0, keepdims=True))
        * frame_valid
    ).reshape(quantized.shape)
    phase_of_row = lax.broadcasted_iota(jnp.int32, (count, count), 0) // dims
    phase_of_column = lax.broadcasted_iota(jnp.int32, (count, count), 1) // dims
    earlier = jnp.where(phase_of_row < phase_of_column, 1.0, 0.0)
    later = jnp.where(phase_of_row > phase_of_column, 1.0, 0.0)
    crossing = exact(out_weight[...], in_weight[...], 1, 1) * earlier
    bias_terms = exact(out_bias[...], in_weight[...], 1, 1)
    nine_rows = lax.broadcasted_iota(jnp.int32, (phases, count), 0)
    nine_columns = lax.broadcasted_iota(jnp.int32, (phases, count), 1) // dims
    bias_terms = jnp.sum(jnp.where(nine_rows < nine_columns, bias_terms, 0.0), axis=0, keepdims=True)
    correction[...] = exact(looked_rows, crossing, 1, 0) + bias_terms - in_bias[...]

    for crop in range(crops):
        places = time * length + lax.broadcasted_iota(jnp.int32, (length, 1), 0)
        keep = jnp.where(places < lengths[crop], 1.0, 0.0)
        hidden[0, crop * length : (crop + 1) * length, :] = signal[crop].T * keep

    pl.semaphore_wait(barrier, 2)

    def block_rows(crop, place):
        return pl.ds(pl.multiple_of((crop * per_crop + place) * ROWS, ROWS), ROWS)

    def pad_rows(place):
        return pl.ds(pl.multiple_of(RIM + place * ROWS, ROWS), ROWS)

    for unit in range(3):
        dilation = DILATIONS[unit]
        width = 16 if 3 * dilation <= 16 else 32
        alpha = row_of(snake_alpha, 2 * unit)
        inverse = 1.0 / alpha

        def first_snake(crop, place, carry, side):
            low = snake_of(hidden[unit, block_rows(crop, place), :], alpha, inverse).astype(bf16)
            pad[crop, pad_rows(place), :] = low.astype(f32)
            keep_edge(unit, crop, side, low)
            return carry

        _, made = each_block(first_snake, 0, lambda: start_halo(unit, width))
        for part in range(unit * parts // 4, (unit + 1) * parts // 4):
            reorder(part)
        fill_rims(made, unit, width)
        for tap in range(TAPS):
            for crop in range(crops):
                start = RIM + (tap - 3) * dilation
                windows[unit, tap, crop * length : (crop + 1) * length, :] = pad[
                    crop, start : start + length, :
                ].astype(bf16)
        wide_copies[unit].wait()
        total = None
        for tap in range(TAPS):
            term = dot(windows[unit, tap], wide[unit, tap], 1, 1)
            total = term if total is None else total + term
        conv[unit] = total + row_of(wide_bias, unit)
        alpha = row_of(snake_alpha, 2 * unit + 1)
        inverse = 1.0 / alpha

        def second_snake(index, carry):
            at = pl.ds(pl.multiple_of(index * ROWS, ROWS), ROWS)
            rounded[unit, at, :] = snake_of(conv[unit, at, :], alpha, inverse).astype(bf16)
            return carry

        lax.fori_loop(0, blocks, second_snake, 0)
        if unit == 0:
            narrow_copy.wait()
        hidden[unit + 1] = (
            hidden[unit] + dot(rounded[unit], narrow[unit], 1, 1) + row_of(narrow_bias, unit)
        )

    lane_tiles = channels // 128
    stretch = length + 16
    alpha = row_of(snake_alpha, 6)
    inverse = 1.0 / alpha

    def last_snake(crop, place, carry, side):
        values = snake_of(hidden[3, block_rows(crop, place), :], alpha, inverse)
        low = (values * valid_rows(crop, place)).astype(bf16)
        keep_edge(3, crop, side, low)
        wider = low.astype(f32)
        for tile in range(lane_tiles):
            at = pl.multiple_of((tile * crops + crop) * stretch + 8 + place * ROWS, 8)
            mixed_pad[pl.ds(at, ROWS), :] = wider[:, tile * 128 : (tile + 1) * 128]
        return carry

    _, made = each_block(last_snake, 0, lambda: start_halo(3, 16))
    for part in range(3 * parts // 4, parts):
        reorder(part)
    made[1].wait_recv()
    made[0].wait_recv()
    low = jnp.where(time > 0, 1.0, 0.0)
    high = jnp.where(time < time_count - 1, 1.0, 0.0)
    for crop in range(crops):
        before = halo_in[3, 0, crop, RIM - 16 : RIM, :].astype(f32)[8:] * low
        after = halo_in[3, 1, crop, 0:16, :].astype(f32)[:8] * high
        for tile in range(lane_tiles):
            base = (tile * crops + crop) * stretch
            lanes = slice(tile * 128, (tile + 1) * 128)
            mixed_pad[base : base + 8, :] = before[:, lanes]
            mixed_pad[base + 8 + length : base + 16 + length, :] = after[:, lanes]
    taps = frames.shape[0]
    for tap in range(taps):
        for crop in range(crops):
            for tile in range(lane_tiles):
                base = (tile * crops + crop) * stretch + tap + 4
                frames[
                    tap,
                    crop * frame_count : (crop + 1) * frame_count,
                    tile * 128 : (tile + 1) * 128,
                ] = mixed_pad[pl.ds(base, frame_count, stride=STRIDE), :].astype(bf16)
    phases_out[...] = frames[taps // 2 - STRIDE // 2 : taps // 2 + STRIDE // 2]
    total = None
    for tap in range(taps):
        term = dot(frames[tap], down[tap], 1, 1)
        total = term if total is None else total + term
    latent[...] = total + down_bias[...]

    gap = exact(latent[...], in_weight[...], 1, 1) - correction[...] - looked_rows
    grouping = jnp.where(
        lax.broadcasted_iota(jnp.int32, (count, phases), 0) // dims
        == lax.broadcasted_iota(jnp.int32, (count, phases), 1),
        1.0,
        0.0,
    )
    commit[...] = exact(gap * gap, grouping, 1, 0) * frame_valid
    gap_back = 2.0 * (exact(commit_cot[...] * frame_valid, grouping, 1, 1) * gap)
    gap_grad[...] = gap_back
    lowered = exact(gap_back, in_weight[...], 1, 0).astype(bf16)
    latent_low[...] = lowered.reshape(latent_low.shape)

    made = halo_copies(4, lambda side: latent_low, lambda side: latent_in.at[side])
    for copy in made:
        copy.start()
    sent.extend(made)

    push = quant_cot[...].reshape(frames_all, latents) * frame_valid
    gap_back = gap_grad[...]
    looked_rows = looked[...].T
    between = exact(looked_rows, gap_back, 0, 0)
    small[...] = jnp.zeros_like(small)

    def keep_small(row, rows):
        for index in range(time_count):
            columns = rows[:, index * wide_of : (index + 1) * wide_of]
            done = 0
            while done < rows.shape[0]:
                fold, at = divmod(row + done, 128)
                size = min(rows.shape[0] - done, 128 - at)
                small[index, at : at + size, fold * wide_of : (fold + 1) * wide_of] = columns[
                    done : done + size
                ]
                done += size

    def keep_channels(row, rows):
        fold, at = divmod(row, 128)
        for index in range(time_count):
            small[index, at : at + rows.shape[0], fold * wide_of : fold * wide_of + share] = rows[
                :, index * share : (index + 1) * share
            ]

    earlier_rows = jnp.where(
        lax.broadcasted_iota(jnp.int32, (count, phases), 0) // dims
        > lax.broadcasted_iota(jnp.int32, (count, phases), 1),
        1.0,
        0.0,
    )
    ones = jnp.ones((frames_all, phases), f32)
    keep_small(
        0,
        exact(gap_back, latent[...], 0, 0)
        - exact(exact(gap_back, looked_rows, 0, 0) * later, out_weight[...], 1, 0)
        - exact(exact(gap_back, ones, 0, 0) * earlier_rows, out_bias[...], 1, 0),
    )
    looked_back = exact(push, out_weight[...], 1, 1) - gap_back
    crossing = exact(out_weight[...], in_weight[...], 1, 1) * earlier
    looked_back = (looked_back - exact(gap_back, crossing, 1, 1)).T
    for phase in range(phases):
        rows = looked_back[phase * dims : (phase + 1) * dims, :]
        three = jnp.concatenate([part.astype(f32) for part in split_three(rows)], axis=0)
        found = dot(three.astype(bf16), onehot(phase), 1, 0)
        keep_small(
            count + phase * dims, found[:dims] + found[dims : 2 * dims] + found[2 * dims :]
        )
    keep_small(
        2 * count,
        exact(looked_rows, push, 0, 0) - exact(between * earlier, in_weight[...], 1, 0),
    )
    gap_sum = jnp.sum(gap_back, axis=0, keepdims=True)
    keep_small(
        3 * count,
        jnp.sum(push, axis=0, keepdims=True)
        - exact(jnp.where(nine_rows < nine_columns, gap_sum, 0.0), in_weight[...], 1, 0),
    )
    lowered = latent_low[...].reshape(frames_all, latents).astype(f32)
    row = 3 * count + phases
    keep_small(row, jnp.sum(lowered, axis=0, keepdims=True))
    wide_bias_row, narrow_bias_row, alpha_row, in_bias_row = row + 1, row + 4, row + 7, row + 14
    fold, at = divmod(in_bias_row, 128)
    for index in range(time_count):
        small[index, at : at + 1, fold * wide_of : fold * wide_of + count] = gap_sum

    made[1].wait_recv()
    made[0].wait_recv()
    latent_pad[...] = jnp.zeros_like(latent_pad)
    for crop in range(crops):
        own = lowered[crop * frame_count : (crop + 1) * frame_count, :]
        latent_pad[crop, 8 : 8 + frame_count, :] = own
        before = latent_in[0, crop].astype(f32)[frame_count - 1 :, :] * low
        after = latent_in[1, crop].astype(f32)[:1, :] * high
        latent_pad[crop, 7:8, :] = before
        latent_pad[crop, 8 + frame_count : 9 + frame_count, :] = after
    reach = frame_count + 8
    same = jnp.concatenate([latent_pad[crop, 8 : 8 + reach, :] for crop in range(crops)], axis=0)
    previous = jnp.concatenate([latent_pad[crop, 7 : 7 + reach, :] for crop in range(crops)], axis=0)
    same, previous = same.astype(bf16), previous.astype(bf16)
    run = reach * STRIDE
    for step in range(STRIDE):
        both = dot(same, down[step], 1, 0) + dot(previous, down[step + STRIDE], 1, 0)
        for crop in range(crops):
            for tile in range(lane_tiles):
                base = (tile * crops + crop) * run + step
                spread[pl.ds(base, reach, stride=STRIDE), :] = both[
                    crop * reach : (crop + 1) * reach, tile * 128 : (tile + 1) * 128
                ]

    alpha = row_of(snake_alpha, 6)
    inverse = 1.0 / alpha
    zero = jnp.zeros((8, channels), f32)

    def mixed_back(crop, place, carry, side):
        pieces = []
        for tile in range(lane_tiles):
            at = (tile * crops + crop) * run + STRIDE // 2 + place * ROWS
            pieces.append(spread[pl.ds(at, ROWS), :])
        upstream = jnp.concatenate(pieces, axis=1) * valid_rows(crop, place)
        at = block_rows(crop, place)
        slope, alpha_slope = snake_slopes(hidden[3, at, :], alpha, inverse)
        following = upstream * slope
        grad[at, :] = following
        branch[at, :] = following.astype(bf16)
        return (
            carry[0] + folded(upstream * alpha_slope),
            carry[1] + folded(following.astype(bf16).astype(f32)),
        )

    (alpha_sum, bias_sum), _ = each_block(mixed_back, (zero, zero))
    keep_channels(alpha_row + 6, jnp.sum(alpha_sum, axis=0, keepdims=True))

    unit_rows = units.shape[2]
    out_copies = []
    for unit in (2, 1, 0):
        dilation = DILATIONS[unit]
        width = 16 if 3 * dilation <= 16 else 32
        slot = unit % 2
        number = 5 + unit
        keep_channels(narrow_bias_row + unit, jnp.sum(bias_sum, axis=0, keepdims=True))
        work[...] = dot(branch[...], narrow[unit], 1, 0)
        alpha = row_of(snake_alpha, 2 * unit + 1)
        inverse = 1.0 / alpha

        def conv_back(crop, place, carry, side):
            at = block_rows(crop, place)
            upstream = work[at, :]
            slope, alpha_slope = snake_slopes(conv[unit, at, :], alpha, inverse)
            lowered = (upstream * slope).astype(bf16)
            moved[at, :] = lowered
            wider = lowered.astype(f32)
            pad[crop, pad_rows(place), :] = wider
            keep_edge(number, crop, side, lowered)
            return carry[0] + folded(upstream * alpha_slope), carry[1] + folded(wider)

        (alpha_sum, bias_sum), made = each_block(
            conv_back, (zero, zero), lambda: start_halo(number, width)
        )
        keep_channels(alpha_row + 2 * unit + 1, jnp.sum(alpha_sum, axis=0, keepdims=True))
        keep_channels(wide_bias_row + unit, jnp.sum(bias_sum, axis=0, keepdims=True))
        if unit == 0:
            out_copies[0].wait()

        def keep_unit(row, rows):
            rows = rows.astype(bf16)
            for index in range(time_count):
                units[slot, index, row : row + share, :] = rows[index * share : (index + 1) * share]

        for tap in range(TAPS):
            keep_unit(tap * share, dot(moved[...], windows[unit, tap], 0, 0))
        keep_unit(TAPS * share, dot(branch[...], rounded[unit], 0, 0))
        copy = pltpu.make_async_copy(
            units.at[slot],
            packed.at[:, pl.ds(small_rows + (2 - unit) * unit_rows, unit_rows)],
            out_sems.at[unit],
        )
        copy.start()
        out_copies.append(copy)
        fill_rims(made, number, width)
        total = None
        for tap in range(TAPS):
            start = RIM - (tap - 3) * dilation
            shifted = jnp.concatenate(
                [pad[crop, start : start + length, :].astype(bf16) for crop in range(crops)], axis=0
            )
            term = dot(shifted, wide[unit, tap], 1, 0)
            total = term if total is None else total + term
        work[...] = total
        alpha = row_of(snake_alpha, 2 * unit)
        inverse = 1.0 / alpha

        def hidden_back(crop, place, carry, side):
            at = block_rows(crop, place)
            upstream = work[at, :]
            slope, alpha_slope = snake_slopes(hidden[unit, at, :], alpha, inverse)
            following = grad[at, :] + upstream * slope
            if unit == 0:
                following = following * valid_rows(crop, place)
            grad[at, :] = following
            lowered = following.astype(bf16)
            branch[at, :] = lowered
            return (
                carry[0] + folded(upstream * alpha_slope),
                carry[1] + folded(lowered.astype(f32)),
            )

        (alpha_sum, bias_sum), _ = each_block(hidden_back, (zero, zero))
        keep_channels(alpha_row + 2 * unit, jnp.sum(alpha_sum, axis=0, keepdims=True))

    small_low[...] = small[...].astype(bf16)
    for start in range(0, small_rows, 128):
        copy = pltpu.make_async_copy(
            small_low, packed.at[:, pl.ds(start, 128)], out_sems.at[3 + start // 128]
        )
        copy.start()
        out_copies.append(copy)
    for crop in range(crops):
        signal_grad[crop] = grad[crop * length : (crop + 1) * length, :].T
    for copy in out_copies[1:]:
        copy.wait()
    for copy in sent:
        copy.wait_send()


def run_block(time_count, small_rows, lengths, *arrays):
    (signal, quant_cot, commit_cot, codes, wide, _, narrow, _, _, down, down_bias) = arrays[:11]
    f32, bf16 = jnp.float32, jnp.bfloat16
    crops, channels, length = signal.shape
    latents = down_bias.shape[1]
    taps = down.shape[0] // latents
    frames = crops * (length // STRIDE)
    rows = crops * length
    phases = codes.shape[1]
    count = arrays[11].shape[0]
    unit_rows = (TAPS + 1) * (channels // time_count)
    vmem = pl.BlockSpec(memory_space=pltpu.VMEM)
    hbm = pl.BlockSpec(memory_space=pl.ANY)
    in_specs = [pl.BlockSpec(memory_space=pltpu.SMEM)] + [vmem] * len(arrays)
    for place in (4, 6, 9):
        in_specs[1 + place] = hbm
    lane_tiles = channels // 128
    dma = pltpu.SemaphoreType.DMA
    return pl.pallas_call(
        functools.partial(block_kernel, time_count, small_rows),
        out_shape=(
            jax.ShapeDtypeStruct(quant_cot.shape, f32),
            jax.ShapeDtypeStruct((frames, phases), f32),
            jax.ShapeDtypeStruct(signal.shape, f32),
            jax.ShapeDtypeStruct((time_count, small_rows + 3 * unit_rows, channels), bf16),
            jax.ShapeDtypeStruct((STRIDE, frames, channels), bf16),
            jax.ShapeDtypeStruct(quant_cot.shape, bf16),
        ),
        in_specs=in_specs,
        out_specs=(vmem, vmem, vmem, hbm, vmem, vmem),
        scratch_shapes=[
            pltpu.VMEM(wide.shape, bf16),
            pltpu.VMEM(narrow.shape, bf16),
            pltpu.VMEM((taps, latents, channels), bf16),
            pltpu.VMEM((2, down.shape[0] // 16, channels), bf16),
            pltpu.VMEM((4, rows, channels), f32),
            pltpu.VMEM((3, rows, channels), f32),
            pltpu.VMEM((3, TAPS, rows, channels), bf16),
            pltpu.VMEM((3, rows, channels), bf16),
            pltpu.VMEM((crops, length + 2 * RIM, channels), f32),
            pltpu.VMEM((rows, channels), f32),
            pltpu.VMEM((rows, channels), f32),
            pltpu.VMEM((rows, channels), bf16),
            pltpu.VMEM((rows, channels), bf16),
            pltpu.VMEM((lane_tiles * crops * (length + 16), 128), f32),
            pltpu.VMEM((taps, frames, channels), bf16),
            pltpu.VMEM((frames, latents), f32),
            pltpu.VMEM((crops, 16 + length // STRIDE, latents), f32),
            pltpu.VMEM((lane_tiles * crops * (length + 8 * STRIDE), 128), f32),
            pltpu.VMEM((count, frames), f32),
            pltpu.VMEM((frames, count), f32),
            pltpu.VMEM((frames, count), f32),
            pltpu.VMEM((2, time_count, unit_rows, channels), bf16),
            pltpu.VMEM((time_count, 128, channels), f32),
            pltpu.VMEM((time_count, 128, channels), bf16),
            pltpu.VMEM((8, 2, crops, RIM, channels), bf16),
            pltpu.VMEM((8, 2, crops, RIM, channels), bf16),
            pltpu.VMEM((2,) + quant_cot.shape, bf16),
            dma((6,)),
            dma((3 + small_rows // 128,)),
            dma((8, 2)),
            dma((8, 2)),
        ],
        compiler_params=pltpu.CompilerParams(
            collective_id=1, has_side_effects=True, vmem_limit_bytes=60 * 2**20
        ),
    )(lengths, *arrays)


def add_rows(rows, sources, target):
    def step(index, carry):
        at = index * BLOCK
        total = None
        for ref, start in sources:
            block = ref[pl.ds(start + at, BLOCK), :].astype(jnp.float32)
            total = block if total is None else total + block
        ref, start = target
        ref[pl.ds(start + at, BLOCK), :] = total.astype(ref.dtype)
        return carry

    lax.fori_loop(0, rows // BLOCK, step, 0)


def reduce_kernel(pieces, batch_size, packed, final, own, from_core, to_x, from_x, to_y, from_y, to_z, from_z, local_sems, send_sems, recv_sems):
    members = batch_size // 2
    batch = lax.axis_index("batch")
    time = lax.axis_index("tm")
    low, high = lax.rem(time, 2), time // 2
    core = 2 * high + 1 - low
    across = 2 * (1 - high) + low
    half = lax.rem(batch, 2)
    place = batch // 2
    pair = 2 * place + 1 - half

    def member(step):
        return 2 * lax.rem(place + step, members) + half

    barrier = pltpu.get_barrier_semaphore()
    peers = [(batch, core), (batch, across), (pair, time)]
    peers += [(member(step), time) for step in range(1, members)]
    for peer in peers:
        pl.semaphore_signal(barrier, inc=1, device_id=peer, device_id_type=MESH)
    pl.semaphore_wait(barrier, len(peers))

    def send(source, target, number, slot, device):
        return pltpu.make_async_remote_copy(
            src_ref=source,
            dst_ref=target,
            send_sem=send_sems.at[number, slot],
            recv_sem=recv_sems.at[number, slot],
            device_id=device,
            device_id_type=MESH,
        )

    spread = members - 1
    slot_y, slot_z, slot_back, slot_last = 3, 4, 4 + spread, 4 + 2 * spread
    copies = {}
    for number, (start, rows) in enumerate(pieces):
        here = pl.ds(start, rows)
        copies[number, 0] = send(
            packed.at[core, here], from_core.at[0, here], number, 0, (batch, core)
        )
        far = 2 * (1 - high) + 1 - low
        copies[number, 1] = send(
            packed.at[far, here], from_core.at[1, here], number, 1, (batch, core)
        )
        copies[number, 1].start()
        copies[number, 0].start()
    locals_ = []
    for number, (start, rows) in enumerate(pieces):
        here = pl.ds(start, rows)
        first = pltpu.make_async_copy(packed.at[across, here], own.at[1, here], local_sems.at[number, 1])
        second = pltpu.make_async_copy(packed.at[time, here], own.at[0, here], local_sems.at[number, 0])
        first.start()
        second.start()
        locals_.append((second, first))

    def stage_core(number):
        start, rows = pieces[number]
        locals_[number][1].wait()
        copies[number, 1].wait_recv()
        add_rows(rows, [(own.at[1], start), (from_core.at[1], start)], (to_x, start))
        here = pl.ds(start, rows)
        copies[number, 2] = send(to_x.at[here], from_x.at[here], number, 2, (batch, across))
        copies[number, 2].start()

    def stage_x(number):
        start, rows = pieces[number]
        locals_[number][0].wait()
        copies[number, 0].wait_recv()
        copies[number, 2].wait_recv()
        add_rows(
            rows, [(own.at[0], start), (from_core.at[0], start), (from_x, start)], (to_y, start)
        )
        other = pl.ds(start + (1 - half) * (rows // 2), rows // 2)
        copies[number, slot_y] = send(
            to_y.at[other], from_y.at[pl.ds(start // 2, rows // 2)], number, slot_y, (pair, time)
        )
        copies[number, slot_y].start()

    def stage_y(number):
        start, rows = pieces[number]
        copies[number, slot_y].wait_recv()
        add_rows(
            rows // 2,
            [(to_y, start + half * (rows // 2)), (from_y, start // 2)],
            (to_z, start // 2),
        )
        chunk = rows // batch_size
        for step in range(1, members):
            target = lax.rem(place + step, members)
            copies[number, slot_z + step - 1] = send(
                to_z.at[pl.ds(start // 2 + target * chunk, chunk)],
                from_z.at[step - 1, pl.ds(start // batch_size, chunk)],
                number,
                slot_z + step - 1,
                (member(step), time),
            )
            copies[number, slot_z + step - 1].start()

    def stage_z(number):
        start, rows = pieces[number]
        chunk = rows // batch_size
        for step in range(1, members):
            copies[number, slot_z + step - 1].wait_recv()
        mine = start + half * (rows // 2) + place * chunk
        sources = [(to_z, start // 2 + place * chunk)]
        sources += [(from_z.at[step], start // batch_size) for step in range(members - 1)]
        total = None
        for ref, at in sources:
            block = ref[pl.ds(at, chunk), :].astype(jnp.float32)
            total = block if total is None else total + block
        final[pl.ds(mine, chunk), :] = total.astype(final.dtype)
        for step in range(1, members):
            copies[number, slot_back + step - 1] = send(
                final.at[pl.ds(mine, chunk)],
                final.at[pl.ds(mine, chunk)],
                number,
                slot_back + step - 1,
                (member(step), time),
            )
            copies[number, slot_back + step - 1].start()

    def stage_back(number):
        start, rows = pieces[number]
        for step in range(1, members):
            copies[number, slot_back + step - 1].wait_recv()
        mine = pl.ds(start + half * (rows // 2), rows // 2)
        copies[number, slot_last] = send(
            final.at[mine], final.at[mine], number, slot_last, (pair, time)
        )
        copies[number, slot_last].start()

    def stage_last(number):
        copies[number, slot_last].wait_recv()

    stages = [stage_core, stage_x, stage_y, stage_z, stage_back, stage_last]
    for wave in range(len(pieces) + len(stages) - 1):
        for depth in range(len(stages)):
            number = wave - depth
            if 0 <= number < len(pieces):
                stages[depth](number)
    for copy in copies.values():
        copy.wait_send()


def reduce_all(packed, pieces, batch_size):
    rows, width = packed.shape[1:]
    members = batch_size // 2
    slots = 5 + 2 * (members - 1)
    kind = packed.dtype
    return pl.pallas_call(
        functools.partial(reduce_kernel, pieces, batch_size),
        out_shape=jax.ShapeDtypeStruct((rows, width), kind),
        in_specs=[pl.BlockSpec(memory_space=pl.ANY)],
        out_specs=pl.BlockSpec(memory_space=pltpu.VMEM),
        scratch_shapes=[
            pltpu.VMEM((2, rows, width), kind),
            pltpu.VMEM((2, rows, width), kind),
            pltpu.VMEM((rows, width), kind),
            pltpu.VMEM((rows, width), kind),
            pltpu.VMEM((rows, width), kind),
            pltpu.VMEM((rows // 2, width), kind),
            pltpu.VMEM((rows // 2, width), kind),
            pltpu.VMEM((members - 1, rows // batch_size, width), kind),
            pltpu.SemaphoreType.DMA((len(pieces), 2)),
            pltpu.SemaphoreType.DMA((len(pieces), slots)),
            pltpu.SemaphoreType.DMA((len(pieces), slots)),
        ],
        compiler_params=pltpu.CompilerParams(
            collective_id=0, has_side_effects=True, vmem_limit_bytes=56 * 2**20
        ),
    )(packed)


def down_kernel(lows, phases, out, held, columns, in_sems, out_sems):
    count = lows.shape[2]
    group, lanes = held.shape[1], held.shape[4]
    rows = group * held.shape[3]
    tiles = lanes // 128
    groups = phases.shape[0] // group
    items = [(part, at) for part in range(phases.shape[3] // lanes) for at in range(groups)]
    loads = [
        pltpu.make_async_copy(
            phases.at[pl.ds(at * group, group), :, :, pl.ds(part * lanes, lanes)],
            held.at[index % 2],
            in_sems.at[index % 2],
        )
        for index, (part, at) in enumerate(items)
    ]
    for load in loads[:2]:
        load.start()
    stores = []
    after = before = None
    for index, (part, at) in enumerate(items):
        if after is None or groups > 1:
            turned = [lows[kind, at * rows : (at + 1) * rows].T for kind in range(3)]
            after = jnp.concatenate([turned[0], turned[1]], axis=0)
            before = jnp.concatenate([turned[0], turned[2]], axis=0)
        loads[index].wait()
        for step in range(STRIDE):
            block = held[index % 2, :, step].reshape(rows, lanes)
            late = step >= STRIDE // 2
            both = dot(after if late else before, block, 1, 0)
            middle = step + STRIDE // 2
            for tap, row in ((middle, 0), (middle - STRIDE if late else middle + STRIDE, count)):
                for tile in range(tiles):
                    place = pl.ds(tap, count, stride=2 * STRIDE)
                    value = both[row : row + count, tile * 128 : (tile + 1) * 128]
                    if at > 0:
                        value = value + columns[part * tiles + tile, place, :]
                    columns[part * tiles + tile, place, :] = value
        if index + 2 < len(items):
            loads[index + 2].start()
        if at == groups - 1:
            for tile in range(part * tiles, (part + 1) * tiles):
                stores.append(
                    pltpu.make_async_copy(
                        columns.at[tile], out.at[:, pl.ds(tile * 128, 128)], out_sems.at[tile]
                    )
                )
                stores[-1].start()
    for store in stores:
        store.wait()


def down_gradient(lows, phases):
    devices, _, rows, channels = phases.shape
    count = lows.shape[2]
    lanes = 256
    hbm = pl.BlockSpec(memory_space=pl.ANY)
    return pl.pallas_call(
        down_kernel,
        out_shape=jax.ShapeDtypeStruct((count * 2 * STRIDE, channels), jnp.float32),
        in_specs=[pl.BlockSpec(memory_space=pltpu.VMEM), hbm],
        out_specs=hbm,
        scratch_shapes=[
            pltpu.VMEM((2, min(devices, 32), STRIDE, rows, lanes), phases.dtype),
            pltpu.VMEM((channels // 128, count * 2 * STRIDE, 128), jnp.float32),
            pltpu.SemaphoreType.DMA((2,)),
            pltpu.SemaphoreType.DMA((channels // 128,)),
        ],
        compiler_params=pltpu.CompilerParams(vmem_limit_bytes=60 * 2**20),
    )(lows, phases)


def body(
    signal,
    quant_cot,
    commit_cot,
    lengths,
    codes,
    wide_weight,
    wide_bias,
    narrow_weight,
    narrow_bias,
    snake_alpha,
    down_weight,
    down_bias,
    in_weight,
    in_bias,
    codebook,
    out_weight,
    out_bias,
):
    time_count = lax.axis_size("tm")
    batch_count = lax.axis_size("batch")
    crop_count, channel_count, length = signal.shape
    latent_count, tap_count, _ = down_weight.shape
    phases, dims = in_weight.shape[:2]
    count = phases * dims
    frame_count = length // STRIDE
    small_rows = 16 * batch_count
    quantized, commit, signal_grad, packed, own_phases, latent_low = run_block(
        time_count,
        small_rows,
        lengths,
        signal,
        quant_cot,
        jnp.swapaxes(commit_cot, 1, 2).reshape(-1, phases),
        jnp.swapaxes(codes, 1, 2).reshape(-1, phases),
        jnp.swapaxes(wide_weight, 1, 2),
        wide_bias,
        narrow_weight,
        narrow_bias,
        snake_alpha,
        down_weight.reshape(-1, channel_count),
        down_bias.reshape(1, -1),
        in_weight.reshape(count, -1),
        in_bias.reshape(1, -1),
        codebook.reshape(count, -1),
        out_weight.reshape(count, -1),
        out_bias,
    )
    commit = jnp.swapaxes(commit.reshape(crop_count, frame_count, phases), 1, 2)

    all_phases = lax.all_gather(own_phases, ("batch", "tm"))
    all_low = lax.all_gather(latent_low, ("batch", "tm"))
    share = latent_count // time_count
    mine = lax.dynamic_slice_in_dim(all_low, lax.axis_index("tm") * share, share, axis=3)
    mine = mine.reshape(batch_count, time_count, crop_count, frame_count, share)
    line = jnp.swapaxes(mine, 1, 2).reshape(-1, time_count * frame_count, share)
    after = jnp.pad(line[:, 1:], ((0, 0), (0, 1), (0, 0)))
    before = jnp.pad(line[:, :-1], ((0, 0), (1, 0), (0, 0)))
    lows = jnp.stack([line, after, before])
    lows = lows.reshape(3, batch_count, crop_count, time_count, frame_count, share)
    lows = jnp.swapaxes(lows, 2, 3).reshape(3, -1, share)

    unit_extent = (packed.shape[1] - small_rows) // 3
    piece = max(unit_extent // 2, 16 * batch_count)
    pieces = [(0, small_rows)]
    pieces += [(at, piece) for at in range(small_rows, packed.shape[1], piece)]
    summed = reduce_all(packed, tuple(pieces), batch_count)

    wide_of = latent_count // time_count
    small = summed[:128].astype(jnp.float32)
    small = jnp.concatenate([small[:, :wide_of], small[:, wide_of : 2 * wide_of]], axis=0)
    in_weight_out = small[:count].reshape(phases, dims, -1)
    codebook_out = small[count : 2 * count].reshape(phases, dims, -1)
    out_weight_out = small[2 * count : 3 * count].reshape(phases, dims, -1)
    row = 3 * count + phases
    out_bias_out = small[3 * count : row]
    down_bias_out = small[row]
    narrow_of = channel_count // time_count
    wide_bias_out = small[row + 1 : row + 4, :narrow_of]
    narrow_bias_out = small[row + 4 : row + 7, :narrow_of]
    alpha_out = small[row + 7 : row + 14, :narrow_of]
    in_bias_all = small[row + 14, :count].reshape(phases, dims)
    part = dims // time_count
    in_bias_out = lax.dynamic_slice_in_dim(in_bias_all, lax.axis_index("tm") * part, part, axis=1)
    units = summed[small_rows:].reshape(3, unit_extent, channel_count)[::-1].astype(jnp.float32)
    wide_out = units[:, : TAPS * narrow_of].reshape(3, TAPS, narrow_of, channel_count)
    wide_out = jnp.swapaxes(wide_out, 1, 2)
    narrow_out = units[:, TAPS * narrow_of :]
    down_out = down_gradient(lows, all_phases).reshape(share, tap_count, channel_count)
    return (
        quantized,
        commit,
        signal_grad,
        wide_out,
        wide_bias_out,
        narrow_out,
        narrow_bias_out,
        alpha_out,
        down_out,
        down_bias_out,
        in_weight_out,
        in_bias_out,
        codebook_out,
        out_weight_out,
        out_bias_out,
    )


def solution(mesh):
    return jax.shard_map(
        body,
        mesh=mesh,
        in_specs=(
            P("batch", None, "tm"),
            P("batch", "tm", None),
            P("batch", None, "tm"),
            P("batch"),
            P("batch", None, "tm"),
            P(),
            P(),
            P(),
            P(),
            P(),
            P(),
            P(),
            P(),
            P(),
            P(),
            P(),
            P(),
        ),
        out_specs=(
            P("batch", "tm", None),
            P("batch", None, "tm"),
            P("batch", None, "tm"),
            P(None, "tm", None, None),
            P(None, "tm"),
            P(None, "tm", None),
            P(None, "tm"),
            P(None, "tm"),
            P("tm", None, None),
            P("tm"),
            P(None, None, "tm"),
            P(None, "tm"),
            P(None, None, "tm"),
            P(None, None, "tm"),
            P(None, "tm"),
        ),
        check_vma=False,
    )
```

```python
import functools

import jax
import jax.numpy as jnp
from jax import lax
from jax.experimental import pallas as pl
from jax.experimental.pallas import tpu as pltpu
from jax.sharding import PartitionSpec as P

STRIDE = 8


DILATIONS = (1, 3, 9)
MESH = pl.DeviceIdType.MESH
BLOCK = 64


TAPS = 7
RIM = 32
ROWS = 32


def dot(left, right, left_dim, right_dim, precision=None):
    return lax.dot_general(
        left,
        right,
        (((left_dim,), (right_dim,)), ((), ())),
        precision=precision,
        preferred_element_type=jnp.float32,
    )


def exact(left, right, left_dim, right_dim):
    return dot(left, right, left_dim, right_dim, lax.Precision.HIGHEST)


def reduced_angle(angle):
    turns = jnp.floor(angle * 0.3183098861837907 + 0.5)
    rest = angle - turns * 3.140625
    rest = rest - turns * 9.67502593994140625e-4
    return rest - turns * 1.509957990978376432e-7


def sine(rest, square):
    series = -1.0 / 5040.0 + square * (1.0 / 362880.0 - square * (1.0 / 39916800.0))
    return rest + rest * square * (-1.0 / 6.0 + square * (1.0 / 120.0 + square * series))


def cosine(square):
    series = 1.0 / 40320.0 + square * (-1.0 / 3628800.0 + square * (1.0 / 479001600.0))
    return 1.0 + square * (-0.5 + square * (1.0 / 24.0 + square * (-1.0 / 720.0 + square * series)))


def snake_of(values, alpha, inverse):
    rest = reduced_angle(alpha * values)
    wave = sine(rest, rest * rest)
    return values + wave * wave * inverse


def snake_slopes(values, alpha, inverse):
    rest = reduced_angle(alpha * values)
    square = rest * rest
    wave = sine(rest, square)
    double = 2.0 * wave * cosine(square)
    return 1.0 + double, (values * double - wave * wave * inverse) * inverse


def split_three(values):
    first = values.astype(jnp.bfloat16)
    rest = values - first.astype(jnp.float32)
    second = rest.astype(jnp.bfloat16)
    third = (rest - second.astype(jnp.float32)).astype(jnp.bfloat16)
    return first, second, third


def folded(values):
    return jnp.sum(values.reshape(values.shape[0] // 8, 8, values.shape[1]), axis=0)


def block_kernel(
    time_count,
    batch_count,
    pieces,
    lengths,
    signal,
    quant_cot,
    coded,
    wide_hbm,
    wide_bias,
    narrow_hbm,
    narrow_bias,
    snake_alpha,
    down_hbm,
    down_bias,
    in_weight,
    in_bias,
    codebook,
    out_weight,
    out_bias,
    quantized,
    commit,
    signal_grad,
    final,
    all_phases,
    all_lows,
    wide,
    narrow,
    down,
    hidden,
    conv,
    gathered,
    pad,
    grad,
    work,
    branch,
    shares,
    share_all,
    share_pad,
    mixed_pad,
    frames,
    latent,
    latent_pad,
    spread,
    looked,
    gap_grad,
    correction,
    small,
    small_low,
    small_in,
    alpha_out,
    alpha_in,
    low_shares,
    low_all,
    halo_out,
    halo_in,
    latent_low,
    latent_in,
    signal_in,
    quant_in,
    coded_in,
    commit_out,
    signal_out,
    signal_back,
    swap_local,
    swap_send,
    swap_recv,
    from_pair,
    from_members,
    weight_sems,
    local_sems,
    send_sems,
    recv_sems,
    gather_send,
    gather_recv,
    relay_send,
    relay_recv,
    share_send,
    share_recv,
    small_send,
    small_recv,
    low_send,
    low_recv,
    block_send,
    block_recv,
    piece_send,
    piece_recv,
):
    f32, bf16 = jnp.float32, jnp.bfloat16
    sent = []
    batch = lax.axis_index("batch")
    time = lax.axis_index("tm")
    crops, channels, length = signal.shape
    latents = down_bias.shape[1]
    mine = time // crops
    side = lax.rem(time, crops)
    rows_all = crops * length
    blocks = rows_all // ROWS
    frame_count = length // STRIDE
    frames_all = crops * frame_count
    phases = out_bias.shape[0]
    dims = in_weight.shape[0] // phases
    count = phases * dims
    share = channels // time_count
    wide_of = latents // time_count

    core = crops * mine + 1 - side
    across = lax.rem(time + crops, time_count)
    members = batch_count // 2
    half = lax.rem(batch, 2)
    place_z = batch // 2
    pair = 2 * place_z + 1 - half

    def member(step):
        return 2 * lax.rem(place_z + step, members) + half

    def sibling(step):
        return lax.rem(time + step, time_count)

    peers = [(batch, sibling(step)) for step in range(1, time_count)]
    peers += [(pair, time)] + [(member(step), time) for step in range(1, members)]
    barrier = pltpu.get_barrier_semaphore()
    for peer in peers:
        pl.semaphore_signal(barrier, inc=1, device_id=peer, device_id_type=MESH)

    def remote(source, target, send_sem, recv_sem, device):
        copy = pltpu.make_async_remote_copy(
            src_ref=source,
            dst_ref=target,
            send_sem=send_sem,
            recv_sem=recv_sem,
            device_id=device,
            device_id_type=MESH,
        )
        copy.start()
        sent.append(copy)
        return copy

    wide_copies = [
        pltpu.make_async_copy(wide_hbm.at[unit], wide.at[unit], weight_sems.at[unit])
        for unit in range(3)
    ]
    narrow_copy = pltpu.make_async_copy(narrow_hbm, narrow, weight_sems.at[3])
    taps = frames.shape[0]
    group = 16 * taps
    quarter = down.shape[0] // 4
    down_copies = [
        pltpu.make_async_copy(
            down_hbm.at[pl.ds(part * quarter, quarter)],
            down.at[pl.ds(part * quarter, quarter)],
            weight_sems.at[4 + part],
        )
        for part in range(4)
    ]
    first, last = jnp.where(side == 0, 1.0, 0.0), jnp.where(side == 1, 1.0, 0.0)

    def swap(number, source, target, slot, back):
        made = []
        for part in range(crops):
            peer = crops * side + part if back else crops * part + mine
            origin = crops * part + mine if back else crops * side + part
            away = pltpu.make_async_remote_copy(
                src_ref=source(part),
                dst_ref=target(slot),
                send_sem=swap_send.at[number, part],
                recv_sem=swap_recv.at[number, slot],
                device_id=(batch, peer),
                device_id_type=MESH,
            )
            here = pltpu.make_async_copy(source(part), target(slot), swap_local.at[number])
            arrived = pltpu.make_async_remote_copy(
                src_ref=source(part),
                dst_ref=target(part),
                send_sem=swap_send.at[number, part],
                recv_sem=swap_recv.at[number, part],
                device_id=(batch, peer),
                device_id_type=MESH,
            )

            @pl.when(peer != time)
            def _():
                away.start()

            @pl.when(peer == time)
            def _():
                here.start()

            made.append((peer, origin, away, here, arrived))
        swaps.append(made)
        return made

    def swapped_in(made):
        for peer, origin, away, here, arrived in made:

            @pl.when(origin != time)
            def _():
                arrived.wait_recv()

            @pl.when(origin == time)
            def _():
                here.wait()

    swaps = []

    halo_rows = (16, 16, 32, 16, 0, 16, 16, 32)
    halo_start = [sum(halo_rows[:number]) for number in range(len(halo_rows))]

    def start_halo(number):
        rows = pl.ds(halo_start[number], halo_rows[number])
        return remote(
            halo_out.at[rows],
            halo_in.at[rows],
            send_sems.at[number],
            recv_sems.at[number],
            (batch, core),
        )

    def fill_rims(made, number):
        width, begin = halo_rows[number], halo_start[number]
        made.wait_recv()
        rim = halo_in[begin : begin + width, :].astype(f32)
        pad[RIM - width : RIM, :] = rim * last
        pad[RIM + rows_all : RIM + rows_all + width, :] = rim * first

    def each_block(step, carry, edge_then=None):
        carry = step((1 - side) * (blocks - 1), carry, True)
        made = edge_then() if edge_then is not None else None

        def inside(index, carry):
            return step(index + side, carry, False)

        return lax.fori_loop(0, blocks - 1, inside, carry), made

    def keep_edge(number, edge, rows):
        if edge:
            width, begin = halo_rows[number], halo_start[number]
            ahead, behind = rows[ROWS - width :].astype(f32), rows[:width].astype(f32)
            halo_out[begin : begin + width, :] = (ahead * first + behind * last).astype(bf16)

    def row_of(ref, row):
        return ref[row : row + 1, :]

    def valid_rows(place):
        places = side * rows_all + place * ROWS + lax.broadcasted_iota(jnp.int32, (ROWS, 1), 0)
        return jnp.where(places < lengths[mine], 1.0, 0.0)

    def reorder(part):
        rows = lax.broadcasted_iota(jnp.int32, (group, group), 0)
        columns = lax.broadcasted_iota(jnp.int32, (group, group), 1)
        turn = jnp.where(columns == lax.rem(rows, 16) * taps + rows // 16, 1.0, 0.0).astype(bf16)
        down_copies[part].wait()

        def step(index, carry):
            places = [
                pl.ds(pl.multiple_of(part * quarter + (4 * index + which) * group, group), group)
                for which in range(4)
            ]
            turned = [dot(turn, down[at, :], 1, 0).astype(bf16) for at in places]
            for at, rows in zip(places, turned):
                down[at, :] = rows
            return carry

        lax.fori_loop(0, quarter // group // 4, step, 0)

    def down_tap(tap):
        tiles = down.reshape(latents // 16, taps, 16, channels)
        return tiles[:, tap].reshape(latents, channels)

    pl.semaphore_wait(barrier, len(peers))
    swap_signal = swap(0, lambda part: signal.at[part], lambda slot: signal_in.at[slot], side, False)
    swap_quant = swap(1, lambda part: quant_cot.at[part], lambda slot: quant_in.at[slot], side, False)
    swap_coded = swap(2, lambda part: coded.at[part], lambda slot: coded_in.at[slot], side, False)
    wide_copies[0].start()
    narrow_copy.start()
    for copy in down_copies:
        copy.start()
    wide_copies[1].start()
    wide_copies[2].start()

    code_lanes = lax.broadcasted_iota(jnp.int32, (frames_all, codebook.shape[1]), 1).astype(f32)
    frame_rows = lax.broadcasted_iota(jnp.int32, (frames_all, 1), 0)

    def onehot(codes, phase):
        return jnp.where(codes[:, phase : phase + 1] == code_lanes, 1.0, 0.0).astype(bf16)

    def look_up(codes):
        found = []
        for phase in range(phases):
            rows = codebook[phase * dims : (phase + 1) * dims, :]
            three = jnp.concatenate([part.astype(f32) for part in split_three(rows)], axis=0)
            all_three = dot(three.astype(bf16), onehot(codes, phase), 1, 1)
            found.append(all_three[:dims] + all_three[dims : 2 * dims] + all_three[2 * dims :])
        return jnp.concatenate(found, axis=0).T

    looked_rows = look_up(coded[...].reshape(frames_all, -1))
    frame_place = time * frame_count + lax.rem(frame_rows, frame_count)
    frame_length = jnp.where(frame_rows < frame_count, lengths[0], lengths[crops - 1])
    frame_valid = jnp.where(STRIDE * frame_place < frame_length, 1.0, 0.0)
    quantized[...] = (
        (exact(looked_rows, out_weight[...], 1, 0) + jnp.sum(out_bias[...], axis=0, keepdims=True))
        * frame_valid
    ).reshape(quantized.shape)
    swapped_in(swap_coded)
    codes = coded_in[...].reshape(frames_all, -1)
    looked[...] = look_up(codes)
    looked_rows = looked[...]
    frame_place = side * frames_all + frame_rows
    frame_valid = jnp.where(STRIDE * frame_place < lengths[mine], 1.0, 0.0)
    phase_of_row = lax.broadcasted_iota(jnp.int32, (count, count), 0) // dims
    phase_of_column = lax.broadcasted_iota(jnp.int32, (count, count), 1) // dims
    earlier = jnp.where(phase_of_row < phase_of_column, 1.0, 0.0)
    later = jnp.where(phase_of_row > phase_of_column, 1.0, 0.0)
    crossing = exact(out_weight[...], in_weight[...], 1, 1) * earlier
    bias_terms = exact(out_bias[...], in_weight[...], 1, 1)
    nine_rows = lax.broadcasted_iota(jnp.int32, (phases, count), 0)
    nine_columns = lax.broadcasted_iota(jnp.int32, (phases, count), 1) // dims
    bias_terms = jnp.sum(jnp.where(nine_rows < nine_columns, bias_terms, 0.0), axis=0, keepdims=True)
    correction[...] = exact(looked_rows, crossing, 1, 0) + bias_terms - in_bias[...]

    for part in range(4):
        reorder(part)

    swapped_in(swap_signal)
    for part in range(crops):
        places = side * rows_all + part * length + lax.broadcasted_iota(jnp.int32, (length, 1), 0)
        keep = jnp.where(places < lengths[mine], 1.0, 0.0)
        hidden[0, part * length : (part + 1) * length, :] = signal_in[part].T * keep

    def block_rows(place):
        return pl.ds(pl.multiple_of(place * ROWS, ROWS), ROWS)

    def own_rows(place):
        return pl.ds(pl.multiple_of(side * rows_all + place * ROWS, ROWS), ROWS)

    own = pl.ds(pl.multiple_of(side * rows_all, rows_all), rows_all)

    def pad_rows(place):
        return pl.ds(pl.multiple_of(RIM + place * ROWS, ROWS), ROWS)

    def shifted(offset):
        start = RIM + offset
        return pad[start : start + rows_all, :].astype(bf16)

    gather_across, gather_core = {}, {}

    def gather(unit):
        slot = gathered.at[unit, :, mine, own]
        gather_across[unit] = remote(
            slot, slot, gather_send.at[unit, 0], gather_recv.at[unit, 0], (batch, across)
        )
        gather_core[unit] = remote(
            slot, slot, gather_send.at[unit, 1], gather_recv.at[unit, 1], (batch, core)
        )

    for unit in range(3):
        dilation = DILATIONS[unit]
        alpha = row_of(snake_alpha, 2 * unit)
        inverse = 1.0 / alpha

        def first_snake(place, carry, edge):
            low = snake_of(hidden[unit, block_rows(place), :], alpha, inverse).astype(bf16)
            gathered[unit, 0, mine, own_rows(place), :] = low
            pad[pad_rows(place), :] = low.astype(f32)
            keep_edge(unit, edge, low)
            return carry

        _, made = each_block(first_snake, 0, lambda: start_halo(unit))
        fill_rims(made, unit)
        wide_copies[unit].wait()
        result = None
        for tap in range(TAPS):
            term = dot(shifted((tap - 3) * dilation), wide[unit, tap], 1, 1)
            result = term if result is None else result + term
        conv[unit] = result + row_of(wide_bias, unit)
        alpha = row_of(snake_alpha, 2 * unit + 1)
        inverse = 1.0 / alpha

        def second_snake(place, carry, edge):
            values = snake_of(conv[unit, block_rows(place), :], alpha, inverse)
            gathered[unit, 1, mine, own_rows(place), :] = values.astype(bf16)
            return carry

        each_block(second_snake, 0)
        if unit == 0:
            narrow_copy.wait()
        if unit != 1:
            gather(unit)
        rounded = gathered[unit, 1, mine, own, :]
        hidden[unit + 1] = (
            hidden[unit] + dot(rounded, narrow[unit], 1, 1) + row_of(narrow_bias, unit)
        )

    lane_tiles = channels // 128
    stretch = rows_all + 16
    alpha = row_of(snake_alpha, 6)
    inverse = 1.0 / alpha

    def last_snake(place, carry, edge):
        values = snake_of(hidden[3, block_rows(place), :], alpha, inverse)
        low = (values * valid_rows(place)).astype(bf16)
        keep_edge(3, edge, low)
        wider = low.astype(f32)
        for tile in range(lane_tiles):
            at = pl.multiple_of(tile * stretch + 8 + place * ROWS, 8)
            mixed_pad[pl.ds(at, ROWS), :] = wider[:, tile * 128 : (tile + 1) * 128]
        return carry

    _, made = each_block(last_snake, 0, lambda: start_halo(3))
    made.wait_recv()
    begin = halo_start[3]
    rim = halo_in[begin : begin + 16, :].astype(f32)
    before, after = rim[8:] * last, rim[:8] * first
    for tile in range(lane_tiles):
        base = tile * stretch
        lanes = slice(tile * 128, (tile + 1) * 128)
        mixed_pad[base : base + 8, :] = before[:, lanes]
        mixed_pad[base + 8 + rows_all : base + 16 + rows_all, :] = after[:, lanes]
    for tap in range(taps):
        for tile in range(lane_tiles):
            base = tile * stretch + tap + 4
            frames[tap, :, tile * 128 : (tile + 1) * 128] = mixed_pad[
                pl.ds(base, frames_all, stride=STRIDE), :
            ].astype(bf16)
    local_copies = []

    def local(source, target, number):
        copy = pltpu.make_async_copy(source, target, local_sems.at[number])
        copy.start()
        local_copies.append(copy)

    own_phases = frames.at[pl.ds(taps // 2 - STRIDE // 2, STRIDE)]
    local(own_phases, all_phases.at[batch, time], 0)
    pair_blocks = {
        0: remote(
            own_phases,
            all_phases.at[batch, time],
            block_send.at[members],
            block_recv.at[members],
            (pair, time),
        )
    }
    near_first = sorted(range(1, members), key=lambda step: min(step, members - step))
    z_blocks = {
        step: remote(
            own_phases,
            all_phases.at[batch, time],
            block_send.at[step],
            block_recv.at[step],
            (member(step), time),
        )
        for step in near_first
    }

    result = None
    for tap in range(taps):
        term = dot(frames[tap], down_tap(tap), 1, 1)
        result = term if result is None else result + term
    latent[...] = result + down_bias[...]

    gap = exact(latent[...], in_weight[...], 1, 1) - correction[...] - looked_rows
    grouping = jnp.where(
        lax.broadcasted_iota(jnp.int32, (count, phases), 0) // dims
        == lax.broadcasted_iota(jnp.int32, (count, phases), 1),
        1.0,
        0.0,
    )
    squares = exact(gap * gap, grouping, 1, 0) * frame_valid
    commit_out[...] = jnp.concatenate(
        [squares, jnp.zeros((frames_all, 128 - phases), f32)], axis=1
    ).reshape(commit_out.shape)
    swap_commit = swap(3, lambda part: commit_out.at[part], lambda slot: commit.at[slot], mine, True)
    commit_cot = codes[:, phases : 2 * phases]
    gap_back = 2.0 * (exact(commit_cot * frame_valid, grouping, 1, 1) * gap)
    gap_grad[...] = gap_back
    lowered = exact(gap_back, in_weight[...], 1, 0).astype(bf16)
    latent_low[...] = lowered
    for index in range(time_count):
        low_shares[index] = lowered[:, index * wide_of : (index + 1) * wide_of]

    edge_frames = pl.ds(pl.multiple_of((1 - side) * (frames_all - 16), 16), 16)
    made = remote(
        latent_low.at[edge_frames], latent_in, send_sems.at[4], recv_sems.at[4], (batch, core)
    )

    low_all[time] = low_shares[time]
    lows_in = [
        remote(
            low_shares.at[sibling(step)],
            low_all.at[time],
            low_send.at[step - 1],
            low_recv.at[step - 1],
            (batch, sibling(step)),
        )
        for step in range(1, time_count)
    ]

    across_blocks, low_blocks, core_blocks = [], [], []

    def block_of(step, half):
        return 2 * lax.rem(place_z - step + members, members) + half

    def forward_pair(step):
        z_blocks[step].wait_recv()
        slot = all_phases.at[block_of(step, half), time]
        sems = members + step
        pair_blocks[step] = remote(
            slot, slot, block_send.at[sems], block_recv.at[sems], (pair, time)
        )

    def forward_across(step):
        pair_blocks[step].wait_recv()
        for order, which in enumerate((half, 1 - half)):
            slot = all_phases.at[block_of(step, which), time]
            sems = 2 * members + 2 * step + order
            if step == 0 and order == 0:
                local_copies.pop(0).wait()
            across_blocks.append(
                remote(slot, slot, block_send.at[sems], block_recv.at[sems], (batch, across))
            )

    def forward_core(which):
        sems = 4 * members + which
        if which == 0:
            slot = all_phases.at[:, time]
        else:
            for copy in across_blocks:
                copy.wait_recv()
            slot = all_phases.at[:, across]
        core_blocks.append(
            remote(slot, slot, block_send.at[sems], block_recv.at[sems], (batch, core))
        )

    lowered = latent_low[...].astype(f32)

    def keep_alpha(row, rows):
        for index in range(time_count):
            alpha_out[index, row : row + 1, :] = rows[:, index * share : (index + 1) * share]

    def quantizer_gradient():
        swapped_in(swap_quant)
        push = quant_in[...].reshape(frames_all, latents) * frame_valid
        gap_back = gap_grad[...]
        looked_rows = looked[...]
        between = exact(looked_rows, gap_back, 0, 0)
        small[...] = jnp.zeros_like(small)

        def keep_small(row, rows):
            for index in range(time_count):
                columns = rows[:, index * wide_of : (index + 1) * wide_of]
                done = 0
                while done < rows.shape[0]:
                    fold, at = divmod(row + done, 128)
                    size = min(rows.shape[0] - done, 128 - at)
                    small[index, at : at + size, fold * wide_of : (fold + 1) * wide_of] = columns[
                        done : done + size
                    ]
                    done += size

        earlier_rows = jnp.where(
            lax.broadcasted_iota(jnp.int32, (count, phases), 0) // dims
            > lax.broadcasted_iota(jnp.int32, (count, phases), 1),
            1.0,
            0.0,
        )
        ones = jnp.ones((frames_all, phases), f32)
        keep_small(
            0,
            exact(gap_back, latent[...], 0, 0)
            - exact(exact(gap_back, looked_rows, 0, 0) * later, out_weight[...], 1, 0)
            - exact(exact(gap_back, ones, 0, 0) * earlier_rows, out_bias[...], 1, 0),
        )
        looked_back = exact(push, out_weight[...], 1, 1) - gap_back
        crossing = exact(out_weight[...], in_weight[...], 1, 1) * earlier
        looked_back = (looked_back - exact(gap_back, crossing, 1, 1)).T
        for phase in range(phases):
            rows = looked_back[phase * dims : (phase + 1) * dims, :]
            three = jnp.concatenate([part.astype(f32) for part in split_three(rows)], axis=0)
            found = dot(three.astype(bf16), onehot(codes, phase), 1, 0)
            keep_small(
                count + phase * dims, found[:dims] + found[dims : 2 * dims] + found[2 * dims :]
            )
        keep_small(
            2 * count,
            exact(looked_rows, push, 0, 0) - exact(between * earlier, in_weight[...], 1, 0),
        )
        gap_sum = jnp.sum(gap_back, axis=0, keepdims=True)
        keep_small(
            3 * count,
            jnp.sum(push, axis=0, keepdims=True)
            - exact(jnp.where(nine_rows < nine_columns, gap_sum, 0.0), in_weight[...], 1, 0),
        )
        row = 3 * count + phases
        keep_small(row, jnp.sum(lowered, axis=0, keepdims=True))
        fold, at = divmod(row + 1, 128)
        for index in range(time_count):
            small[index, at : at + 1, fold * wide_of : fold * wide_of + count] = gap_sum
        small_low[...] = small[...].astype(bf16)
        smalls_in = [
            remote(
                small_low.at[sibling(step)],
                small_in.at[step - 1],
                small_send.at[step - 1],
                small_recv.at[step - 1],
                (batch, sibling(step)),
            )
            for step in range(1, time_count)
        ]
        return smalls_in

    forward_pair(near_first[0])

    made.wait_recv()
    latent_pad[...] = jnp.zeros_like(latent_pad)
    latent_pad[8 : 8 + frames_all, :] = lowered
    neighbour = latent_in[...].astype(f32)
    latent_pad[7:8, :] = neighbour[15:, :] * last
    latent_pad[8 + frames_all : 9 + frames_all, :] = neighbour[:1, :] * first
    reach = frames_all + 8
    same = latent_pad[8 : 8 + reach, :].astype(bf16)
    previous = latent_pad[7 : 7 + reach, :].astype(bf16)
    run = reach * STRIDE
    for step in range(STRIDE):
        both = dot(same, down_tap(step), 1, 0) + dot(previous, down_tap(step + STRIDE), 1, 0)
        for tile in range(lane_tiles):
            spread[pl.ds(tile * run + step, reach, stride=STRIDE), :] = both[
                :, tile * 128 : (tile + 1) * 128
            ]

    alpha = row_of(snake_alpha, 6)
    inverse = 1.0 / alpha
    zero = jnp.zeros((8, channels), f32)

    def mixed_back(place, carry, edge):
        tiles = []
        for tile in range(lane_tiles):
            at = tile * run + STRIDE // 2 + place * ROWS
            tiles.append(spread[pl.ds(at, ROWS), :])
        upstream = jnp.concatenate(tiles, axis=1) * valid_rows(place)
        at = block_rows(place)
        slope, alpha_slope = snake_slopes(hidden[3, at, :], alpha, inverse)
        following = upstream * slope
        grad[at, :] = following
        keep_branch(2, place, following.astype(bf16))
        return carry + folded(upstream * alpha_slope)

    def keep_branch(unit, place, rows):
        branch[block_rows(place), :] = rows
        for index in range(time_count):
            shares[unit, index, 1, block_rows(place), :] = rows[
                :, index * share : (index + 1) * share
            ]

    alpha_sum, _ = each_block(mixed_back, zero)
    alpha_out[...] = jnp.zeros_like(alpha_out)
    keep_alpha(6, jnp.sum(alpha_sum, axis=0, keepdims=True))

    total = down.at[pl.ds(0, pieces[-1][0] + pieces[-1][1])]

    chunk_of = {start: rows // batch_count for start, rows in pieces}
    spread_z = members - 1
    copies = {}

    def add_into(target, start, sources, rows):
        def step(index, carry):
            at = index * 16
            block = target[pl.ds(pl.multiple_of(start + at, 16), 16), :].astype(f32)
            for ref, begin in sources:
                block += ref[pl.ds(pl.multiple_of(begin + at, 16), 16), :].astype(f32)
            target[pl.ds(pl.multiple_of(start + at, 16), 16), :] = block.astype(bf16)
            return carry

        lax.fori_loop(0, rows // 16, step, 0, unroll=min(4, rows // 16))

    def send_pair(number):
        start, rows = pieces[number]
        other = pl.ds(pl.multiple_of(start + (1 - half) * (rows // 2), 16), rows // 2)
        copies[number, 0] = remote(
            total.at[other],
            from_pair.at[pl.ds(start // 2, rows // 2)],
            piece_send.at[number, 0],
            piece_recv.at[number, 0],
            (pair, time),
        )

    def send_members(number):
        start, rows = pieces[number]
        copies[number, 0].wait_recv()
        mine = pl.multiple_of(start + half * (rows // 2), 16)
        add_into(total, mine, [(from_pair, start // 2)], rows // 2)
        chunk = rows // batch_count
        for step in range(1, members):
            at = mine + lax.rem(place_z + step, members) * chunk
            copies[number, step] = remote(
                total.at[pl.ds(pl.multiple_of(at, 16), chunk)],
                from_members.at[step - 1, pl.ds(start // batch_count, chunk)],
                piece_send.at[number, step],
                piece_recv.at[number, step],
                (member(step), time),
            )

    def send_back(number):
        start, rows = pieces[number]
        chunk = rows // batch_count
        for step in range(1, members):
            copies[number, step].wait_recv()
        mine = pl.multiple_of(start + half * (rows // 2) + place_z * chunk, 16)
        sources = [(from_members.at[step], start // batch_count) for step in range(spread_z)]
        block = total[pl.ds(mine, chunk), :].astype(f32)
        for ref, begin in sources:
            block += ref[pl.ds(begin, chunk), :].astype(f32)
        final[pl.ds(mine, chunk), :] = block.astype(bf16)
        for step in range(1, members):
            copies[number, spread_z + step] = remote(
                final.at[pl.ds(mine, chunk)],
                final.at[pl.ds(mine, chunk)],
                piece_send.at[number, spread_z + step],
                piece_recv.at[number, spread_z + step],
                (member(step), time),
            )

    def send_last(number):
        start, rows = pieces[number]
        for step in range(1, members):
            copies[number, spread_z + step].wait_recv()
        mine = pl.ds(pl.multiple_of(start + half * (rows // 2), 16), rows // 2)
        copies[number, 1 + 2 * spread_z] = remote(
            final.at[mine],
            final.at[mine],
            piece_send.at[number, 1 + 2 * spread_z],
            piece_recv.at[number, 1 + 2 * spread_z],
            (pair, time),
        )

    def finish(number):
        copies[number, 1 + 2 * spread_z].wait_recv()

    relays = {}

    def relay(unit):
        gather_across[unit].wait_recv()
        slot = gathered.at[unit, :, crops - 1 - mine, own]
        relays[unit] = remote(
            slot, slot, relay_send.at[unit], relay_recv.at[unit], (batch, core)
        )

    unit_rows = (TAPS + 1) * share
    unit_start = {unit: pieces[0][1] + unit * unit_rows for unit in range(3)}
    numbers = {
        unit: [
            number
            for number, (start, rows) in enumerate(pieces)
            if unit_start[unit] <= start < unit_start[unit] + unit_rows
        ]
        for unit in range(3)
    }
    everywhere = crops * rows_all
    shifted_start = down.shape[0] // 2
    share_pad[...] = jnp.zeros_like(share_pad)
    shares_in = {}
    bias_rows = {}

    def unit_gradient(unit):
        dilation = DILATIONS[unit]
        for copy in shares_in[unit]:
            copy.wait_recv()
        for crop in range(crops):
            share_pad[crop, RIM : RIM + everywhere, :] = share_all[unit, 0, crop].astype(f32)
        bias_rows[unit] = [
            jnp.sum(
                folded(
                    jnp.concatenate(
                        [share_all[unit, kind, crop].astype(f32) for crop in range(crops)], axis=0
                    )
                ),
                axis=0,
                keepdims=True,
            )
            for kind in range(2)
        ]
        for tap in range(TAPS):
            start = RIM - (tap - 3) * dilation
            for crop in range(crops):
                bank, lane = divmod(tap, time_count)
                begin = shifted_start + (bank * crops + crop) * everywhere
                down[begin : begin + everywhere, lane * share : (lane + 1) * share] = share_pad[
                    crop, start : start + everywhere, :
                ].astype(bf16)
        gather_core[unit].wait_recv()
        relays[unit].wait_recv()
        taken = gathered[unit, 0].reshape(crops * everywhere, channels)
        at = unit_start[unit]
        for bank in range(-(-TAPS // time_count)):
            begin = shifted_start + bank * crops * everywhere
            columns = min(TAPS - bank * time_count, time_count) * share
            moved = down[begin : begin + crops * everywhere, :columns]
            row = at + bank * channels
            total[row : row + columns, :] = dot(moved, taken, 0, 0).astype(bf16)
        taken = gathered[unit, 1].reshape(crops * everywhere, channels)
        narrow_share = share_all[unit, 1].reshape(crops * everywhere, share)
        total[at + TAPS * share : at + unit_rows, :] = dot(narrow_share, taken, 0, 0).astype(bf16)
        for number in numbers[unit]:
            send_pair(number)

    def small_gradient(smalls_in):
        for copy in smalls_in:
            copy.wait_recv()
        block = small[time]
        for step in range(time_count - 1):
            block += small_in[step].astype(f32)
        small[0] = block

    def lows_members():
        for copy in lows_in:
            copy.wait_recv()
        local(low_all, all_lows.at[batch], 1)
        for step in range(1, members):
            low_blocks.append(
                remote(
                    low_all,
                    all_lows.at[batch],
                    low_send.at[2 + step],
                    low_recv.at[2 + step],
                    (member(step), time),
                )
            )
        low_blocks.append(
            remote(
                low_all,
                all_lows.at[batch],
                low_send.at[2 + members],
                low_recv.at[2 + members],
                (pair, time),
            )
        )

    def lows_pair():
        for step in range(1, members):
            low_blocks[step - 1].wait_recv()
            slot = all_lows.at[block_of(step, half)]
            sems = 2 + members + step
            low_blocks.append(
                remote(slot, slot, low_send.at[sems], low_recv.at[sems], (pair, time))
            )

    def between_units(unit):
        if unit == 2:
            lows_members()
            for step in near_first[2:]:
                forward_pair(step)
        else:
            relay(unit + 1)
            if unit == 1:
                lows_pair()
            unit_gradient(unit + 1)

    def finish_all():
        order = numbers[2] + numbers[1] + numbers[0] + [0]
        stages = [send_members, send_back, send_last]
        for wave in range(len(order) + len(stages)):
            for depth, stage in enumerate(stages):
                if 0 <= wave - depth < len(order):
                    stage(order[wave - depth])
            if wave < members:
                forward_across(([0] + near_first)[wave])
        for step in ([0] + near_first)[len(order) + len(stages) :]:
            forward_across(step)
        forward_core(0)
        forward_core(1)
        for number in order:
            finish(number)
        for copy in core_blocks:
            copy.wait_recv()
        for copy in low_blocks[members - 1 :]:
            copy.wait_recv()

    for step in near_first[1:2]:
        forward_pair(step)
    for unit in (2, 1, 0):
        dilation = DILATIONS[unit]
        number = 5 + unit
        work[...] = dot(branch[...], narrow[unit], 1, 0)
        alpha = row_of(snake_alpha, 2 * unit + 1)
        inverse = 1.0 / alpha

        def conv_back(place, carry, edge):
            at = block_rows(place)
            upstream = work[at, :]
            slope, alpha_slope = snake_slopes(conv[unit, at, :], alpha, inverse)
            lowered = (upstream * slope).astype(bf16)
            for index in range(time_count):
                shares[unit, index, 0, at, :] = lowered[
                    :, index * share : (index + 1) * share
                ]
            pad[pad_rows(place), :] = lowered.astype(f32)
            keep_edge(number, edge, lowered)
            return carry + folded(upstream * alpha_slope)

        alpha_sum, made = each_block(conv_back, zero, lambda: start_halo(number))
        shares_in[unit] = [
            remote(
                shares.at[unit, sibling(step)],
                share_all.at[unit, :, mine, own],
                share_send.at[unit, step - 1],
                share_recv.at[unit, step - 1],
                (batch, sibling(step)),
            )
            for step in range(1, time_count)
        ]
        if unit == 2:
            gather(1)
        for kind in range(2):
            share_all[unit, kind, mine, own, :] = shares[unit, time, kind]
        keep_alpha(2 * unit + 1, jnp.sum(alpha_sum, axis=0, keepdims=True))
        between_units(unit)
        fill_rims(made, number)
        result = None
        for tap in range(TAPS):
            term = dot(shifted(-(tap - 3) * dilation), wide[unit, tap], 1, 0)
            result = term if result is None else result + term
        work[...] = result
        alpha = row_of(snake_alpha, 2 * unit)
        inverse = 1.0 / alpha

        def hidden_back(place, carry, edge):
            at = block_rows(place)
            upstream = work[at, :]
            slope, alpha_slope = snake_slopes(hidden[unit, at, :], alpha, inverse)
            following = grad[at, :] + upstream * slope
            if unit > 0:
                grad[at, :] = following
                keep_branch(unit - 1, place, following.astype(bf16))
            else:
                signal_out[at, :] = following * valid_rows(place)
            return carry + folded(upstream * alpha_slope)

        alpha_sum, _ = each_block(hidden_back, zero)
        keep_alpha(2 * unit, jnp.sum(alpha_sum, axis=0, keepdims=True))

    alphas_in = [
        remote(
            alpha_out.at[sibling(step)],
            alpha_in.at[step - 1],
            small_send.at[time_count - 1 + step - 1],
            small_recv.at[time_count - 1 + step - 1],
            (batch, sibling(step)),
        )
        for step in range(1, time_count)
    ]
    relay(0)
    unit_gradient(0)
    swap_back = swap(
        4,
        lambda part: signal_out.at[pl.ds(part * length, length)],
        lambda slot: signal_back.at[slot],
        mine,
        True,
    )
    small_gradient(quantizer_gradient())
    for copy in alphas_in:
        copy.wait_recv()
    alpha_rows = alpha_out[time]
    for step in range(time_count - 1):
        alpha_rows += alpha_in[step]
    rest = [alpha_rows] + [bias_rows[unit][kind] for kind in range(2) for unit in range(3)]
    rest = jnp.concatenate(rest + [jnp.zeros((2, share), f32)], axis=0)
    small[0, small.shape[1] - 16 :, channels - share :] = rest
    for start in range(0, pieces[0][1], small.shape[1]):
        total[start : start + small.shape[1], :] = small[0].astype(bf16)
    send_pair(0)

    finish_all()
    swapped_in(swap_back)
    swapped_in(swap_commit)
    for crop in range(crops):
        signal_grad[crop] = signal_back[crop].T
    for made in swaps:
        for peer, origin, away, here, arrived in made:

            @pl.when(peer != time)
            def _():
                away.wait_send()

    for copy in local_copies:
        copy.wait()
    for copy in sent:
        copy.wait_send()


def run_block(time_count, batch_count, pieces, lengths, *arrays):
    (signal, quant_cot, coded, wide, _, narrow, _, _, down, down_bias, in_weight) = arrays[:11]
    f32, bf16 = jnp.float32, jnp.bfloat16
    crops, channels, length = signal.shape
    latents = down_bias.shape[1]
    taps = down.shape[0] // latents
    frames = crops * (length // STRIDE)
    rows = crops * length
    count = in_weight.shape[0]
    share = channels // time_count
    wide_of = latents // time_count
    members = batch_count // 2
    everywhere = crops * rows
    total_rows = pieces[-1][0] + pieces[-1][1]
    vmem = pl.BlockSpec(memory_space=pltpu.VMEM)
    hbm = pl.BlockSpec(memory_space=pl.ANY)
    in_specs = [pl.BlockSpec(memory_space=pltpu.SMEM)] + [vmem] * len(arrays)
    for place in (3, 5, 8):
        in_specs[1 + place] = hbm
    lane_tiles = channels // 128
    dma = pltpu.SemaphoreType.DMA
    slots = 2 * members
    return pl.pallas_call(
        functools.partial(block_kernel, time_count, batch_count, pieces),
        out_shape=(
            jax.ShapeDtypeStruct(quant_cot.shape, f32),
            jax.ShapeDtypeStruct(coded.shape, f32),
            jax.ShapeDtypeStruct(signal.shape, f32),
            jax.ShapeDtypeStruct((total_rows, channels), bf16),
            jax.ShapeDtypeStruct((batch_count, time_count, STRIDE, frames, channels), bf16),
            jax.ShapeDtypeStruct((batch_count, time_count, frames, wide_of), bf16),
        ),
        in_specs=in_specs,
        out_specs=(vmem, vmem, vmem, vmem, hbm, hbm),
        scratch_shapes=[
            pltpu.VMEM(wide.shape, bf16),
            pltpu.VMEM(narrow.shape, bf16),
            pltpu.VMEM((taps * latents, channels), bf16),
            pltpu.VMEM((4, rows, channels), f32),
            pltpu.VMEM((3, rows, channels), f32),
            pltpu.VMEM((3, 2, crops, everywhere, channels), bf16),
            pltpu.VMEM((rows + 2 * RIM, channels), f32),
            pltpu.VMEM((rows, channels), f32),
            pltpu.VMEM((rows, channels), f32),
            pltpu.VMEM((rows, channels), bf16),
            pltpu.VMEM((3, time_count, 2, rows, share), bf16),
            pltpu.VMEM((3, 2, crops, everywhere, share), bf16),
            pltpu.VMEM((crops, everywhere + 2 * RIM, share), f32),
            pltpu.VMEM((lane_tiles * (rows + 16), 128), f32),
            pltpu.VMEM((taps, frames, channels), bf16),
            pltpu.VMEM((frames, latents), f32),
            pltpu.VMEM((frames + 16, latents), f32),
            pltpu.VMEM((lane_tiles * (rows + 8 * STRIDE), 128), f32),
            pltpu.VMEM((frames, count), f32),
            pltpu.VMEM((frames, count), f32),
            pltpu.VMEM((frames, count), f32),
            pltpu.VMEM((time_count, 128, channels), f32),
            pltpu.VMEM((time_count, 128, channels), bf16),
            pltpu.VMEM((time_count - 1, 128, channels), bf16),
            pltpu.VMEM((time_count, 8, share), f32),
            pltpu.VMEM((time_count - 1, 8, share), f32),
            pltpu.VMEM((time_count, frames, wide_of), bf16),
            pltpu.VMEM((time_count, frames, wide_of), bf16),
            pltpu.VMEM((144, channels), bf16),
            pltpu.VMEM((144, channels), bf16),
            pltpu.VMEM((frames, latents), bf16),
            pltpu.VMEM((16, latents), bf16),
            pltpu.VMEM(signal.shape, f32),
            pltpu.VMEM(quant_cot.shape, f32),
            pltpu.VMEM(coded.shape, f32),
            pltpu.VMEM(coded.shape, f32),
            pltpu.VMEM((rows, channels), f32),
            pltpu.VMEM((crops, length, channels), f32),
            dma((5,)),
            dma((5, 2)),
            dma((5, 2)),
            pltpu.VMEM((total_rows // 2, channels), bf16),
            pltpu.VMEM((members - 1, total_rows // batch_count, channels), bf16),
            dma((8,)),
            dma((2,)),
            dma((8,)),
            dma((8,)),
            dma((3, 2)),
            dma((3, 2)),
            dma((3,)),
            dma((3,)),
            dma((3, time_count - 1)),
            dma((3, time_count - 1)),
            dma((2 * (time_count - 1),)),
            dma((2 * (time_count - 1),)),
            dma((2 + 2 * members,)),
            dma((2 + 2 * members,)),
            dma((4 * members + 2,)),
            dma((4 * members + 2,)),
            dma((len(pieces), slots)),
            dma((len(pieces), slots)),
        ],
        compiler_params=pltpu.CompilerParams(
            collective_id=1, has_side_effects=True, vmem_limit_bytes=62 * 2**20
        ),
    )(lengths, *arrays)


def down_kernel(lows, phases, out, held, columns, in_sems, out_sems):
    count = lows.shape[2]
    group, lanes = held.shape[1], held.shape[4]
    rows = group * held.shape[3]
    tiles = lanes // 128
    groups = phases.shape[0] // group
    items = [(part, at) for part in range(phases.shape[3] // lanes) for at in range(groups)]
    loads = [
        pltpu.make_async_copy(
            phases.at[pl.ds(at * group, group), :, :, pl.ds(part * lanes, lanes)],
            held.at[index % 2],
            in_sems.at[index % 2],
        )
        for index, (part, at) in enumerate(items)
    ]
    for load in loads[:2]:
        load.start()
    stores = []
    after = before = None
    for index, (part, at) in enumerate(items):
        if after is None or groups > 1:
            turned = [lows[kind, at * rows : (at + 1) * rows].T for kind in range(3)]
            after = jnp.concatenate([turned[0], turned[1]], axis=0)
            before = jnp.concatenate([turned[0], turned[2]], axis=0)
        loads[index].wait()
        for step in range(STRIDE):
            block = held[index % 2, :, step].reshape(rows, lanes)
            late = step >= STRIDE // 2
            both = dot(after if late else before, block, 1, 0)
            middle = step + STRIDE // 2
            for tap, row in ((middle, 0), (middle - STRIDE if late else middle + STRIDE, count)):
                for tile in range(tiles):
                    place = pl.ds(tap, count, stride=2 * STRIDE)
                    value = both[row : row + count, tile * 128 : (tile + 1) * 128]
                    if at > 0:
                        value = value + columns[part * tiles + tile, place, :]
                    columns[part * tiles + tile, place, :] = value
        if index + 2 < len(items):
            loads[index + 2].start()
        if at == groups - 1:
            for tile in range(part * tiles, (part + 1) * tiles):
                stores.append(
                    pltpu.make_async_copy(
                        columns.at[tile], out.at[:, pl.ds(tile * 128, 128)], out_sems.at[tile]
                    )
                )
                stores[-1].start()
    for store in stores:
        store.wait()


def down_gradient(lows, phases):
    devices, _, rows, channels = phases.shape
    count = lows.shape[2]
    lanes = 256
    hbm = pl.BlockSpec(memory_space=pl.ANY)
    return pl.pallas_call(
        down_kernel,
        out_shape=jax.ShapeDtypeStruct((count * 2 * STRIDE, channels), jnp.float32),
        in_specs=[pl.BlockSpec(memory_space=pltpu.VMEM), hbm],
        out_specs=hbm,
        scratch_shapes=[
            pltpu.VMEM((2, min(devices, 32), STRIDE, rows, lanes), phases.dtype),
            pltpu.VMEM((channels // 128, count * 2 * STRIDE, 128), jnp.float32),
            pltpu.SemaphoreType.DMA((2,)),
            pltpu.SemaphoreType.DMA((channels // 128,)),
        ],
        compiler_params=pltpu.CompilerParams(vmem_limit_bytes=60 * 2**20),
    )(lows, phases)


def body(
    signal,
    quant_cot,
    commit_cot,
    lengths,
    codes,
    wide_weight,
    wide_bias,
    narrow_weight,
    narrow_bias,
    snake_alpha,
    down_weight,
    down_bias,
    in_weight,
    in_bias,
    codebook,
    out_weight,
    out_bias,
):
    time_count = lax.axis_size("tm")
    batch_count = lax.axis_size("batch")
    crop_count, channel_count, length = signal.shape
    latent_count, tap_count, _ = down_weight.shape
    phases, dims = in_weight.shape[:2]
    count = phases * dims
    frame_count = length // STRIDE
    small_rows = 16 * batch_count
    unit_rows = (TAPS + 1) * (channel_count // time_count)
    piece = max(unit_rows // 2, small_rows)
    pieces = [(0, small_rows)]
    pieces += [(at, piece) for at in range(small_rows, small_rows + 3 * unit_rows, piece)]
    coded = [jnp.swapaxes(codes, 1, 2).astype(jnp.float32), jnp.swapaxes(commit_cot, 1, 2)]
    coded = jnp.pad(jnp.concatenate(coded, axis=2), ((0, 0), (0, 0), (0, 128 - 2 * phases)))
    quantized, commit, signal_grad, summed, all_phases, all_low = run_block(
        time_count,
        batch_count,
        tuple(pieces),
        lengths,
        signal,
        quant_cot,
        coded,
        jnp.swapaxes(wide_weight, 1, 2),
        wide_bias,
        narrow_weight,
        narrow_bias,
        snake_alpha,
        down_weight.reshape(-1, channel_count),
        down_bias.reshape(1, -1),
        in_weight.reshape(count, -1),
        in_bias.reshape(1, -1),
        codebook.reshape(count, -1),
        out_weight.reshape(count, -1),
        out_bias,
    )
    commit = jnp.swapaxes(commit[:, :, :phases], 1, 2)

    share = latent_count // time_count
    all_phases = all_phases.reshape((-1,) + all_phases.shape[2:])
    line = all_low.reshape(batch_count * crop_count, time_count * frame_count, share)
    after = jnp.pad(line[:, 1:], ((0, 0), (0, 1), (0, 0)))
    before = jnp.pad(line[:, :-1], ((0, 0), (1, 0), (0, 0)))
    lows = jnp.stack([line, after, before])
    lows = lows.reshape(3, -1, share)

    wide_of = latent_count // time_count
    small = summed[:128].astype(jnp.float32)
    small = jnp.concatenate([small[:, :wide_of], small[:, wide_of : 2 * wide_of]], axis=0)
    in_weight_out = small[:count].reshape(phases, dims, -1)
    codebook_out = small[count : 2 * count].reshape(phases, dims, -1)
    out_weight_out = small[2 * count : 3 * count].reshape(phases, dims, -1)
    row = 3 * count + phases
    out_bias_out = small[3 * count : row]
    down_bias_out = small[row]
    narrow_of = channel_count // time_count
    in_bias_all = small[row + 1, :count].reshape(phases, dims)
    part = dims // time_count
    in_bias_out = lax.dynamic_slice_in_dim(in_bias_all, lax.axis_index("tm") * part, part, axis=1)
    last = summed[112:128, -narrow_of:].astype(jnp.float32)
    alpha_out, wide_bias_out, narrow_bias_out = last[:7], last[8:11], last[11:14]
    units = summed[small_rows:].reshape(3, unit_rows, channel_count)
    wide_out = units[:, : TAPS * narrow_of].astype(jnp.float32)
    wide_out = wide_out.reshape(3, TAPS, narrow_of, channel_count)
    wide_out = jnp.swapaxes(wide_out, 1, 2)
    narrow_out = units[:, TAPS * narrow_of :].astype(jnp.float32)
    down_out = down_gradient(lows, all_phases).reshape(share, tap_count, channel_count)
    return (
        quantized,
        commit,
        signal_grad,
        wide_out,
        wide_bias_out,
        narrow_out,
        narrow_bias_out,
        alpha_out,
        down_out,
        down_bias_out,
        in_weight_out,
        in_bias_out,
        codebook_out,
        out_weight_out,
        out_bias_out,
    )


def solution(mesh):
    return jax.shard_map(
        body,
        mesh=mesh,
        in_specs=(
            P("batch", None, "tm"),
            P("batch", "tm", None),
            P("batch", None, "tm"),
            P("batch"),
            P("batch", None, "tm"),
            P(),
            P(),
            P(),
            P(),
            P(),
            P(),
            P(),
            P(),
            P(),
            P(),
            P(),
            P(),
        ),
        out_specs=(
            P("batch", "tm", None),
            P("batch", None, "tm"),
            P("batch", None, "tm"),
            P(None, "tm", None, None),
            P(None, "tm"),
            P(None, "tm", None),
            P(None, "tm"),
            P(None, "tm"),
            P("tm", None, None),
            P("tm"),
            P(None, None, "tm"),
            P(None, "tm"),
            P(None, None, "tm"),
            P(None, None, "tm"),
            P(None, "tm"),
        ),
        check_vma=False,
    )
```

```python
import functools

import jax
import jax.numpy as jnp
from jax import lax
from jax.experimental import pallas as pl
from jax.experimental.pallas import tpu as pltpu
from jax.sharding import PartitionSpec as P

STRIDE = 8


DILATIONS = (1, 3, 9)
MESH = pl.DeviceIdType.MESH
BLOCK = 64


TAPS = 7
RIM = 32
ROWS = 32


def dot(left, right, left_dim, right_dim, precision=None):
    return lax.dot_general(
        left,
        right,
        (((left_dim,), (right_dim,)), ((), ())),
        precision=precision,
        preferred_element_type=jnp.float32,
    )


def exact(left, right, left_dim, right_dim):
    return dot(left, right, left_dim, right_dim, lax.Precision.HIGHEST)


def reduced_angle(angle):
    turns = jnp.floor(angle * 0.3183098861837907 + 0.5)
    rest = angle - turns * 3.140625
    rest = rest - turns * 9.67502593994140625e-4
    return rest - turns * 1.509957990978376432e-7


def sine(rest, square):
    series = -1.0 / 5040.0 + square * (1.0 / 362880.0 - square * (1.0 / 39916800.0))
    return rest + rest * square * (-1.0 / 6.0 + square * (1.0 / 120.0 + square * series))


def cosine(square):
    series = 1.0 / 40320.0 + square * (-1.0 / 3628800.0 + square * (1.0 / 479001600.0))
    return 1.0 + square * (-0.5 + square * (1.0 / 24.0 + square * (-1.0 / 720.0 + square * series)))


def snake_of(values, alpha, inverse):
    rest = reduced_angle(alpha * values)
    wave = sine(rest, rest * rest)
    return values + wave * wave * inverse


def snake_slopes(values, alpha, inverse):
    rest = reduced_angle(alpha * values)
    square = rest * rest
    wave = sine(rest, square)
    double = 2.0 * wave * cosine(square)
    return 1.0 + double, (values * double - wave * wave * inverse) * inverse


def split_three(values):
    first = values.astype(jnp.bfloat16)
    rest = values - first.astype(jnp.float32)
    second = rest.astype(jnp.bfloat16)
    third = (rest - second.astype(jnp.float32)).astype(jnp.bfloat16)
    return first, second, third


def folded(values):
    return jnp.sum(values.reshape(values.shape[0] // 8, 8, values.shape[1]), axis=0)


def block_kernel(
    time_count,
    batch_count,
    pieces,
    lengths,
    signal,
    quant_cot,
    coded,
    wide_hbm,
    wide_bias,
    narrow_hbm,
    narrow_bias,
    snake_alpha,
    down_hbm,
    down_bias,
    in_weight,
    in_bias,
    codebook,
    out_weight,
    out_bias,
    quantized,
    commit,
    signal_grad,
    final,
    all_phases,
    all_lows,
    wide,
    narrow,
    down,
    hidden,
    conv,
    gathered,
    pad,
    grad,
    work,
    branch,
    shares,
    share_all,
    share_pad,
    mixed_pad,
    frames,
    latent,
    latent_pad,
    spread,
    looked,
    gap_grad,
    correction,
    small,
    small_low,
    small_in,
    alpha_out,
    alpha_in,
    low_shares,
    low_all,
    halo_out,
    halo_in,
    latent_low,
    latent_in,
    signal_in,
    quant_in,
    coded_in,
    commit_out,
    signal_out,
    signal_back,
    swap_local,
    swap_send,
    swap_recv,
    from_pair,
    weight_sems,
    local_sems,
    send_sems,
    recv_sems,
    gather_send,
    gather_recv,
    relay_send,
    relay_recv,
    share_send,
    share_recv,
    small_send,
    small_recv,
    low_send,
    low_recv,
    block_send,
    block_recv,
    piece_send,
    piece_recv,
):
    f32, bf16 = jnp.float32, jnp.bfloat16
    sent = []
    batch = lax.axis_index("batch")
    time = lax.axis_index("tm")
    crops, channels, length = signal.shape
    latents = down_bias.shape[1]
    mine = time // crops
    side = lax.rem(time, crops)
    rows_all = crops * length
    blocks = rows_all // ROWS
    frame_count = length // STRIDE
    frames_all = crops * frame_count
    phases = out_bias.shape[0]
    dims = in_weight.shape[0] // phases
    count = phases * dims
    share = channels // time_count
    wide_of = latents // time_count

    core = crops * mine + 1 - side
    across = lax.rem(time + crops, time_count)
    members = batch_count // 2
    half = lax.rem(batch, 2)
    place_z = batch // 2
    pair = 2 * place_z + 1 - half

    def member(step):
        return 2 * lax.rem(place_z + step, members) + half

    def sibling(step):
        return lax.rem(time + step, time_count)

    peers = [(batch, sibling(step)) for step in range(1, time_count)]
    peers += [(pair, time)] + [(member(step), time) for step in range(1, members)]
    barrier = pltpu.get_barrier_semaphore()
    for peer in peers:
        pl.semaphore_signal(barrier, inc=1, device_id=peer, device_id_type=MESH)

    def remote(source, target, send_sem, recv_sem, device):
        copy = pltpu.make_async_remote_copy(
            src_ref=source,
            dst_ref=target,
            send_sem=send_sem,
            recv_sem=recv_sem,
            device_id=device,
            device_id_type=MESH,
        )
        copy.start()
        sent.append(copy)
        return copy

    wide_copies = [
        pltpu.make_async_copy(wide_hbm.at[unit], wide.at[unit], weight_sems.at[unit])
        for unit in range(3)
    ]
    narrow_copy = pltpu.make_async_copy(narrow_hbm, narrow, weight_sems.at[3])
    taps = frames.shape[0]
    group = 16 * taps
    quarter = down.shape[0] // 4
    down_copies = [
        pltpu.make_async_copy(
            down_hbm.at[pl.ds(part * quarter, quarter)],
            down.at[pl.ds(part * quarter, quarter)],
            weight_sems.at[4 + part],
        )
        for part in range(4)
    ]
    first, last = jnp.where(side == 0, 1.0, 0.0), jnp.where(side == 1, 1.0, 0.0)

    def swap(number, source, target, slot, back):
        made = []
        for part in range(crops):
            peer = crops * side + part if back else crops * part + mine
            origin = crops * part + mine if back else crops * side + part
            away = pltpu.make_async_remote_copy(
                src_ref=source(part),
                dst_ref=target(slot),
                send_sem=swap_send.at[number, part],
                recv_sem=swap_recv.at[number, slot],
                device_id=(batch, peer),
                device_id_type=MESH,
            )
            here = pltpu.make_async_copy(source(part), target(slot), swap_local.at[number])
            arrived = pltpu.make_async_remote_copy(
                src_ref=source(part),
                dst_ref=target(part),
                send_sem=swap_send.at[number, part],
                recv_sem=swap_recv.at[number, part],
                device_id=(batch, peer),
                device_id_type=MESH,
            )

            @pl.when(peer != time)
            def _():
                away.start()

            @pl.when(peer == time)
            def _():
                here.start()

            made.append((peer, origin, away, here, arrived))
        swaps.append(made)
        return made

    def swapped_in(made):
        for peer, origin, away, here, arrived in made:

            @pl.when(origin != time)
            def _():
                arrived.wait_recv()

            @pl.when(origin == time)
            def _():
                here.wait()

    swaps = []

    halo_rows = (16, 16, 32, 16, 0, 16, 16, 32)
    halo_start = [sum(halo_rows[:number]) for number in range(len(halo_rows))]

    def start_halo(number):
        rows = pl.ds(halo_start[number], halo_rows[number])
        return remote(
            halo_out.at[rows],
            halo_in.at[rows],
            send_sems.at[number],
            recv_sems.at[number],
            (batch, core),
        )

    def fill_rims(made, number):
        width, begin = halo_rows[number], halo_start[number]
        made.wait_recv()
        rim = halo_in[begin : begin + width, :].astype(f32)
        pad[RIM - width : RIM, :] = rim * last
        pad[RIM + rows_all : RIM + rows_all + width, :] = rim * first

    def each_block(step, carry, edge_then=None):
        carry = step((1 - side) * (blocks - 1), carry, True)
        made = edge_then() if edge_then is not None else None

        def inside(index, carry):
            return step(index + side, carry, False)

        return lax.fori_loop(0, blocks - 1, inside, carry), made

    def keep_edge(number, edge, rows):
        if edge:
            width, begin = halo_rows[number], halo_start[number]
            ahead, behind = rows[ROWS - width :].astype(f32), rows[:width].astype(f32)
            halo_out[begin : begin + width, :] = (ahead * first + behind * last).astype(bf16)

    def row_of(ref, row):
        return ref[row : row + 1, :]

    def valid_rows(place):
        places = side * rows_all + place * ROWS + lax.broadcasted_iota(jnp.int32, (ROWS, 1), 0)
        return jnp.where(places < lengths[mine], 1.0, 0.0)

    def reorder(part):
        rows = lax.broadcasted_iota(jnp.int32, (group, group), 0)
        columns = lax.broadcasted_iota(jnp.int32, (group, group), 1)
        turn = jnp.where(columns == lax.rem(rows, 16) * taps + rows // 16, 1.0, 0.0).astype(bf16)
        down_copies[part].wait()

        def step(index, carry):
            places = [
                pl.ds(pl.multiple_of(part * quarter + (4 * index + which) * group, group), group)
                for which in range(4)
            ]
            turned = [dot(turn, down[at, :], 1, 0).astype(bf16) for at in places]
            for at, rows in zip(places, turned):
                down[at, :] = rows
            return carry

        lax.fori_loop(0, quarter // group // 4, step, 0)

    def down_tap(tap):
        tiles = down.reshape(latents // 16, taps, 16, channels)
        return tiles[:, tap].reshape(latents, channels)

    pl.semaphore_wait(barrier, len(peers))
    swap_coded = swap(2, lambda part: coded.at[part], lambda slot: coded_in.at[slot], side, False)
    swap_signal = swap(0, lambda part: signal.at[part], lambda slot: signal_in.at[slot], side, False)
    swap_quant = swap(1, lambda part: quant_cot.at[part], lambda slot: quant_in.at[slot], side, False)
    wide_copies[0].start()
    narrow_copy.start()
    for copy in down_copies:
        copy.start()
    wide_copies[1].start()
    wide_copies[2].start()

    code_lanes = lax.broadcasted_iota(jnp.int32, (frames_all, codebook.shape[1]), 1).astype(f32)
    frame_rows = lax.broadcasted_iota(jnp.int32, (frames_all, 1), 0)

    def onehot(codes, phase):
        return jnp.where(codes[:, phase : phase + 1] == code_lanes, 1.0, 0.0).astype(bf16)

    def look_up(codes):
        found = []
        for phase in range(phases):
            rows = codebook[phase * dims : (phase + 1) * dims, :]
            three = jnp.concatenate([part.astype(f32) for part in split_three(rows)], axis=0)
            all_three = dot(three.astype(bf16), onehot(codes, phase), 1, 1)
            found.append(all_three[:dims] + all_three[dims : 2 * dims] + all_three[2 * dims :])
        return jnp.concatenate(found, axis=0).T

    looked_rows = look_up(coded[...].reshape(frames_all, -1))
    frame_place = time * frame_count + lax.rem(frame_rows, frame_count)
    frame_length = jnp.where(frame_rows < frame_count, lengths[0], lengths[crops - 1])
    frame_valid = jnp.where(STRIDE * frame_place < frame_length, 1.0, 0.0)
    quantized[...] = (
        (exact(looked_rows, out_weight[...], 1, 0) + jnp.sum(out_bias[...], axis=0, keepdims=True))
        * frame_valid
    ).reshape(quantized.shape)
    for part in range(4):
        reorder(part)

    swapped_in(swap_signal)
    for part in range(crops):
        places = side * rows_all + part * length + lax.broadcasted_iota(jnp.int32, (length, 1), 0)
        keep = jnp.where(places < lengths[mine], 1.0, 0.0)
        hidden[0, part * length : (part + 1) * length, :] = signal_in[part].T * keep

    def block_rows(place):
        return pl.ds(pl.multiple_of(place * ROWS, ROWS), ROWS)

    def own_rows(place):
        return pl.ds(pl.multiple_of(side * rows_all + place * ROWS, ROWS), ROWS)

    own = pl.ds(pl.multiple_of(side * rows_all, rows_all), rows_all)

    def pad_rows(place):
        return pl.ds(pl.multiple_of(RIM + place * ROWS, ROWS), ROWS)

    def shifted(offset):
        start = RIM + offset
        return pad[start : start + rows_all, :].astype(bf16)

    gather_across, gather_core = {}, {}

    def gather(unit):
        slot = gathered.at[unit, :, mine, own]
        gather_across[unit] = remote(
            slot, slot, gather_send.at[unit, 0], gather_recv.at[unit, 0], (batch, across)
        )
        gather_core[unit] = remote(
            slot, slot, gather_send.at[unit, 1], gather_recv.at[unit, 1], (batch, core)
        )

    for unit in range(3):
        dilation = DILATIONS[unit]
        alpha = row_of(snake_alpha, 2 * unit)
        inverse = 1.0 / alpha

        def first_snake(place, carry, edge):
            low = snake_of(hidden[unit, block_rows(place), :], alpha, inverse).astype(bf16)
            gathered[unit, 0, mine, own_rows(place), :] = low
            pad[pad_rows(place), :] = low.astype(f32)
            keep_edge(unit, edge, low)
            return carry

        _, made = each_block(first_snake, 0, lambda: start_halo(unit))
        fill_rims(made, unit)
        wide_copies[unit].wait()
        result = None
        for tap in range(TAPS):
            term = dot(shifted((tap - 3) * dilation), wide[unit, tap], 1, 1)
            result = term if result is None else result + term
        conv[unit] = result + row_of(wide_bias, unit)
        alpha = row_of(snake_alpha, 2 * unit + 1)
        inverse = 1.0 / alpha

        def second_snake(place, carry, edge):
            values = snake_of(conv[unit, block_rows(place), :], alpha, inverse)
            gathered[unit, 1, mine, own_rows(place), :] = values.astype(bf16)
            return carry

        each_block(second_snake, 0)
        if unit == 0:
            narrow_copy.wait()
        if unit != 1:
            gather(unit)
        rounded = gathered[unit, 1, mine, own, :]
        hidden[unit + 1] = (
            hidden[unit] + dot(rounded, narrow[unit], 1, 1) + row_of(narrow_bias, unit)
        )

    lane_tiles = channels // 128
    stretch = rows_all + 16
    alpha = row_of(snake_alpha, 6)
    inverse = 1.0 / alpha

    def last_snake(place, carry, edge):
        values = snake_of(hidden[3, block_rows(place), :], alpha, inverse)
        low = (values * valid_rows(place)).astype(bf16)
        keep_edge(3, edge, low)
        wider = low.astype(f32)
        for tile in range(lane_tiles):
            at = pl.multiple_of(tile * stretch + 8 + place * ROWS, 8)
            mixed_pad[pl.ds(at, ROWS), :] = wider[:, tile * 128 : (tile + 1) * 128]
        return carry

    _, made = each_block(last_snake, 0, lambda: start_halo(3))
    swapped_in(swap_coded)
    codes = coded_in[...].reshape(frames_all, -1)
    looked[...] = look_up(codes)
    looked_rows = looked[...]
    frame_place = side * frames_all + frame_rows
    frame_valid = jnp.where(STRIDE * frame_place < lengths[mine], 1.0, 0.0)
    phase_of_row = lax.broadcasted_iota(jnp.int32, (count, count), 0) // dims
    phase_of_column = lax.broadcasted_iota(jnp.int32, (count, count), 1) // dims
    earlier = jnp.where(phase_of_row < phase_of_column, 1.0, 0.0)
    later = jnp.where(phase_of_row > phase_of_column, 1.0, 0.0)
    crossing = exact(out_weight[...], in_weight[...], 1, 1) * earlier
    bias_terms = exact(out_bias[...], in_weight[...], 1, 1)
    nine_rows = lax.broadcasted_iota(jnp.int32, (phases, count), 0)
    nine_columns = lax.broadcasted_iota(jnp.int32, (phases, count), 1) // dims
    bias_terms = jnp.sum(jnp.where(nine_rows < nine_columns, bias_terms, 0.0), axis=0, keepdims=True)
    correction[...] = exact(looked_rows, crossing, 1, 0) + bias_terms - in_bias[...]

    made.wait_recv()
    begin = halo_start[3]
    rim = halo_in[begin : begin + 16, :].astype(f32)
    before, after = rim[8:] * last, rim[:8] * first
    for tile in range(lane_tiles):
        base = tile * stretch
        lanes = slice(tile * 128, (tile + 1) * 128)
        mixed_pad[base : base + 8, :] = before[:, lanes]
        mixed_pad[base + 8 + rows_all : base + 16 + rows_all, :] = after[:, lanes]
    for tap in range(taps):
        for tile in range(lane_tiles):
            base = tile * stretch + tap + 4
            frames[tap, :, tile * 128 : (tile + 1) * 128] = mixed_pad[
                pl.ds(base, frames_all, stride=STRIDE), :
            ].astype(bf16)
    local_copies = []

    def local(source, target, number):
        copy = pltpu.make_async_copy(source, target, local_sems.at[number])
        copy.start()
        local_copies.append(copy)

    own_phases = frames.at[pl.ds(taps // 2 - STRIDE // 2, STRIDE)]
    local(own_phases, all_phases.at[batch, time], 0)
    pair_blocks = {
        0: remote(
            own_phases,
            all_phases.at[batch, time],
            block_send.at[members],
            block_recv.at[members],
            (pair, time),
        )
    }
    near_first = sorted(range(1, members), key=lambda step: min(step, members - step))
    z_blocks = {
        step: remote(
            own_phases,
            all_phases.at[batch, time],
            block_send.at[step],
            block_recv.at[step],
            (member(step), time),
        )
        for step in near_first
    }

    result = None
    for tap in range(taps):
        term = dot(frames[tap], down_tap(tap), 1, 1)
        result = term if result is None else result + term
    latent[...] = result + down_bias[...]

    gap = exact(latent[...], in_weight[...], 1, 1) - correction[...] - looked_rows
    grouping = jnp.where(
        lax.broadcasted_iota(jnp.int32, (count, phases), 0) // dims
        == lax.broadcasted_iota(jnp.int32, (count, phases), 1),
        1.0,
        0.0,
    )
    squares = exact(gap * gap, grouping, 1, 0) * frame_valid
    commit_out[...] = jnp.concatenate(
        [squares, jnp.zeros((frames_all, 128 - phases), f32)], axis=1
    ).reshape(commit_out.shape)
    swap_commit = swap(3, lambda part: commit_out.at[part], lambda slot: commit.at[slot], mine, True)
    commit_cot = codes[:, phases : 2 * phases]
    gap_back = 2.0 * (exact(commit_cot * frame_valid, grouping, 1, 1) * gap)
    gap_grad[...] = gap_back
    lowered = exact(gap_back, in_weight[...], 1, 0).astype(bf16)
    latent_low[...] = lowered
    for index in range(time_count):
        low_shares[index] = lowered[:, index * wide_of : (index + 1) * wide_of]

    edge_frames = pl.ds(pl.multiple_of((1 - side) * (frames_all - 16), 16), 16)
    made = remote(
        latent_low.at[edge_frames], latent_in, send_sems.at[4], recv_sems.at[4], (batch, core)
    )

    low_all[time] = low_shares[time]
    lows_in = [
        remote(
            low_shares.at[sibling(step)],
            low_all.at[time],
            low_send.at[step - 1],
            low_recv.at[step - 1],
            (batch, sibling(step)),
        )
        for step in range(1, time_count)
    ]

    across_blocks, low_blocks, core_blocks = [], [], []

    def block_of(step, half):
        return 2 * lax.rem(place_z - step + members, members) + half

    def forward_pair(step):
        z_blocks[step].wait_recv()
        slot = all_phases.at[block_of(step, half), time]
        sems = members + step
        pair_blocks[step] = remote(
            slot, slot, block_send.at[sems], block_recv.at[sems], (pair, time)
        )

    def forward_across(step):
        pair_blocks[step].wait_recv()
        for order, which in enumerate((half, 1 - half)):
            slot = all_phases.at[block_of(step, which), time]
            sems = 2 * members + 2 * step + order
            if step == 0 and order == 0:
                local_copies.pop(0).wait()
            across_blocks.append(
                remote(slot, slot, block_send.at[sems], block_recv.at[sems], (batch, across))
            )

    def forward_core(which):
        sems = 4 * members + which
        if which == 0:
            slot = all_phases.at[:, time]
        else:
            for copy in across_blocks:
                copy.wait_recv()
            slot = all_phases.at[:, across]
        core_blocks.append(
            remote(slot, slot, block_send.at[sems], block_recv.at[sems], (batch, core))
        )

    lowered = latent_low[...].astype(f32)

    def keep_alpha(row, rows):
        for index in range(time_count):
            alpha_out[index, row : row + 1, :] = rows[:, index * share : (index + 1) * share]

    def quantizer_gradient():
        swapped_in(swap_quant)
        push = quant_in[...].reshape(frames_all, latents) * frame_valid
        gap_back = gap_grad[...]
        looked_rows = looked[...]
        between = exact(looked_rows, gap_back, 0, 0)
        small[...] = jnp.zeros_like(small)

        def keep_small(row, rows):
            for index in range(time_count):
                columns = rows[:, index * wide_of : (index + 1) * wide_of]
                done = 0
                while done < rows.shape[0]:
                    fold, at = divmod(row + done, 128)
                    size = min(rows.shape[0] - done, 128 - at)
                    small[index, at : at + size, fold * wide_of : (fold + 1) * wide_of] = columns[
                        done : done + size
                    ]
                    done += size

        earlier_rows = jnp.where(
            lax.broadcasted_iota(jnp.int32, (count, phases), 0) // dims
            > lax.broadcasted_iota(jnp.int32, (count, phases), 1),
            1.0,
            0.0,
        )
        ones = jnp.ones((frames_all, phases), f32)
        keep_small(
            0,
            exact(gap_back, latent[...], 0, 0)
            - exact(exact(gap_back, looked_rows, 0, 0) * later, out_weight[...], 1, 0)
            - exact(exact(gap_back, ones, 0, 0) * earlier_rows, out_bias[...], 1, 0),
        )
        looked_back = exact(push, out_weight[...], 1, 1) - gap_back
        crossing = exact(out_weight[...], in_weight[...], 1, 1) * earlier
        looked_back = (looked_back - exact(gap_back, crossing, 1, 1)).T
        for phase in range(phases):
            rows = looked_back[phase * dims : (phase + 1) * dims, :]
            three = jnp.concatenate([part.astype(f32) for part in split_three(rows)], axis=0)
            found = dot(three.astype(bf16), onehot(codes, phase), 1, 0)
            keep_small(
                count + phase * dims, found[:dims] + found[dims : 2 * dims] + found[2 * dims :]
            )
        keep_small(
            2 * count,
            exact(looked_rows, push, 0, 0) - exact(between * earlier, in_weight[...], 1, 0),
        )
        gap_sum = jnp.sum(gap_back, axis=0, keepdims=True)
        keep_small(
            3 * count,
            jnp.sum(push, axis=0, keepdims=True)
            - exact(jnp.where(nine_rows < nine_columns, gap_sum, 0.0), in_weight[...], 1, 0),
        )
        row = 3 * count + phases
        keep_small(row, jnp.sum(lowered, axis=0, keepdims=True))
        fold, at = divmod(row + 1, 128)
        for index in range(time_count):
            small[index, at : at + 1, fold * wide_of : fold * wide_of + count] = gap_sum
        small_low[...] = small[...].astype(bf16)
        smalls_in = [
            remote(
                small_low.at[sibling(step)],
                small_in.at[step - 1],
                small_send.at[step - 1],
                small_recv.at[step - 1],
                (batch, sibling(step)),
            )
            for step in range(1, time_count)
        ]
        return smalls_in

    forward_pair(near_first[0])

    made.wait_recv()
    latent_pad[...] = jnp.zeros_like(latent_pad)
    latent_pad[8 : 8 + frames_all, :] = lowered
    neighbour = latent_in[...].astype(f32)
    latent_pad[7:8, :] = neighbour[15:, :] * last
    latent_pad[8 + frames_all : 9 + frames_all, :] = neighbour[:1, :] * first
    reach = frames_all + 8
    same = latent_pad[8 : 8 + reach, :].astype(bf16)
    previous = latent_pad[7 : 7 + reach, :].astype(bf16)
    run = reach * STRIDE
    for step in range(STRIDE):
        both = dot(same, down_tap(step), 1, 0) + dot(previous, down_tap(step + STRIDE), 1, 0)
        for tile in range(lane_tiles):
            spread[pl.ds(tile * run + step, reach, stride=STRIDE), :] = both[
                :, tile * 128 : (tile + 1) * 128
            ]

    alpha = row_of(snake_alpha, 6)
    inverse = 1.0 / alpha
    zero = jnp.zeros((8, channels), f32)

    def mixed_back(place, carry, edge):
        tiles = []
        for tile in range(lane_tiles):
            at = tile * run + STRIDE // 2 + place * ROWS
            tiles.append(spread[pl.ds(at, ROWS), :])
        upstream = jnp.concatenate(tiles, axis=1) * valid_rows(place)
        at = block_rows(place)
        slope, alpha_slope = snake_slopes(hidden[3, at, :], alpha, inverse)
        following = upstream * slope
        grad[at, :] = following
        keep_branch(2, place, following.astype(bf16))
        return carry + folded(upstream * alpha_slope)

    def keep_branch(unit, place, rows):
        branch[block_rows(place), :] = rows
        for index in range(time_count):
            shares[unit, index, 1, block_rows(place), :] = rows[
                :, index * share : (index + 1) * share
            ]

    alpha_sum, _ = each_block(mixed_back, zero)
    alpha_out[...] = jnp.zeros_like(alpha_out)
    keep_alpha(6, jnp.sum(alpha_sum, axis=0, keepdims=True))

    total = down.at[pl.ds(0, pieces[-1][0] + pieces[-1][1])]

    copies, regions = {}, {}

    def add_into(target, start, source, begin, other, at_other, rows):
        def step(index, carry):
            at = index * 16
            block = source[pl.ds(pl.multiple_of(begin + at, 16), 16), :].astype(f32)
            block += other[pl.ds(pl.multiple_of(at_other + at, 16), 16), :].astype(f32)
            target[pl.ds(pl.multiple_of(start + at, 16), 16), :] = block.astype(bf16)
            return carry

        lax.fori_loop(0, rows // 16, step, 0, unroll=min(4, rows // 16))

    def partner_of(bit):
        return batch + bit - 2 * bit * lax.rem(batch // bit, 2)

    def rows_at(start, rows):
        return pl.ds(pl.multiple_of(start, 16), rows)

    def send_half(number, level):
        begin, rows = regions[number, level]
        bit = bits_of[number][level]
        upper = lax.rem(batch // bit, 2)
        rows = rows // 2
        inbox = pieces[number][0] + pieces[number][1] - 2 * rows
        regions[number, level + 1] = (begin + upper * rows, rows)
        copies[number, level] = remote(
            total.at[rows_at(begin + (1 - upper) * rows, rows)],
            from_pair.at[pl.ds(inbox, rows)],
            piece_send.at[number, level],
            piece_recv.at[number, level],
            (partner_of(bit), time),
        )

    def send_back(number, level):
        begin, rows = regions[number, level + 1]
        sems = 2 * len(bits_of[number]) - 1 - level
        copies[number, sems] = remote(
            final.at[rows_at(begin, rows)],
            final.at[rows_at(begin, rows)],
            piece_send.at[number, sems],
            piece_recv.at[number, sems],
            (partner_of(bits_of[number][level]), time),
        )

    def send_pair(number):
        regions[number, 0] = pieces[number]
        send_half(number, 0)

    def advance(stage, number):
        levels = len(bits_of[number])
        copies[number, stage].wait_recv()
        if stage < levels:
            begin, rows = regions[number, stage + 1]
            inbox = pieces[number][0] + pieces[number][1] - 2 * rows
            target = final if stage + 1 == levels else total
            add_into(target, begin, total, begin, from_pair, inbox, rows)
            if stage + 1 < levels:
                send_half(number, stage + 1)
            else:
                send_back(number, stage)
        elif stage + 1 < 2 * levels:
            send_back(number, 2 * levels - 2 - stage)

    relays = {}

    def relay(unit):
        gather_across[unit].wait_recv()
        slot = gathered.at[unit, :, crops - 1 - mine, own]
        relays[unit] = remote(
            slot, slot, relay_send.at[unit], relay_recv.at[unit], (batch, core)
        )

    unit_rows = (TAPS + 1) * share
    unit_start = {unit: pieces[0][1] + unit * unit_rows for unit in range(3)}
    numbers = {
        unit: [
            number
            for number, (start, rows) in enumerate(pieces)
            if unit_start[unit] <= start < unit_start[unit] + unit_rows
        ]
        for unit in range(3)
    }
    everywhere = crops * rows_all
    shifted_start = down.shape[0] // 2
    levels = batch_count.bit_length() - 1
    bits_of = {}
    for number in range(len(pieces)):
        bits_of[number] = [2**level for level in range(levels)]
        if number in [numbers[unit][0 if unit == 0 else -1] for unit in range(3)]:
            bits_of[number][:2] = [2, 1]
    share_pad[...] = jnp.zeros_like(share_pad)
    shares_in = {}
    bias_rows = {}

    def unit_gradient(unit):
        dilation = DILATIONS[unit]
        for copy in shares_in[unit]:
            copy.wait_recv()
        for crop in range(crops):
            share_pad[crop, RIM : RIM + everywhere, :] = share_all[unit, 0, crop].astype(f32)
        bias_rows[unit] = [
            jnp.sum(
                folded(
                    jnp.concatenate(
                        [share_all[unit, kind, crop].astype(f32) for crop in range(crops)], axis=0
                    )
                ),
                axis=0,
                keepdims=True,
            )
            for kind in range(2)
        ]
        for tap in range(TAPS):
            start = RIM - (tap - 3) * dilation
            for crop in range(crops):
                bank, lane = divmod(tap, time_count)
                begin = shifted_start + (bank * crops + crop) * everywhere
                down[begin : begin + everywhere, lane * share : (lane + 1) * share] = share_pad[
                    crop, start : start + everywhere, :
                ].astype(bf16)
        gather_core[unit].wait_recv()
        relays[unit].wait_recv()
        taken = gathered[unit, 0].reshape(crops * everywhere, channels)
        at = unit_start[unit]
        for bank in range(-(-TAPS // time_count)):
            begin = shifted_start + bank * crops * everywhere
            columns = min(TAPS - bank * time_count, time_count) * share
            moved = down[begin : begin + crops * everywhere, :columns]
            row = at + bank * channels
            total[row : row + columns, :] = dot(moved, taken, 0, 0).astype(bf16)
        taken = gathered[unit, 1].reshape(crops * everywhere, channels)
        narrow_share = share_all[unit, 1].reshape(crops * everywhere, share)
        total[at + TAPS * share : at + unit_rows, :] = dot(narrow_share, taken, 0, 0).astype(bf16)
        for number in numbers[unit]:
            send_pair(number)

    def small_gradient(smalls_in):
        for copy in smalls_in:
            copy.wait_recv()
        block = small[time]
        for step in range(time_count - 1):
            block += small_in[step].astype(f32)
        small[0] = block

    def lows_members():
        for copy in lows_in:
            copy.wait_recv()
        local(low_all, all_lows.at[batch], 1)
        for step in range(1, members):
            low_blocks.append(
                remote(
                    low_all,
                    all_lows.at[batch],
                    low_send.at[2 + step],
                    low_recv.at[2 + step],
                    (member(step), time),
                )
            )
        low_blocks.append(
            remote(
                low_all,
                all_lows.at[batch],
                low_send.at[2 + members],
                low_recv.at[2 + members],
                (pair, time),
            )
        )

    def lows_pair():
        for step in range(1, members):
            low_blocks[step - 1].wait_recv()
            slot = all_lows.at[block_of(step, half)]
            sems = 2 + members + step
            low_blocks.append(
                remote(slot, slot, low_send.at[sems], low_recv.at[sems], (pair, time))
            )

    def between_units(unit):
        if unit == 2:
            lows_members()
            for step in near_first[2:]:
                forward_pair(step)
        else:
            relay(unit + 1)
            if unit == 1:
                lows_pair()
            unit_gradient(unit + 1)

    def finish_all():
        order = numbers[2] + numbers[1] + numbers[0] + [0]
        stages = [functools.partial(advance, stage) for stage in range(2 * levels)]
        for wave in range(len(order) + len(stages)):
            for depth, stage in enumerate(stages):
                if 0 <= wave - depth < len(order):
                    stage(order[wave - depth])
            if wave < members:
                forward_across(([0] + near_first)[wave])
        for step in ([0] + near_first)[len(order) + len(stages) :]:
            forward_across(step)
        forward_core(0)
        forward_core(1)
        for copy in core_blocks:
            copy.wait_recv()
        for copy in low_blocks[members - 1 :]:
            copy.wait_recv()

    for step in near_first[1:2]:
        forward_pair(step)
    for unit in (2, 1, 0):
        dilation = DILATIONS[unit]
        number = 5 + unit
        work[...] = dot(branch[...], narrow[unit], 1, 0)
        alpha = row_of(snake_alpha, 2 * unit + 1)
        inverse = 1.0 / alpha

        def conv_back(place, carry, edge):
            at = block_rows(place)
            upstream = work[at, :]
            slope, alpha_slope = snake_slopes(conv[unit, at, :], alpha, inverse)
            lowered = (upstream * slope).astype(bf16)
            for index in range(time_count):
                shares[unit, index, 0, at, :] = lowered[
                    :, index * share : (index + 1) * share
                ]
            pad[pad_rows(place), :] = lowered.astype(f32)
            keep_edge(number, edge, lowered)
            return carry + folded(upstream * alpha_slope)

        alpha_sum, made = each_block(conv_back, zero, lambda: start_halo(number))
        shares_in[unit] = [
            remote(
                shares.at[unit, sibling(step)],
                share_all.at[unit, :, mine, own],
                share_send.at[unit, step - 1],
                share_recv.at[unit, step - 1],
                (batch, sibling(step)),
            )
            for step in range(1, time_count)
        ]
        if unit == 2:
            gather(1)
        for kind in range(2):
            share_all[unit, kind, mine, own, :] = shares[unit, time, kind]
        keep_alpha(2 * unit + 1, jnp.sum(alpha_sum, axis=0, keepdims=True))
        between_units(unit)
        fill_rims(made, number)
        result = None
        for tap in range(TAPS):
            term = dot(shifted(-(tap - 3) * dilation), wide[unit, tap], 1, 0)
            result = term if result is None else result + term
        work[...] = result
        alpha = row_of(snake_alpha, 2 * unit)
        inverse = 1.0 / alpha

        def hidden_back(place, carry, edge):
            at = block_rows(place)
            upstream = work[at, :]
            slope, alpha_slope = snake_slopes(hidden[unit, at, :], alpha, inverse)
            following = grad[at, :] + upstream * slope
            if unit > 0:
                grad[at, :] = following
                keep_branch(unit - 1, place, following.astype(bf16))
            else:
                signal_out[at, :] = following * valid_rows(place)
            return carry + folded(upstream * alpha_slope)

        alpha_sum, _ = each_block(hidden_back, zero)
        keep_alpha(2 * unit, jnp.sum(alpha_sum, axis=0, keepdims=True))

    alphas_in = [
        remote(
            alpha_out.at[sibling(step)],
            alpha_in.at[step - 1],
            small_send.at[time_count - 1 + step - 1],
            small_recv.at[time_count - 1 + step - 1],
            (batch, sibling(step)),
        )
        for step in range(1, time_count)
    ]
    relay(0)
    unit_gradient(0)
    swap_back = swap(
        4,
        lambda part: signal_out.at[pl.ds(part * length, length)],
        lambda slot: signal_back.at[slot],
        mine,
        True,
    )
    small_gradient(quantizer_gradient())
    for copy in alphas_in:
        copy.wait_recv()
    alpha_rows = alpha_out[time]
    for step in range(time_count - 1):
        alpha_rows += alpha_in[step]
    rest = [alpha_rows] + [bias_rows[unit][kind] for kind in range(2) for unit in range(3)]
    rest = jnp.concatenate(rest + [jnp.zeros((2, share), f32)], axis=0)
    small[0, small.shape[1] - 16 :, channels - share :] = rest
    for start in range(0, pieces[0][1], small.shape[1]):
        total[start : start + small.shape[1], :] = small[0].astype(bf16)
    send_pair(0)

    finish_all()
    swapped_in(swap_back)
    swapped_in(swap_commit)
    for crop in range(crops):
        signal_grad[crop] = signal_back[crop].T
    for made in swaps:
        for peer, origin, away, here, arrived in made:

            @pl.when(peer != time)
            def _():
                away.wait_send()

    for copy in local_copies:
        copy.wait()
    for copy in sent:
        copy.wait_send()


def run_block(time_count, batch_count, pieces, lengths, *arrays):
    (signal, quant_cot, coded, wide, _, narrow, _, _, down, down_bias, in_weight) = arrays[:11]
    f32, bf16 = jnp.float32, jnp.bfloat16
    crops, channels, length = signal.shape
    latents = down_bias.shape[1]
    taps = down.shape[0] // latents
    frames = crops * (length // STRIDE)
    rows = crops * length
    count = in_weight.shape[0]
    share = channels // time_count
    wide_of = latents // time_count
    members = batch_count // 2
    everywhere = crops * rows
    total_rows = pieces[-1][0] + pieces[-1][1]
    vmem = pl.BlockSpec(memory_space=pltpu.VMEM)
    hbm = pl.BlockSpec(memory_space=pl.ANY)
    in_specs = [pl.BlockSpec(memory_space=pltpu.SMEM)] + [vmem] * len(arrays)
    for place in (0, 1, 3, 5, 8):
        in_specs[1 + place] = hbm
    lane_tiles = channels // 128
    dma = pltpu.SemaphoreType.DMA
    slots = 2 * members
    return pl.pallas_call(
        functools.partial(block_kernel, time_count, batch_count, pieces),
        out_shape=(
            jax.ShapeDtypeStruct(quant_cot.shape, f32),
            jax.ShapeDtypeStruct(coded.shape, f32),
            jax.ShapeDtypeStruct(signal.shape, f32),
            jax.ShapeDtypeStruct((total_rows, channels), bf16),
            jax.ShapeDtypeStruct((batch_count, time_count, STRIDE, frames, channels), bf16),
            jax.ShapeDtypeStruct((batch_count, time_count, frames, wide_of), bf16),
        ),
        in_specs=in_specs,
        out_specs=(vmem, vmem, vmem, vmem, hbm, hbm),
        scratch_shapes=[
            pltpu.VMEM(wide.shape, bf16),
            pltpu.VMEM(narrow.shape, bf16),
            pltpu.VMEM((taps * latents, channels), bf16),
            pltpu.VMEM((4, rows, channels), f32),
            pltpu.VMEM((3, rows, channels), f32),
            pltpu.VMEM((3, 2, crops, everywhere, channels), bf16),
            pltpu.VMEM((rows + 2 * RIM, channels), f32),
            pltpu.VMEM((rows, channels), f32),
            pltpu.VMEM((rows, channels), f32),
            pltpu.VMEM((rows, channels), bf16),
            pltpu.VMEM((3, time_count, 2, rows, share), bf16),
            pltpu.VMEM((3, 2, crops, everywhere, share), bf16),
            pltpu.VMEM((crops, everywhere + 2 * RIM, share), f32),
            pltpu.VMEM((lane_tiles * (rows + 16), 128), f32),
            pltpu.VMEM((taps, frames, channels), bf16),
            pltpu.VMEM((frames, latents), f32),
            pltpu.VMEM((frames + 16, latents), f32),
            pltpu.VMEM((lane_tiles * (rows + 8 * STRIDE), 128), f32),
            pltpu.VMEM((frames, count), f32),
            pltpu.VMEM((frames, count), f32),
            pltpu.VMEM((frames, count), f32),
            pltpu.VMEM((time_count, 128, channels), f32),
            pltpu.VMEM((time_count, 128, channels), bf16),
            pltpu.VMEM((time_count - 1, 128, channels), bf16),
            pltpu.VMEM((time_count, 8, share), f32),
            pltpu.VMEM((time_count - 1, 8, share), f32),
            pltpu.VMEM((time_count, frames, wide_of), bf16),
            pltpu.VMEM((time_count, frames, wide_of), bf16),
            pltpu.VMEM((144, channels), bf16),
            pltpu.VMEM((144, channels), bf16),
            pltpu.VMEM((frames, latents), bf16),
            pltpu.VMEM((16, latents), bf16),
            pltpu.VMEM(signal.shape, f32),
            pltpu.VMEM(quant_cot.shape, f32),
            pltpu.VMEM(coded.shape, f32),
            pltpu.VMEM(coded.shape, f32),
            pltpu.VMEM((rows, channels), f32),
            pltpu.VMEM((crops, length, channels), f32),
            dma((5,)),
            dma((5, 2)),
            dma((5, 2)),
            pltpu.VMEM((total_rows, channels), bf16),
            dma((8,)),
            dma((2,)),
            dma((8,)),
            dma((8,)),
            dma((3, 2)),
            dma((3, 2)),
            dma((3,)),
            dma((3,)),
            dma((3, time_count - 1)),
            dma((3, time_count - 1)),
            dma((2 * (time_count - 1),)),
            dma((2 * (time_count - 1),)),
            dma((2 + 2 * members,)),
            dma((2 + 2 * members,)),
            dma((4 * members + 2,)),
            dma((4 * members + 2,)),
            dma((len(pieces), slots)),
            dma((len(pieces), slots)),
        ],
        compiler_params=pltpu.CompilerParams(
            collective_id=1, has_side_effects=True, vmem_limit_bytes=62 * 2**20
        ),
    )(lengths, *arrays)


def down_kernel(line, lows, phases, out, held, columns, in_sems, out_sems):
    count = lows.shape[1]
    group, lanes = held.shape[1], held.shape[4]
    rows = group * held.shape[3]
    tiles = lanes // 128
    groups = phases.shape[0] // group
    items = [(part, at) for part in range(phases.shape[3] // lanes) for at in range(groups)]
    loads = [
        pltpu.make_async_copy(
            phases.at[pl.ds(at * group, group), :, :, pl.ds(part * lanes, lanes)],
            held.at[index % 2],
            in_sems.at[index % 2],
        )
        for index, (part, at) in enumerate(items)
    ]
    for load in loads[:2]:
        load.start()
    stores = []
    after = before = None
    for index, (part, at) in enumerate(items):
        if after is None or groups > 1:
            rows_here = lows[at * rows : (at + 1) * rows, :].astype(jnp.float32).T
            place = lax.rem(lax.broadcasted_iota(jnp.int32, rows_here.shape, 1), line)
            following = jnp.where(place < line - 1, pltpu.roll(rows_here, rows - 1, 1), 0.0)
            preceding = jnp.where(place > 0, pltpu.roll(rows_here, 1, 1), 0.0)
            after = jnp.concatenate([rows_here, following], axis=0).astype(lows.dtype)
            before = jnp.concatenate([rows_here, preceding], axis=0).astype(lows.dtype)
        loads[index].wait()
        for step in range(STRIDE):
            block = held[index % 2, :, step].reshape(rows, lanes)
            late = step >= STRIDE // 2
            both = dot(after if late else before, block, 1, 0)
            middle = step + STRIDE // 2
            for tap, row in ((middle, 0), (middle - STRIDE if late else middle + STRIDE, count)):
                for tile in range(tiles):
                    place = pl.ds(tap, count, stride=2 * STRIDE)
                    value = both[row : row + count, tile * 128 : (tile + 1) * 128]
                    if at > 0:
                        value = value + columns[part * tiles + tile, place, :]
                    columns[part * tiles + tile, place, :] = value
        if index + 2 < len(items):
            loads[index + 2].start()
        if at == groups - 1:
            for tile in range(part * tiles, (part + 1) * tiles):
                stores.append(
                    pltpu.make_async_copy(
                        columns.at[tile], out.at[:, pl.ds(tile * 128, 128)], out_sems.at[tile]
                    )
                )
                stores[-1].start()
    for store in stores:
        store.wait()


def down_gradient(lows, phases, line):
    devices, _, rows, channels = phases.shape
    count = lows.shape[1]
    lanes = 256
    hbm = pl.BlockSpec(memory_space=pl.ANY)
    return pl.pallas_call(
        functools.partial(down_kernel, line),
        out_shape=jax.ShapeDtypeStruct((count * 2 * STRIDE, channels), jnp.float32),
        in_specs=[pl.BlockSpec(memory_space=pltpu.VMEM), hbm],
        out_specs=hbm,
        scratch_shapes=[
            pltpu.VMEM((2, min(devices, 32), STRIDE, rows, lanes), phases.dtype),
            pltpu.VMEM((channels // 128, count * 2 * STRIDE, 128), jnp.float32),
            pltpu.SemaphoreType.DMA((2,)),
            pltpu.SemaphoreType.DMA((channels // 128,)),
        ],
        compiler_params=pltpu.CompilerParams(vmem_limit_bytes=60 * 2**20),
    )(lows, phases)


def body(
    signal,
    quant_cot,
    commit_cot,
    lengths,
    codes,
    wide_weight,
    wide_bias,
    narrow_weight,
    narrow_bias,
    snake_alpha,
    down_weight,
    down_bias,
    in_weight,
    in_bias,
    codebook,
    out_weight,
    out_bias,
):
    time_count = lax.axis_size("tm")
    batch_count = lax.axis_size("batch")
    crop_count, channel_count, length = signal.shape
    latent_count, tap_count, _ = down_weight.shape
    phases, dims = in_weight.shape[:2]
    count = phases * dims
    frame_count = length // STRIDE
    small_rows = 16 * batch_count
    unit_rows = (TAPS + 1) * (channel_count // time_count)
    piece = max(unit_rows // 2, small_rows)
    pieces = [(0, small_rows)]
    pieces += [(at, piece) for at in range(small_rows, small_rows + 3 * unit_rows, piece)]
    coded = [jnp.swapaxes(codes, 1, 2).astype(jnp.float32), jnp.swapaxes(commit_cot, 1, 2)]
    coded = jnp.pad(jnp.concatenate(coded, axis=2), ((0, 0), (0, 0), (0, 128 - 2 * phases)))
    quantized, commit, signal_grad, summed, all_phases, all_low = run_block(
        time_count,
        batch_count,
        tuple(pieces),
        lengths,
        signal,
        quant_cot,
        coded,
        jnp.swapaxes(wide_weight, 1, 2),
        wide_bias,
        narrow_weight,
        narrow_bias,
        snake_alpha,
        down_weight.reshape(-1, channel_count),
        down_bias.reshape(1, -1),
        in_weight.reshape(count, -1),
        in_bias.reshape(1, -1),
        codebook.reshape(count, -1),
        out_weight.reshape(count, -1),
        out_bias,
    )
    commit = jnp.swapaxes(commit[:, :, :phases], 1, 2)

    share = latent_count // time_count
    all_phases = all_phases.reshape((-1,) + all_phases.shape[2:])
    lows = all_low.reshape(-1, share)
    wide_of = latent_count // time_count
    small = summed[:128].astype(jnp.float32)
    small = jnp.concatenate([small[:, :wide_of], small[:, wide_of : 2 * wide_of]], axis=0)
    in_weight_out = small[:count].reshape(phases, dims, -1)
    codebook_out = small[count : 2 * count].reshape(phases, dims, -1)
    out_weight_out = small[2 * count : 3 * count].reshape(phases, dims, -1)
    row = 3 * count + phases
    out_bias_out = small[3 * count : row]
    down_bias_out = small[row]
    narrow_of = channel_count // time_count
    in_bias_all = small[row + 1, :count].reshape(phases, dims)
    part = dims // time_count
    in_bias_out = lax.dynamic_slice_in_dim(in_bias_all, lax.axis_index("tm") * part, part, axis=1)
    last = summed[112:128, -narrow_of:].astype(jnp.float32)
    alpha_out, wide_bias_out, narrow_bias_out = last[:7], last[8:11], last[11:14]
    units = summed[small_rows:].reshape(3, unit_rows, channel_count)
    wide_out = units[:, : TAPS * narrow_of].astype(jnp.float32)
    wide_out = wide_out.reshape(3, TAPS, narrow_of, channel_count)
    wide_out = jnp.swapaxes(wide_out, 1, 2)
    narrow_out = units[:, TAPS * narrow_of :].astype(jnp.float32)
    down_out = down_gradient(lows, all_phases, time_count * frame_count).reshape(share, tap_count, channel_count)
    return (
        quantized,
        commit,
        signal_grad,
        wide_out,
        wide_bias_out,
        narrow_out,
        narrow_bias_out,
        alpha_out,
        down_out,
        down_bias_out,
        in_weight_out,
        in_bias_out,
        codebook_out,
        out_weight_out,
        out_bias_out,
    )


def solution(mesh):
    return jax.shard_map(
        body,
        mesh=mesh,
        in_specs=(
            P("batch", None, "tm"),
            P("batch", "tm", None),
            P("batch", None, "tm"),
            P("batch"),
            P("batch", None, "tm"),
            P(),
            P(),
            P(),
            P(),
            P(),
            P(),
            P(),
            P(),
            P(),
            P(),
            P(),
            P(),
        ),
        out_specs=(
            P("batch", "tm", None),
            P("batch", None, "tm"),
            P("batch", None, "tm"),
            P(None, "tm", None, None),
            P(None, "tm"),
            P(None, "tm", None),
            P(None, "tm"),
            P(None, "tm"),
            P("tm", None, None),
            P("tm"),
            P(None, None, "tm"),
            P(None, "tm"),
            P(None, None, "tm"),
            P(None, None, "tm"),
            P(None, "tm"),
        ),
        check_vma=False,
    )
```

```python
import functools

import jax
import jax.numpy as jnp
from jax import lax
from jax.experimental import pallas as pl
from jax.experimental.pallas import tpu as pltpu
from jax.sharding import PartitionSpec as P

STRIDE = 8


DILATIONS = (1, 3, 9)
MESH = pl.DeviceIdType.MESH
BLOCK = 64


TAPS = 7
RIM = 32
ROWS = 32


def dot(left, right, left_dim, right_dim, precision=None):
    return lax.dot_general(
        left,
        right,
        (((left_dim,), (right_dim,)), ((), ())),
        precision=precision,
        preferred_element_type=jnp.float32,
    )


def exact(left, right, left_dim, right_dim):
    return dot(left, right, left_dim, right_dim, lax.Precision.HIGHEST)


def reduced_angle(angle):
    turns = jnp.floor(angle * 0.3183098861837907 + 0.5)
    rest = angle - turns * 3.140625
    rest = rest - turns * 9.67502593994140625e-4
    return rest - turns * 1.509957990978376432e-7


def sine(rest, square):
    series = -1.0 / 5040.0 + square * (1.0 / 362880.0 - square * (1.0 / 39916800.0))
    return rest + rest * square * (-1.0 / 6.0 + square * (1.0 / 120.0 + square * series))


def cosine(square):
    series = 1.0 / 40320.0 + square * (-1.0 / 3628800.0 + square * (1.0 / 479001600.0))
    return 1.0 + square * (-0.5 + square * (1.0 / 24.0 + square * (-1.0 / 720.0 + square * series)))


def snake_of(values, alpha, inverse):
    rest = reduced_angle(alpha * values)
    wave = sine(rest, rest * rest)
    return values + wave * wave * inverse


def snake_slopes(values, alpha, inverse):
    rest = reduced_angle(alpha * values)
    square = rest * rest
    wave = sine(rest, square)
    double = 2.0 * wave * cosine(square)
    return 1.0 + double, (values * double - wave * wave * inverse) * inverse


def split_three(values):
    first = values.astype(jnp.bfloat16)
    rest = values - first.astype(jnp.float32)
    second = rest.astype(jnp.bfloat16)
    third = (rest - second.astype(jnp.float32)).astype(jnp.bfloat16)
    return first, second, third


def folded(values):
    return jnp.sum(values.reshape(values.shape[0] // 8, 8, values.shape[1]), axis=0)


def block_kernel(
    time_count,
    batch_count,
    pieces,
    lengths,
    signal,
    quant_cot,
    coded,
    wide_hbm,
    wide_bias,
    narrow_hbm,
    narrow_bias,
    snake_alpha,
    down_hbm,
    down_bias,
    in_weight,
    in_bias,
    codebook,
    out_weight,
    out_bias,
    quantized,
    commit,
    signal_grad,
    final,
    all_phases,
    all_lows,
    wide,
    narrow,
    down,
    hidden,
    conv,
    gathered,
    pad,
    grad,
    work,
    branch,
    shares,
    share_all,
    share_pad,
    mixed_pad,
    frames,
    latent,
    latent_pad,
    spread,
    looked,
    gap_grad,
    correction,
    small,
    small_low,
    small_in,
    alpha_out,
    alpha_in,
    low_shares,
    low_all,
    halo_out,
    halo_in,
    latent_low,
    latent_in,
    signal_in,
    quant_in,
    coded_in,
    commit_out,
    signal_out,
    signal_back,
    swap_local,
    swap_send,
    swap_recv,
    from_pair,
    weight_sems,
    local_sems,
    send_sems,
    recv_sems,
    gather_send,
    gather_recv,
    relay_send,
    relay_recv,
    share_send,
    share_recv,
    small_send,
    small_recv,
    low_send,
    low_recv,
    block_send,
    block_recv,
    piece_send,
    piece_recv,
):
    f32, bf16 = jnp.float32, jnp.bfloat16
    sent = []
    batch = lax.axis_index("batch")
    time = lax.axis_index("tm")
    crops, channels, length = signal.shape
    latents = down_bias.shape[1]
    mine = time // crops
    side = lax.rem(time, crops)
    rows_all = crops * length
    blocks = rows_all // ROWS
    frame_count = length // STRIDE
    frames_all = crops * frame_count
    phases = out_bias.shape[0]
    dims = in_weight.shape[0] // phases
    count = phases * dims
    share = channels // time_count
    wide_of = latents // time_count

    core = crops * mine + 1 - side
    across = lax.rem(time + crops, time_count)
    members = batch_count // 2
    half = lax.rem(batch, 2)
    place_z = batch // 2
    pair = 2 * place_z + 1 - half

    def member(step):
        return 2 * lax.rem(place_z + step, members) + half

    def sibling(step):
        return lax.rem(time + step, time_count)

    peers = [(batch, sibling(step)) for step in range(1, time_count)]
    peers += [(pair, time)] + [(member(step), time) for step in range(1, members)]
    barrier = pltpu.get_barrier_semaphore()
    for peer in peers:
        pl.semaphore_signal(barrier, inc=1, device_id=peer, device_id_type=MESH)

    def remote(source, target, send_sem, recv_sem, device):
        copy = pltpu.make_async_remote_copy(
            src_ref=source,
            dst_ref=target,
            send_sem=send_sem,
            recv_sem=recv_sem,
            device_id=device,
            device_id_type=MESH,
        )
        copy.start()
        sent.append(copy)
        return copy

    wide_copies = [
        pltpu.make_async_copy(wide_hbm.at[unit], wide.at[unit], weight_sems.at[unit])
        for unit in range(3)
    ]
    narrow_copy = pltpu.make_async_copy(narrow_hbm, narrow, weight_sems.at[3])
    taps = frames.shape[0]
    group = 16 * taps
    quarter = down.shape[0] // 4
    down_copies = [
        pltpu.make_async_copy(
            down_hbm.at[pl.ds(part * quarter, quarter)],
            down.at[pl.ds(part * quarter, quarter)],
            weight_sems.at[4 + part],
        )
        for part in range(4)
    ]
    first, last = jnp.where(side == 0, 1.0, 0.0), jnp.where(side == 1, 1.0, 0.0)

    def swap(number, source, target, slot, back):
        made = []
        for part in range(crops):
            peer = crops * side + part if back else crops * part + mine
            origin = crops * part + mine if back else crops * side + part
            away = pltpu.make_async_remote_copy(
                src_ref=source(part),
                dst_ref=target(slot),
                send_sem=swap_send.at[number, part],
                recv_sem=swap_recv.at[number, slot],
                device_id=(batch, peer),
                device_id_type=MESH,
            )
            here = pltpu.make_async_copy(source(part), target(slot), swap_local.at[number])
            arrived = pltpu.make_async_remote_copy(
                src_ref=source(part),
                dst_ref=target(part),
                send_sem=swap_send.at[number, part],
                recv_sem=swap_recv.at[number, part],
                device_id=(batch, peer),
                device_id_type=MESH,
            )

            @pl.when(peer != time)
            def _():
                away.start()

            @pl.when(peer == time)
            def _():
                here.start()

            made.append((peer, origin, away, here, arrived))
        swaps.append(made)
        return made

    def swapped_in(made):
        for peer, origin, away, here, arrived in made:

            @pl.when(origin != time)
            def _():
                arrived.wait_recv()

            @pl.when(origin == time)
            def _():
                here.wait()

    swaps = []

    halo_rows = (16, 16, 32, 16, 0, 16, 16, 32)
    halo_start = [sum(halo_rows[:number]) for number in range(len(halo_rows))]

    def start_halo(number):
        rows = pl.ds(halo_start[number], halo_rows[number])
        return remote(
            halo_out.at[rows],
            halo_in.at[rows],
            send_sems.at[number],
            recv_sems.at[number],
            (batch, core),
        )

    def fill_rims(made, number):
        width, begin = halo_rows[number], halo_start[number]
        made.wait_recv()
        rim = halo_in[begin : begin + width, :].astype(f32)
        pad[RIM - width : RIM, :] = rim * last
        pad[RIM + rows_all : RIM + rows_all + width, :] = rim * first

    def each_block(step, carry, edge_then=None):
        carry = step((1 - side) * (blocks - 1), carry, True)
        made = edge_then() if edge_then is not None else None

        def inside(index, carry):
            return step(index + side, carry, False)

        return lax.fori_loop(0, blocks - 1, inside, carry), made

    def keep_edge(number, edge, rows):
        if edge:
            width, begin = halo_rows[number], halo_start[number]
            ahead, behind = rows[ROWS - width :].astype(f32), rows[:width].astype(f32)
            halo_out[begin : begin + width, :] = (ahead * first + behind * last).astype(bf16)

    def row_of(ref, row):
        return ref[row : row + 1, :]

    def valid_rows(place):
        places = side * rows_all + place * ROWS + lax.broadcasted_iota(jnp.int32, (ROWS, 1), 0)
        return jnp.where(places < lengths[mine], 1.0, 0.0)

    def reorder(part):
        rows = lax.broadcasted_iota(jnp.int32, (group, group), 0)
        columns = lax.broadcasted_iota(jnp.int32, (group, group), 1)
        turn = jnp.where(columns == lax.rem(rows, 16) * taps + rows // 16, 1.0, 0.0).astype(bf16)
        down_copies[part].wait()

        def step(index, carry):
            places = [
                pl.ds(pl.multiple_of(part * quarter + (4 * index + which) * group, group), group)
                for which in range(4)
            ]
            turned = [dot(turn, down[at, :], 1, 0).astype(bf16) for at in places]
            for at, rows in zip(places, turned):
                down[at, :] = rows
            return carry

        lax.fori_loop(0, quarter // group // 4, step, 0)

    def down_tap(tap):
        tiles = down.reshape(latents // 16, taps, 16, channels)
        return tiles[:, tap].reshape(latents, channels)

    pl.semaphore_wait(barrier, len(peers))
    swap_coded = swap(2, lambda part: coded.at[part], lambda slot: coded_in.at[slot], side, False)
    swap_signal = swap(0, lambda part: signal.at[part], lambda slot: signal_in.at[slot], side, False)
    swap_quant = swap(1, lambda part: quant_cot.at[part], lambda slot: quant_in.at[slot], side, False)
    wide_copies[0].start()
    narrow_copy.start()
    for copy in down_copies:
        copy.start()
    wide_copies[1].start()
    wide_copies[2].start()

    code_lanes = lax.broadcasted_iota(jnp.int32, (frames_all, codebook.shape[1]), 1).astype(f32)
    frame_rows = lax.broadcasted_iota(jnp.int32, (frames_all, 1), 0)

    def onehot(codes, phase):
        return jnp.where(codes[:, phase : phase + 1] == code_lanes, 1.0, 0.0).astype(bf16)

    def look_up(codes):
        found = []
        for phase in range(phases):
            rows = codebook[phase * dims : (phase + 1) * dims, :]
            three = jnp.concatenate([part.astype(f32) for part in split_three(rows)], axis=0)
            all_three = dot(three.astype(bf16), onehot(codes, phase), 1, 1)
            found.append(all_three[:dims] + all_three[dims : 2 * dims] + all_three[2 * dims :])
        return jnp.concatenate(found, axis=0).T

    looked_rows = look_up(coded[...].reshape(frames_all, -1))
    frame_place = time * frame_count + lax.rem(frame_rows, frame_count)
    frame_length = jnp.where(frame_rows < frame_count, lengths[0], lengths[crops - 1])
    frame_valid = jnp.where(STRIDE * frame_place < frame_length, 1.0, 0.0)
    quantized[...] = (
        (exact(looked_rows, out_weight[...], 1, 0) + jnp.sum(out_bias[...], axis=0, keepdims=True))
        * frame_valid
    ).reshape(quantized.shape)
    for part in range(4):
        reorder(part)

    swapped_in(swap_signal)
    for part in range(crops):
        places = side * rows_all + part * length + lax.broadcasted_iota(jnp.int32, (length, 1), 0)
        keep = jnp.where(places < lengths[mine], 1.0, 0.0)
        hidden[0, part * length : (part + 1) * length, :] = signal_in[part].T * keep

    def block_rows(place):
        return pl.ds(pl.multiple_of(place * ROWS, ROWS), ROWS)

    def own_rows(place):
        return pl.ds(pl.multiple_of(side * rows_all + place * ROWS, ROWS), ROWS)

    own = pl.ds(pl.multiple_of(side * rows_all, rows_all), rows_all)

    def pad_rows(place):
        return pl.ds(pl.multiple_of(RIM + place * ROWS, ROWS), ROWS)

    def shifted(offset):
        start = RIM + offset
        return pad[start : start + rows_all, :].astype(bf16)

    gather_across, gather_core = {}, {}

    def gather(unit):
        slot = gathered.at[unit, :, mine, own]
        gather_across[unit] = remote(
            slot, slot, gather_send.at[unit, 0], gather_recv.at[unit, 0], (batch, across)
        )
        gather_core[unit] = remote(
            slot, slot, gather_send.at[unit, 1], gather_recv.at[unit, 1], (batch, core)
        )

    for unit in range(3):
        dilation = DILATIONS[unit]
        alpha = row_of(snake_alpha, 2 * unit)
        inverse = 1.0 / alpha

        def first_snake(place, carry, edge):
            low = snake_of(hidden[unit, block_rows(place), :], alpha, inverse).astype(bf16)
            gathered[unit, 0, mine, own_rows(place), :] = low
            pad[pad_rows(place), :] = low.astype(f32)
            keep_edge(unit, edge, low)
            return carry

        _, made = each_block(first_snake, 0, lambda: start_halo(unit))
        fill_rims(made, unit)
        wide_copies[unit].wait()
        result = None
        for tap in range(TAPS):
            term = dot(shifted((tap - 3) * dilation), wide[unit, tap], 1, 1)
            result = term if result is None else result + term
        conv[unit] = result + row_of(wide_bias, unit)
        alpha = row_of(snake_alpha, 2 * unit + 1)
        inverse = 1.0 / alpha

        def second_snake(place, carry, edge):
            values = snake_of(conv[unit, block_rows(place), :], alpha, inverse)
            gathered[unit, 1, mine, own_rows(place), :] = values.astype(bf16)
            return carry

        each_block(second_snake, 0)
        if unit == 0:
            narrow_copy.wait()
        if unit != 1:
            gather(unit)
        rounded = gathered[unit, 1, mine, own, :]
        hidden[unit + 1] = (
            hidden[unit] + dot(rounded, narrow[unit], 1, 1) + row_of(narrow_bias, unit)
        )

    lane_tiles = channels // 128
    stretch = rows_all + 16
    alpha = row_of(snake_alpha, 6)
    inverse = 1.0 / alpha

    def last_snake(place, carry, edge):
        values = snake_of(hidden[3, block_rows(place), :], alpha, inverse)
        low = (values * valid_rows(place)).astype(bf16)
        keep_edge(3, edge, low)
        wider = low.astype(f32)
        for tile in range(lane_tiles):
            at = pl.multiple_of(tile * stretch + 8 + place * ROWS, 8)
            mixed_pad[pl.ds(at, ROWS), :] = wider[:, tile * 128 : (tile + 1) * 128]
        return carry

    _, made = each_block(last_snake, 0, lambda: start_halo(3))
    swapped_in(swap_coded)
    codes = coded_in[...].reshape(frames_all, -1)
    looked[...] = look_up(codes)
    looked_rows = looked[...]
    frame_place = side * frames_all + frame_rows
    frame_valid = jnp.where(STRIDE * frame_place < lengths[mine], 1.0, 0.0)
    phase_of_row = lax.broadcasted_iota(jnp.int32, (count, count), 0) // dims
    phase_of_column = lax.broadcasted_iota(jnp.int32, (count, count), 1) // dims
    earlier = jnp.where(phase_of_row < phase_of_column, 1.0, 0.0)
    later = jnp.where(phase_of_row > phase_of_column, 1.0, 0.0)
    crossing = exact(out_weight[...], in_weight[...], 1, 1) * earlier
    bias_terms = exact(out_bias[...], in_weight[...], 1, 1)
    nine_rows = lax.broadcasted_iota(jnp.int32, (phases, count), 0)
    nine_columns = lax.broadcasted_iota(jnp.int32, (phases, count), 1) // dims
    bias_terms = jnp.sum(jnp.where(nine_rows < nine_columns, bias_terms, 0.0), axis=0, keepdims=True)
    correction[...] = exact(looked_rows, crossing, 1, 0) + bias_terms - in_bias[...]

    made.wait_recv()
    begin = halo_start[3]
    rim = halo_in[begin : begin + 16, :].astype(f32)
    before, after = rim[8:] * last, rim[:8] * first
    for tile in range(lane_tiles):
        base = tile * stretch
        lanes = slice(tile * 128, (tile + 1) * 128)
        mixed_pad[base : base + 8, :] = before[:, lanes]
        mixed_pad[base + 8 + rows_all : base + 16 + rows_all, :] = after[:, lanes]
    for tap in range(taps):
        for tile in range(lane_tiles):
            base = tile * stretch + tap + 4
            frames[tap, :, tile * 128 : (tile + 1) * 128] = mixed_pad[
                pl.ds(base, frames_all, stride=STRIDE), :
            ].astype(bf16)
    local_copies = []

    def local(source, target, number):
        copy = pltpu.make_async_copy(source, target, local_sems.at[number])
        copy.start()
        local_copies.append(copy)

    own_phases = frames.at[pl.ds(taps // 2 - STRIDE // 2, STRIDE)]
    local(own_phases, all_phases.at[batch, time], 0)
    pair_blocks = {
        0: remote(
            own_phases,
            all_phases.at[batch, time],
            block_send.at[members],
            block_recv.at[members],
            (pair, time),
        )
    }
    near_first = sorted(range(1, members), key=lambda step: min(step, members - step))
    z_blocks = {
        step: remote(
            own_phases,
            all_phases.at[batch, time],
            block_send.at[step],
            block_recv.at[step],
            (member(step), time),
        )
        for step in near_first
    }

    result = None
    for tap in range(taps):
        term = dot(frames[tap], down_tap(tap), 1, 1)
        result = term if result is None else result + term
    latent[...] = result + down_bias[...]

    gap = exact(latent[...], in_weight[...], 1, 1) - correction[...] - looked_rows
    grouping = jnp.where(
        lax.broadcasted_iota(jnp.int32, (count, phases), 0) // dims
        == lax.broadcasted_iota(jnp.int32, (count, phases), 1),
        1.0,
        0.0,
    )
    squares = exact(gap * gap, grouping, 1, 0) * frame_valid
    commit_out[...] = jnp.concatenate(
        [squares, jnp.zeros((frames_all, 128 - phases), f32)], axis=1
    ).reshape(commit_out.shape)
    swap_commit = swap(3, lambda part: commit_out.at[part], lambda slot: commit.at[slot], mine, True)
    commit_cot = codes[:, phases : 2 * phases]
    gap_back = 2.0 * (exact(commit_cot * frame_valid, grouping, 1, 1) * gap)
    gap_grad[...] = gap_back
    lowered = exact(gap_back, in_weight[...], 1, 0).astype(bf16)
    latent_low[...] = lowered
    for index in range(time_count):
        low_shares[index] = lowered[:, index * wide_of : (index + 1) * wide_of]

    edge_frames = pl.ds(pl.multiple_of((1 - side) * (frames_all - 16), 16), 16)
    made = remote(
        latent_low.at[edge_frames], latent_in, send_sems.at[4], recv_sems.at[4], (batch, core)
    )

    low_all[time] = low_shares[time]
    lows_in = [
        remote(
            low_shares.at[sibling(step)],
            low_all.at[time],
            low_send.at[step - 1],
            low_recv.at[step - 1],
            (batch, sibling(step)),
        )
        for step in range(1, time_count)
    ]

    across_blocks, low_blocks, core_blocks = [], [], []

    def block_of(step, half):
        return 2 * lax.rem(place_z - step + members, members) + half

    def forward_pair(step):
        z_blocks[step].wait_recv()
        slot = all_phases.at[block_of(step, half), time]
        sems = members + step
        pair_blocks[step] = remote(
            slot, slot, block_send.at[sems], block_recv.at[sems], (pair, time)
        )

    def forward_across(step):
        pair_blocks[step].wait_recv()
        for order, which in enumerate((half, 1 - half)):
            slot = all_phases.at[block_of(step, which), time]
            sems = 2 * members + 2 * step + order
            if step == 0 and order == 0:
                local_copies.pop(0).wait()
            across_blocks.append(
                remote(slot, slot, block_send.at[sems], block_recv.at[sems], (batch, across))
            )

    def forward_core(which):
        sems = 4 * members + which
        if which == 0:
            slot = all_phases.at[:, time]
        else:
            for copy in across_blocks:
                copy.wait_recv()
            slot = all_phases.at[:, across]
        core_blocks.append(
            remote(slot, slot, block_send.at[sems], block_recv.at[sems], (batch, core))
        )

    lowered = latent_low[...].astype(f32)

    def keep_alpha(row, rows):
        for index in range(time_count):
            alpha_out[index, row : row + 1, :] = rows[:, index * share : (index + 1) * share]

    def quantizer_gradient():
        swapped_in(swap_quant)
        push = quant_in[...].reshape(frames_all, latents) * frame_valid
        gap_back = gap_grad[...]
        looked_rows = looked[...]
        between = exact(looked_rows, gap_back, 0, 0)
        small[...] = jnp.zeros_like(small)

        def keep_small(row, rows):
            for index in range(time_count):
                columns = rows[:, index * wide_of : (index + 1) * wide_of]
                done = 0
                while done < rows.shape[0]:
                    fold, at = divmod(row + done, 128)
                    size = min(rows.shape[0] - done, 128 - at)
                    small[index, at : at + size, fold * wide_of : (fold + 1) * wide_of] = columns[
                        done : done + size
                    ]
                    done += size

        earlier_rows = jnp.where(
            lax.broadcasted_iota(jnp.int32, (count, phases), 0) // dims
            > lax.broadcasted_iota(jnp.int32, (count, phases), 1),
            1.0,
            0.0,
        )
        ones = jnp.ones((frames_all, phases), f32)
        keep_small(
            0,
            exact(gap_back, latent[...], 0, 0)
            - exact(exact(gap_back, looked_rows, 0, 0) * later, out_weight[...], 1, 0)
            - exact(exact(gap_back, ones, 0, 0) * earlier_rows, out_bias[...], 1, 0),
        )
        looked_back = exact(push, out_weight[...], 1, 1) - gap_back
        crossing = exact(out_weight[...], in_weight[...], 1, 1) * earlier
        looked_back = (looked_back - exact(gap_back, crossing, 1, 1)).T
        for phase in range(phases):
            rows = looked_back[phase * dims : (phase + 1) * dims, :]
            three = jnp.concatenate([part.astype(f32) for part in split_three(rows)], axis=0)
            found = dot(three.astype(bf16), onehot(codes, phase), 1, 0)
            keep_small(
                count + phase * dims, found[:dims] + found[dims : 2 * dims] + found[2 * dims :]
            )
        keep_small(
            2 * count,
            exact(looked_rows, push, 0, 0) - exact(between * earlier, in_weight[...], 1, 0),
        )
        gap_sum = jnp.sum(gap_back, axis=0, keepdims=True)
        keep_small(
            3 * count,
            jnp.sum(push, axis=0, keepdims=True)
            - exact(jnp.where(nine_rows < nine_columns, gap_sum, 0.0), in_weight[...], 1, 0),
        )
        row = 3 * count + phases
        keep_small(row, jnp.sum(lowered, axis=0, keepdims=True))
        fold, at = divmod(row + 1, 128)
        for index in range(time_count):
            small[index, at : at + 1, fold * wide_of : fold * wide_of + count] = gap_sum
        small_low[...] = small[...].astype(bf16)
        smalls_in = [
            remote(
                small_low.at[sibling(step)],
                small_in.at[step - 1],
                small_send.at[step - 1],
                small_recv.at[step - 1],
                (batch, sibling(step)),
            )
            for step in range(1, time_count)
        ]
        return smalls_in

    forward_pair(near_first[0])

    made.wait_recv()
    latent_pad[...] = jnp.zeros_like(latent_pad)
    latent_pad[8 : 8 + frames_all, :] = lowered
    neighbour = latent_in[...].astype(f32)
    latent_pad[7:8, :] = neighbour[15:, :] * last
    latent_pad[8 + frames_all : 9 + frames_all, :] = neighbour[:1, :] * first
    reach = frames_all + 8
    same = latent_pad[8 : 8 + reach, :].astype(bf16)
    previous = latent_pad[7 : 7 + reach, :].astype(bf16)
    run = reach * STRIDE
    for step in range(STRIDE):
        both = dot(same, down_tap(step), 1, 0) + dot(previous, down_tap(step + STRIDE), 1, 0)
        for tile in range(lane_tiles):
            spread[pl.ds(tile * run + step, reach, stride=STRIDE), :] = both[
                :, tile * 128 : (tile + 1) * 128
            ]

    alpha = row_of(snake_alpha, 6)
    inverse = 1.0 / alpha
    zero = jnp.zeros((8, channels), f32)

    def mixed_back(place, carry, edge):
        tiles = []
        for tile in range(lane_tiles):
            at = tile * run + STRIDE // 2 + place * ROWS
            tiles.append(spread[pl.ds(at, ROWS), :])
        upstream = jnp.concatenate(tiles, axis=1) * valid_rows(place)
        at = block_rows(place)
        slope, alpha_slope = snake_slopes(hidden[3, at, :], alpha, inverse)
        following = upstream * slope
        grad[at, :] = following
        keep_branch(2, place, following.astype(bf16))
        return carry + folded(upstream * alpha_slope)

    def keep_branch(unit, place, rows):
        branch[block_rows(place), :] = rows
        for index in range(time_count):
            shares[unit, index, 1, block_rows(place), :] = rows[
                :, index * share : (index + 1) * share
            ]

    alpha_sum, _ = each_block(mixed_back, zero)
    alpha_out[...] = jnp.zeros_like(alpha_out)
    keep_alpha(6, jnp.sum(alpha_sum, axis=0, keepdims=True))

    total = down.at[pl.ds(0, pieces[-1][0] + pieces[-1][1])]

    copies, regions = {}, {}

    def add_into(target, start, source, begin, other, at_other, rows):
        def step(index, carry):
            at = index * 16
            block = source[pl.ds(pl.multiple_of(begin + at, 16), 16), :].astype(f32)
            block += other[pl.ds(pl.multiple_of(at_other + at, 16), 16), :].astype(f32)
            target[pl.ds(pl.multiple_of(start + at, 16), 16), :] = block.astype(bf16)
            return carry

        lax.fori_loop(0, rows // 16, step, 0, unroll=min(4, rows // 16))

    def partner_of(bit):
        return batch + bit - 2 * bit * lax.rem(batch // bit, 2)

    def rows_at(start, rows):
        return pl.ds(pl.multiple_of(start, 16), rows)

    def send_half(number, level):
        begin, rows = regions[number, level]
        bit = bits_of[number][level]
        upper = lax.rem(batch // bit, 2)
        rows = rows // 2
        inbox = pieces[number][0] + pieces[number][1] - 2 * rows
        regions[number, level + 1] = (begin + upper * rows, rows)
        copies[number, level] = remote(
            total.at[rows_at(begin + (1 - upper) * rows, rows)],
            from_pair.at[pl.ds(inbox, rows)],
            piece_send.at[number, level],
            piece_recv.at[number, level],
            (partner_of(bit), time),
        )

    def send_back(number, level):
        begin, rows = regions[number, level + 1]
        sems = 2 * len(bits_of[number]) - 1 - level
        copies[number, sems] = remote(
            final.at[rows_at(begin, rows)],
            final.at[rows_at(begin, rows)],
            piece_send.at[number, sems],
            piece_recv.at[number, sems],
            (partner_of(bits_of[number][level]), time),
        )

    def send_pair(number):
        regions[number, 0] = pieces[number]
        send_half(number, 0)

    def advance(stage, number):
        levels = len(bits_of[number])
        copies[number, stage].wait_recv()
        if stage < levels:
            begin, rows = regions[number, stage + 1]
            inbox = pieces[number][0] + pieces[number][1] - 2 * rows
            target = final if stage + 1 == levels else total
            add_into(target, begin, total, begin, from_pair, inbox, rows)
            if stage + 1 < levels:
                send_half(number, stage + 1)
            else:
                send_back(number, stage)
        elif stage + 1 < 2 * levels:
            send_back(number, 2 * levels - 2 - stage)

    relays = {}

    def relay(unit):
        gather_across[unit].wait_recv()
        slot = gathered.at[unit, :, crops - 1 - mine, own]
        relays[unit] = remote(
            slot, slot, relay_send.at[unit], relay_recv.at[unit], (batch, core)
        )

    unit_rows = (TAPS + 1) * share
    unit_start = {unit: pieces[0][1] + unit * unit_rows for unit in range(3)}
    numbers = {
        unit: [
            number
            for number, (start, rows) in enumerate(pieces)
            if unit_start[unit] <= start < unit_start[unit] + unit_rows
        ]
        for unit in range(3)
    }
    everywhere = crops * rows_all
    shifted_start = down.shape[0] // 2
    levels = batch_count.bit_length() - 1
    bits_of = {}
    for number in range(len(pieces)):
        bits_of[number] = [2**level for level in range(levels)]
        if number in [numbers[unit][0 if unit == 0 else -1] for unit in range(3)]:
            bits_of[number][:2] = [2, 1]
    share_pad[...] = jnp.zeros_like(share_pad)
    shares_in = {}
    bias_rows = {}

    def unit_gradient(unit):
        dilation = DILATIONS[unit]
        for copy in shares_in[unit]:
            copy.wait_recv()
        for crop in range(crops):
            share_pad[crop, RIM : RIM + everywhere, :] = share_all[unit, 0, crop].astype(f32)
        bias_rows[unit] = [
            jnp.sum(
                folded(
                    jnp.concatenate(
                        [share_all[unit, kind, crop].astype(f32) for crop in range(crops)], axis=0
                    )
                ),
                axis=0,
                keepdims=True,
            )
            for kind in range(2)
        ]
        for tap in range(TAPS):
            start = RIM - (tap - 3) * dilation
            for crop in range(crops):
                bank, lane = divmod(tap, time_count)
                begin = shifted_start + (bank * crops + crop) * everywhere
                down[begin : begin + everywhere, lane * share : (lane + 1) * share] = share_pad[
                    crop, start : start + everywhere, :
                ].astype(bf16)
        gather_core[unit].wait_recv()
        relays[unit].wait_recv()
        taken = gathered[unit, 0].reshape(crops * everywhere, channels)
        at = unit_start[unit]
        for bank in range(-(-TAPS // time_count)):
            begin = shifted_start + bank * crops * everywhere
            columns = min(TAPS - bank * time_count, time_count) * share
            moved = down[begin : begin + crops * everywhere, :columns]
            row = at + bank * channels
            total[row : row + columns, :] = dot(moved, taken, 0, 0).astype(bf16)
        taken = gathered[unit, 1].reshape(crops * everywhere, channels)
        narrow_share = share_all[unit, 1].reshape(crops * everywhere, share)
        total[at + TAPS * share : at + unit_rows, :] = dot(narrow_share, taken, 0, 0).astype(bf16)
        for number in numbers[unit]:
            send_pair(number)

    def small_gradient(smalls_in):
        for copy in smalls_in:
            copy.wait_recv()
        block = small[time]
        for step in range(time_count - 1):
            block += small_in[step].astype(f32)
        small[0] = block

    def lows_members():
        for copy in lows_in:
            copy.wait_recv()
        local(low_all, all_lows.at[batch], 1)
        for step in range(1, members):
            low_blocks.append(
                remote(
                    low_all,
                    all_lows.at[batch],
                    low_send.at[2 + step],
                    low_recv.at[2 + step],
                    (member(step), time),
                )
            )
        low_blocks.append(
            remote(
                low_all,
                all_lows.at[batch],
                low_send.at[2 + members],
                low_recv.at[2 + members],
                (pair, time),
            )
        )

    def lows_pair():
        for step in range(1, members):
            low_blocks[step - 1].wait_recv()
            slot = all_lows.at[block_of(step, half)]
            sems = 2 + members + step
            low_blocks.append(
                remote(slot, slot, low_send.at[sems], low_recv.at[sems], (pair, time))
            )

    def between_units(unit):
        if unit == 2:
            lows_members()
            for step in near_first[2:]:
                forward_pair(step)
        elif unit == 1:
            lows_pair()

    def finish_all(between_waves):
        order = numbers[2] + numbers[1] + numbers[0] + [0]
        stages = [functools.partial(advance, stage) for stage in range(2 * levels)]
        for wave in range(len(order) + len(stages)):
            for depth, stage in enumerate(stages):
                if 0 <= wave - depth < len(order):
                    stage(order[wave - depth])
            if wave in between_waves:
                between_waves[wave]()
            if wave < members:
                forward_across(([0] + near_first)[wave])
        for step in ([0] + near_first)[len(order) + len(stages) :]:
            forward_across(step)
        forward_core(0)
        forward_core(1)
        for copy in core_blocks:
            copy.wait_recv()
        for copy in low_blocks[members - 1 :]:
            copy.wait_recv()

    for step in near_first[1:2]:
        forward_pair(step)
    for unit in (2, 1, 0):
        dilation = DILATIONS[unit]
        number = 5 + unit
        work[...] = dot(branch[...], narrow[unit], 1, 0)
        alpha = row_of(snake_alpha, 2 * unit + 1)
        inverse = 1.0 / alpha

        def conv_back(place, carry, edge):
            at = block_rows(place)
            upstream = work[at, :]
            slope, alpha_slope = snake_slopes(conv[unit, at, :], alpha, inverse)
            lowered = (upstream * slope).astype(bf16)
            for index in range(time_count):
                shares[unit, index, 0, at, :] = lowered[
                    :, index * share : (index + 1) * share
                ]
            pad[pad_rows(place), :] = lowered.astype(f32)
            keep_edge(number, edge, lowered)
            return carry + folded(upstream * alpha_slope)

        alpha_sum, made = each_block(conv_back, zero, lambda: start_halo(number))
        shares_in[unit] = [
            remote(
                shares.at[unit, sibling(step)],
                share_all.at[unit, :, mine, own],
                share_send.at[unit, step - 1],
                share_recv.at[unit, step - 1],
                (batch, sibling(step)),
            )
            for step in range(1, time_count)
        ]
        if unit == 2:
            gather(1)
        for kind in range(2):
            share_all[unit, kind, mine, own, :] = shares[unit, time, kind]
        keep_alpha(2 * unit + 1, jnp.sum(alpha_sum, axis=0, keepdims=True))
        between_units(unit)
        fill_rims(made, number)
        result = None
        for tap in range(TAPS):
            term = dot(shifted(-(tap - 3) * dilation), wide[unit, tap], 1, 0)
            result = term if result is None else result + term
        work[...] = result
        alpha = row_of(snake_alpha, 2 * unit)
        inverse = 1.0 / alpha

        def hidden_back(place, carry, edge):
            at = block_rows(place)
            upstream = work[at, :]
            slope, alpha_slope = snake_slopes(hidden[unit, at, :], alpha, inverse)
            following = grad[at, :] + upstream * slope
            if unit > 0:
                grad[at, :] = following
                keep_branch(unit - 1, place, following.astype(bf16))
            else:
                signal_out[at, :] = following * valid_rows(place)
            return carry + folded(upstream * alpha_slope)

        alpha_sum, _ = each_block(hidden_back, zero)
        keep_alpha(2 * unit, jnp.sum(alpha_sum, axis=0, keepdims=True))

    alphas_in = [
        remote(
            alpha_out.at[sibling(step)],
            alpha_in.at[step - 1],
            small_send.at[time_count - 1 + step - 1],
            small_recv.at[time_count - 1 + step - 1],
            (batch, sibling(step)),
        )
        for step in range(1, time_count)
    ]
    relay(2)
    unit_gradient(2)
    smalls_in = quantizer_gradient()
    relay(1)
    unit_gradient(1)
    swap_back = swap(
        4,
        lambda part: signal_out.at[pl.ds(part * length, length)],
        lambda slot: signal_back.at[slot],
        mine,
        True,
    )
    small_gradient(smalls_in)
    def first_unit():
        relay(0)
        unit_gradient(0)

    def last_piece():
        for copy in alphas_in:
            copy.wait_recv()
        alpha_rows = alpha_out[time]
        for step in range(time_count - 1):
            alpha_rows += alpha_in[step]
        rest = [alpha_rows] + [bias_rows[unit][kind] for kind in range(2) for unit in range(3)]
        rest = jnp.concatenate(rest + [jnp.zeros((2, share), f32)], axis=0)
        small[0, small.shape[1] - 16 :, channels - share :] = rest
        for start in range(0, pieces[0][1], small.shape[1]):
            total[start : start + small.shape[1], :] = small[0].astype(bf16)
        send_pair(0)

    finish_all({0: first_unit, 1: last_piece})
    swapped_in(swap_back)
    swapped_in(swap_commit)
    for crop in range(crops):
        signal_grad[crop] = signal_back[crop].T
    for made in swaps:
        for peer, origin, away, here, arrived in made:

            @pl.when(peer != time)
            def _():
                away.wait_send()

    for copy in local_copies:
        copy.wait()
    for copy in sent:
        copy.wait_send()


def run_block(time_count, batch_count, pieces, lengths, *arrays):
    (signal, quant_cot, coded, wide, _, narrow, _, _, down, down_bias, in_weight) = arrays[:11]
    f32, bf16 = jnp.float32, jnp.bfloat16
    crops, channels, length = signal.shape
    latents = down_bias.shape[1]
    taps = down.shape[0] // latents
    frames = crops * (length // STRIDE)
    rows = crops * length
    count = in_weight.shape[0]
    share = channels // time_count
    wide_of = latents // time_count
    members = batch_count // 2
    everywhere = crops * rows
    total_rows = pieces[-1][0] + pieces[-1][1]
    vmem = pl.BlockSpec(memory_space=pltpu.VMEM)
    hbm = pl.BlockSpec(memory_space=pl.ANY)
    in_specs = [pl.BlockSpec(memory_space=pltpu.SMEM)] + [vmem] * len(arrays)
    for place in (0, 1, 3, 5, 8):
        in_specs[1 + place] = hbm
    lane_tiles = channels // 128
    dma = pltpu.SemaphoreType.DMA
    slots = 2 * members
    return pl.pallas_call(
        functools.partial(block_kernel, time_count, batch_count, pieces),
        out_shape=(
            jax.ShapeDtypeStruct(quant_cot.shape, f32),
            jax.ShapeDtypeStruct(coded.shape, f32),
            jax.ShapeDtypeStruct(signal.shape, f32),
            jax.ShapeDtypeStruct((total_rows, channels), bf16),
            jax.ShapeDtypeStruct((batch_count, time_count, STRIDE, frames, channels), bf16),
            jax.ShapeDtypeStruct((batch_count, time_count, frames, wide_of), bf16),
        ),
        in_specs=in_specs,
        out_specs=(vmem, vmem, vmem, vmem, hbm, hbm),
        scratch_shapes=[
            pltpu.VMEM(wide.shape, bf16),
            pltpu.VMEM(narrow.shape, bf16),
            pltpu.VMEM((taps * latents, channels), bf16),
            pltpu.VMEM((4, rows, channels), f32),
            pltpu.VMEM((3, rows, channels), f32),
            pltpu.VMEM((3, 2, crops, everywhere, channels), bf16),
            pltpu.VMEM((rows + 2 * RIM, channels), f32),
            pltpu.VMEM((rows, channels), f32),
            pltpu.VMEM((rows, channels), f32),
            pltpu.VMEM((rows, channels), bf16),
            pltpu.VMEM((3, time_count, 2, rows, share), bf16),
            pltpu.VMEM((3, 2, crops, everywhere, share), bf16),
            pltpu.VMEM((crops, everywhere + 2 * RIM, share), f32),
            pltpu.VMEM((lane_tiles * (rows + 16), 128), f32),
            pltpu.VMEM((taps, frames, channels), bf16),
            pltpu.VMEM((frames, latents), f32),
            pltpu.VMEM((frames + 16, latents), f32),
            pltpu.VMEM((lane_tiles * (rows + 8 * STRIDE), 128), f32),
            pltpu.VMEM((frames, count), f32),
            pltpu.VMEM((frames, count), f32),
            pltpu.VMEM((frames, count), f32),
            pltpu.VMEM((time_count, 128, channels), f32),
            pltpu.VMEM((time_count, 128, channels), bf16),
            pltpu.VMEM((time_count - 1, 128, channels), bf16),
            pltpu.VMEM((time_count, 8, share), f32),
            pltpu.VMEM((time_count - 1, 8, share), f32),
            pltpu.VMEM((time_count, frames, wide_of), bf16),
            pltpu.VMEM((time_count, frames, wide_of), bf16),
            pltpu.VMEM((144, channels), bf16),
            pltpu.VMEM((144, channels), bf16),
            pltpu.VMEM((frames, latents), bf16),
            pltpu.VMEM((16, latents), bf16),
            pltpu.VMEM(signal.shape, f32),
            pltpu.VMEM(quant_cot.shape, f32),
            pltpu.VMEM(coded.shape, f32),
            pltpu.VMEM(coded.shape, f32),
            pltpu.VMEM((rows, channels), f32),
            pltpu.VMEM((crops, length, channels), f32),
            dma((5,)),
            dma((5, 2)),
            dma((5, 2)),
            pltpu.VMEM((total_rows, channels), bf16),
            dma((8,)),
            dma((2,)),
            dma((8,)),
            dma((8,)),
            dma((3, 2)),
            dma((3, 2)),
            dma((3,)),
            dma((3,)),
            dma((3, time_count - 1)),
            dma((3, time_count - 1)),
            dma((2 * (time_count - 1),)),
            dma((2 * (time_count - 1),)),
            dma((2 + 2 * members,)),
            dma((2 + 2 * members,)),
            dma((4 * members + 2,)),
            dma((4 * members + 2,)),
            dma((len(pieces), slots)),
            dma((len(pieces), slots)),
        ],
        compiler_params=pltpu.CompilerParams(
            collective_id=1, has_side_effects=True, vmem_limit_bytes=62 * 2**20
        ),
    )(lengths, *arrays)


def down_kernel(
    line,
    count_small,
    start,
    lows,
    phases,
    summed,
    quantized,
    signal_grad,
    out,
    wide_out,
    narrow_out,
    quantized_out,
    signal_out,
    in_weight_out,
    codebook_out,
    out_weight_out,
    bias_out,
    down_bias,
    in_bias,
    alpha_out,
    wide_bias,
    narrow_bias,
    held,
    columns,
    sums,
    wide,
    narrow,
    in_sems,
    out_sems,
    sum_sems,
):
    count = lows.shape[1]
    group, lanes = held.shape[1], held.shape[4]
    rows = group * held.shape[3]
    tiles = lanes // 128
    groups = phases.shape[0] // group
    items = [(part, at) for part in range(phases.shape[3] // lanes) for at in range(groups)]
    loads = [
        pltpu.make_async_copy(
            phases.at[pl.ds(at * group, group), :, :, pl.ds(part * lanes, lanes)],
            held.at[index % 2],
            in_sems.at[index % 2],
        )
        for index, (part, at) in enumerate(items)
    ]
    bring = pltpu.make_async_copy(summed, sums, sum_sems.at[0])
    bring.start()
    for load in loads[:2]:
        load.start()
    def turned_rows(at):
        rows_here = lows[at * rows : (at + 1) * rows, :].astype(jnp.float32).T
        place = lax.rem(lax.broadcasted_iota(jnp.int32, rows_here.shape, 1), line)
        following = jnp.where(place < line - 1, pltpu.roll(rows_here, rows - 1, 1), 0.0)
        preceding = jnp.where(place > 0, pltpu.roll(rows_here, 1, 1), 0.0)
        after = jnp.concatenate([rows_here, following], axis=0).astype(lows.dtype)
        before = jnp.concatenate([rows_here, preceding], axis=0).astype(lows.dtype)
        return after, before

    stores = []
    first_rows = turned_rows(0)
    quantized_out[...] = quantized[...]
    signal_out[...] = signal_grad[...]
    bring.wait()
    f32 = jnp.float32
    units, share, channels = narrow.shape
    for unit in range(units):
        at = start + unit * (TAPS + 1) * share
        for tap in range(TAPS):
            wide[unit, tap] = sums[at + tap * share : at + (tap + 1) * share, :].astype(f32)
        narrow[unit] = sums[at + TAPS * share : at + (TAPS + 1) * share, :].astype(f32)
    stores.append(pltpu.make_async_copy(wide, wide_out, sum_sems.at[1]))
    stores.append(pltpu.make_async_copy(narrow, narrow_out, sum_sems.at[2]))
    for store in stores:
        store.start()
    small = jnp.concatenate([sums[:128, :count], sums[:128, count : 2 * count]], axis=0).astype(f32)
    for kind, ref in enumerate((in_weight_out, codebook_out, out_weight_out)):
        ref[...] = small[kind * count_small : (kind + 1) * count_small]
    row = 3 * count_small + bias_out.shape[0]
    bias_out[...] = small[3 * count_small : row]
    down_bias[...] = small[row : row + 1]
    in_bias[...] = small[row + 1 : row + 2]
    last = small[240:256, count - share : count]
    alpha_out[...] = last[:7]
    wide_bias[...] = last[8:11]
    narrow_bias[...] = last[11:14]
    after, before = first_rows
    for index, (part, at) in enumerate(items):
        if index > 0 and groups > 1:
            after, before = turned_rows(at)
        loads[index].wait()
        for step in range(STRIDE):
            block = held[index % 2, :, step].reshape(rows, lanes)
            late = step >= STRIDE // 2
            both = dot(after if late else before, block, 1, 0)
            middle = step + STRIDE // 2
            for tap, row in ((middle, 0), (middle - STRIDE if late else middle + STRIDE, count)):
                for tile in range(tiles):
                    place = pl.ds(tap, count, stride=2 * STRIDE)
                    value = both[row : row + count, tile * 128 : (tile + 1) * 128]
                    if at > 0:
                        value = value + columns[part * tiles + tile, place, :]
                    columns[part * tiles + tile, place, :] = value
        if index + 2 < len(items):
            loads[index + 2].start()
        if at == groups - 1:
            for tile in range(part * tiles, (part + 1) * tiles):
                stores.append(
                    pltpu.make_async_copy(
                        columns.at[tile], out.at[:, pl.ds(tile * 128, 128)], out_sems.at[tile]
                    )
                )
                stores[-1].start()
    for store in stores:
        store.wait()


def down_gradient(lows, phases, line, summed, start, share, count_small, phase_count, quantized, signal_grad):
    devices, _, rows, channels = phases.shape
    count = lows.shape[1]
    lanes = 256
    f32 = jnp.float32
    hbm = pl.BlockSpec(memory_space=pl.ANY)
    vmem = pl.BlockSpec(memory_space=pltpu.VMEM)
    wide = (3, TAPS, share, channels)
    shapes = [
        (count * 2 * STRIDE, channels),
        wide,
        (3, share, channels),
        quantized.shape,
        signal_grad.shape,
        (count_small, count),
        (count_small, count),
        (count_small, count),
        (phase_count, count),
        (1, count),
        (1, count),
        (7, share),
        (3, share),
        (3, share),
    ]
    return pl.pallas_call(
        functools.partial(down_kernel, line, count_small, start),
        out_shape=[jax.ShapeDtypeStruct(shape, f32) for shape in shapes],
        in_specs=[vmem, hbm, hbm, vmem, vmem],
        out_specs=[hbm] * 3 + [vmem] * (len(shapes) - 3),
        scratch_shapes=[
            pltpu.VMEM((2, min(devices, 32), STRIDE, rows, lanes), phases.dtype),
            pltpu.VMEM((channels // 128, count * 2 * STRIDE, 128), f32),
            pltpu.VMEM(summed.shape, summed.dtype),
            pltpu.VMEM(wide, f32),
            pltpu.VMEM((3, share, channels), f32),
            pltpu.SemaphoreType.DMA((2,)),
            pltpu.SemaphoreType.DMA((channels // 128,)),
            pltpu.SemaphoreType.DMA((3,)),
        ],
        compiler_params=pltpu.CompilerParams(vmem_limit_bytes=60 * 2**20),
    )(lows, phases, summed, quantized, signal_grad)


def body(
    signal,
    quant_cot,
    commit_cot,
    lengths,
    codes,
    wide_weight,
    wide_bias,
    narrow_weight,
    narrow_bias,
    snake_alpha,
    down_weight,
    down_bias,
    in_weight,
    in_bias,
    codebook,
    out_weight,
    out_bias,
):
    time_count = lax.axis_size("tm")
    batch_count = lax.axis_size("batch")
    crop_count, channel_count, length = signal.shape
    latent_count, tap_count, _ = down_weight.shape
    phases, dims = in_weight.shape[:2]
    count = phases * dims
    frame_count = length // STRIDE
    small_rows = 16 * batch_count
    unit_rows = (TAPS + 1) * (channel_count // time_count)
    piece = max(unit_rows // 2, small_rows)
    pieces = [(0, small_rows)]
    pieces += [(at, piece) for at in range(small_rows, small_rows + 3 * unit_rows, piece)]
    coded = [jnp.swapaxes(codes, 1, 2).astype(jnp.float32), jnp.swapaxes(commit_cot, 1, 2)]
    coded = jnp.pad(jnp.concatenate(coded, axis=2), ((0, 0), (0, 0), (0, 128 - 2 * phases)))
    quantized, commit, signal_grad, summed, all_phases, all_low = run_block(
        time_count,
        batch_count,
        tuple(pieces),
        lengths,
        signal,
        quant_cot,
        coded,
        jnp.swapaxes(wide_weight, 1, 2),
        wide_bias,
        narrow_weight,
        narrow_bias,
        snake_alpha,
        down_weight.reshape(-1, channel_count),
        down_bias.reshape(1, -1),
        in_weight.reshape(count, -1),
        in_bias.reshape(1, -1),
        codebook.reshape(count, -1),
        out_weight.reshape(count, -1),
        out_bias,
    )
    commit = jnp.swapaxes(commit[:, :, :phases], 1, 2)

    share = latent_count // time_count
    all_phases = all_phases.reshape((-1,) + all_phases.shape[2:])
    lows = all_low.reshape(-1, share)
    results = down_gradient(
        lows,
        all_phases,
        time_count * frame_count,
        summed,
        small_rows,
        channel_count // time_count,
        count,
        phases,
        quantized,
        signal_grad,
    )
    down_out, wide_out, narrow_out, quantized, signal_grad = results[:5]
    out_bias_out, down_bias_out, in_bias_row, alpha_out, wide_bias_out, narrow_bias_out = results[8:]
    down_out = down_out.reshape(share, tap_count, channel_count)
    wide_out = jnp.swapaxes(wide_out, 1, 2)
    in_weight_out, codebook_out, out_weight_out = (
        rows.reshape(phases, dims, -1) for rows in results[5:8]
    )
    down_bias_out = down_bias_out.reshape(-1)
    in_bias_all = in_bias_row[0, :count].reshape(phases, dims)
    part = dims // time_count
    in_bias_out = lax.dynamic_slice_in_dim(in_bias_all, lax.axis_index("tm") * part, part, axis=1)
    return (
        quantized,
        commit,
        signal_grad,
        wide_out,
        wide_bias_out,
        narrow_out,
        narrow_bias_out,
        alpha_out,
        down_out,
        down_bias_out,
        in_weight_out,
        in_bias_out,
        codebook_out,
        out_weight_out,
        out_bias_out,
    )


def solution(mesh):
    return jax.shard_map(
        body,
        mesh=mesh,
        in_specs=(
            P("batch", None, "tm"),
            P("batch", "tm", None),
            P("batch", None, "tm"),
            P("batch"),
            P("batch", None, "tm"),
            P(),
            P(),
            P(),
            P(),
            P(),
            P(),
            P(),
            P(),
            P(),
            P(),
            P(),
            P(),
        ),
        out_specs=(
            P("batch", "tm", None),
            P("batch", None, "tm"),
            P("batch", None, "tm"),
            P(None, "tm", None, None),
            P(None, "tm"),
            P(None, "tm", None),
            P(None, "tm"),
            P(None, "tm"),
            P("tm", None, None),
            P("tm"),
            P(None, None, "tm"),
            P(None, "tm"),
            P(None, None, "tm"),
            P(None, None, "tm"),
            P(None, "tm"),
        ),
        check_vma=False,
    )
```
